128 devices in a mesh: group: 8 (over x, core), member: 16 (over y, z).
Axes of the slice: x: 4, y: 4, z: 4, core: 2. Of those that a mesh axis runs over, the one named last changes fastest.
Arguments:
- embeddings: bfloat16 [98304, 1024], P(('group', 'member')), may hold values from -6 to 6
- labels: int32 [98304], P(('group', 'member')), may hold values from 0 to 7
- send_list: int32 [128, 768], P(('group', 'member')), may hold values from 0 to 767, each once within a row
Outputs:
- row_max: float32 [98304], P(('group', 'member'))
The draws below stay inside these ranges and needn't reach their ends.
Inputs may be any that keep to these rules, and one draw needn't show every extreme that they name: Each row of send_list names each of the 768 local rows once.
All inputs are finite; a program needn't handle non-finite values.
Results may differ from the reference program's by a relative error of at most 0.0014.
Values may be sent and summed in bfloat16 or wider, within the bound.
No kernel may reach another device: no remote copies, remote signals or barrier semaphores. Data moves between devices by JAX's collectives and lax.ppermute only.
A program may use at most 128 MiB of HBM per device.

```python
import jax
import jax.numpy as jnp
from jax import lax

D = 1024
ROW_DEV = 768
CL_GRP = 8
ROWS = 98304
N_GROUP = 8
N_MEMBER = 16


def set_ends(values, key, smallest, largest):
    place = [jax.random.randint(jax.random.fold_in(key, axis), (), 0, length) for axis, length in enumerate(values.shape)]
    main_axis = values.shape.index(max(values.shape))
    neighbour = place[:main_axis] + [(place[main_axis] + 1) % values.shape[main_axis]] + place[main_axis + 1:]
    return values.at[tuple(place)].set(smallest).at[tuple(neighbour)].set(largest)


def level_of(rng, extent, split, smallest, top_value):
    def one(dim, blocks):
        draws = jax.random.uniform(jax.random.fold_in(jax.random.fold_in(rng, 6), dim), (blocks,), jnp.float32, smallest / len(split), top_value / len(split))
        return jnp.repeat(jnp.exp(draws), extent[dim] // blocks).reshape((-1,) + (1,) * (len(extent) - dim - 1))

    level = one(*split[0])
    for cut in split[1:]:
        level = level * one(*cut)
    return level


def bell_draw(stream_key, shape, width, limit, cuts=(), kind=jnp.bfloat16):
    array = jax.random.normal(stream_key, shape, jnp.float32) * width
    if len(cuts) > 0:
        array = level_of(stream_key, shape, cuts, -0.22, 0.18) * array
    return jnp.clip(array, min=-limit, max=limit).astype(kind)


def setup_inputs(seed: int = 0) -> dict:
    seeds = jax.random.split(jax.random.key(seed), 4)
    return {
        "embeddings": bell_draw(seeds[0], (ROWS, D), 1.0, 6.0, ((0, 128),)),
        "labels": set_ends(jax.random.randint(seeds[1], (ROWS,), 0, CL_GRP), jax.random.fold_in(seeds[1], 1), 0, CL_GRP - 1).astype(jnp.int32),
        "send_list": jax.vmap(lambda own: jax.random.permutation(own, ROW_DEV))(jax.random.split(seeds[2], (N_GROUP * N_MEMBER))).reshape((N_GROUP * N_MEMBER, ROW_DEV)).astype(jnp.int32),
    }


def normalize(embeddings):
    values = embeddings.astype(jnp.float32)
    scale = lax.rsqrt(lax.optimization_barrier(jnp.sum(values * values, axis=1, keepdims=True)) + 1e-06)
    return (values * scale).astype(jnp.bfloat16)

def reference(embeddings, labels, send_list):
    dev_count = N_GROUP * N_MEMBER
    slot_rows = ROW_DEV // dev_count
    unit_rows = normalize(embeddings)
    sources = jnp.arange(dev_count, dtype=jnp.int32)
    lists = send_list.reshape(dev_count, dev_count, slot_rows)
    global_rows = sources[:, None, None] * ROW_DEV + lists
    arrive = jnp.transpose(global_rows, (1, 0, 2)).reshape(N_GROUP, N_MEMBER, ROW_DEV)

    def one_group(group_rows):
        flat_rows = group_rows.reshape(-1)
        key_unit = unit_rows[flat_rows]
        key_label = labels[flat_rows]

        def one_block(block_rows):
            queries = unit_rows[block_rows]
            q_label = labels[block_rows]
            scores = jnp.dot(queries, key_unit.T, preferred_element_type=jnp.float32)
            allowed = (q_label[:, None] == key_label[None, :]) & (flat_rows[None, :] < block_rows[:, None])
            return lax.optimization_barrier(jnp.max(jnp.where(allowed, scores, jnp.float32(-1.0)), axis=1))
        return lax.map(one_block, group_rows)
    result = lax.map(one_group, arrive)
    return result.reshape(-1)
```

```python
import functools

import jax
import jax.numpy as jnp
from jax import lax
from jax.experimental import pallas as pl
from jax.experimental.pallas import tpu as pltpu
from jax.sharding import Mesh, PartitionSpec as P

F32 = jnp.float32
BF = jnp.bfloat16
I32 = jnp.int32

D = 1024
ROWS = 768
CHIPS = 64
LABELS = 8
CAP = 15
SLOT = 16
MAIN = CHIPS * SLOT
FIX = LABELS * SLOT
ALL = ("x", "core", "yh", "yl", "z")
CHIP_AXES = ("x", "yh", "yl", "z")
GROUP_CHIPS = ("yl", "z")
PLANE = ("core", "yh", "yl", "z")
NEVER = 1.0e9
VMEM = 48 * 1024 * 1024


def iota(shape, dim):
    return lax.broadcasted_iota(I32, shape, dim)


def onehot(cond):
    return jnp.where(cond, 1.0, 0.0).astype(BF)


def mm(a, b):
    return lax.dot_general(a, b, (((1,), (0,)), ((), ())), preferred_element_type=F32)


def mm_t(a, b):
    return lax.dot_general(a, b, (((1,), (1,)), ((), ())), preferred_element_type=F32)


def pack_kernel(ids_ref, emb_ref, lab_ref, list_ref, out_ref):
    rot = ids_ref[2]
    listed = onehot(iota((ROWS, ROWS), 0) == list_ref[...])
    pos = iota((16, ROWS), 1)
    group_of = lax.shift_right_logical(pos * 683, 16)
    sel = iota((16, ROWS), 0)
    vals = jnp.where(sel == 0, group_of, jnp.where(sel == 1, pos - group_of * 96, 0)).astype(F32).astype(BF)
    gd = mm_t(vals, listed)
    group = gd[0:1]
    dest = gd[1:2]
    label = lab_ref[...].astype(F32)
    cluster = group * 8.0 + label
    member = iota((CHIPS, ROWS), 0).astype(F32) == cluster
    before = onehot(iota((ROWS, ROWS), 0) < iota((ROWS, ROWS), 1))
    ranks = mm(onehot(member), before)
    rank = jnp.sum(jnp.where(member, ranks, 0.0), axis=0, keepdims=True)
    count = jnp.broadcast_to(jnp.sum(jnp.where(member, 1.0, 0.0), axis=1, keepdims=True), (CHIPS, 128))
    over = jnp.maximum(count - CAP, 0.0).astype(BF)
    free = jnp.maximum(CAP - count, 0.0)
    c0, c1 = iota((CHIPS, CHIPS), 0), iota((CHIPS, CHIPS), 1)
    same = lax.shift_right_logical(c0, 3) == lax.shift_right_logical(c1, 3)
    over_pre = mm(onehot(same & (c1 < c0)), over)
    above = (CAP - 1 - (iota((CHIPS, 128), 1) & 15)).astype(F32)
    higher = jnp.clip(free, 0.0, jnp.maximum(above, 0.0)).astype(BF)
    level = onehot(free > above)
    free_pre = mm(onehot(same), higher) + mm(onehot(same & (((c1 - rot) & 7) < ((c0 - rot) & 7))), level)
    over_at = jnp.sum(jnp.where(member, over_pre[:, 0:1], 0.0), axis=0, keepdims=True) + rank - CAP
    row_code = jnp.where(rank < CAP, cluster * 16.0 + rank, 2048.0 + group * 128.0 + over_at)
    slot = iota((MAIN, 128), 0)
    at = (slot & 15).astype(F32)
    chip_hot = onehot(lax.shift_right_logical(iota((MAIN, CHIPS), 0), 4) == iota((MAIN, CHIPS), 1))
    slot_count = mm(chip_hot, count.astype(BF))
    slot_free = jnp.where(iota((MAIN, 128), 1) == (slot & 15), mm(chip_hot, free_pre.astype(BF)), 0.0)
    slot_free = jnp.sum(slot_free, axis=1, keepdims=True)
    spare = 2048.0 + (lax.shift_right_logical(slot, 7) * 128).astype(F32) + slot_free
    slot_code = jnp.where(at >= CAP, -1.0, jnp.where(at < slot_count, slot.astype(F32), spare))
    pick = jnp.concatenate([onehot(slot_code == row_code[:, b * 128:(b + 1) * 128]) for b in range(ROWS // 128)], axis=1)
    values = emb_ref[...].astype(F32)
    scale = lax.rsqrt(jnp.sum(values * values, axis=1, keepdims=True) + 1e-06)
    unit = (values * scale).astype(BF)
    lane = iota((128, ROWS), 0)
    tags = jnp.where(lane < 16, label + 1.0, jnp.where(lane < 32, dest, 0.0)).astype(BF)
    tag = jnp.where((iota((MAIN, 128), 1) & 15) == (slot & 15), mm_t(pick, tags), 0.0)
    tag = jnp.broadcast_to(jnp.sum(tag.reshape(CHIPS, SLOT, 128), axis=1, keepdims=True), (CHIPS, SLOT, 128)).reshape(MAIN, 128)
    for b in range(0, D, 256):
        part = mm(pick, unit[:, b:b + 256])
        if b == 0:
            out_ref[:, 0:128] = jnp.where(at >= CAP, tag, part[:, 0:128]).astype(BF)
            out_ref[:, 128:256] = part[:, 128:256].astype(BF)
        else:
            out_ref[:, b:b + 256] = part.astype(BF)


def tag_rows(first, n):
    pick = onehot(iota((n, n * SLOT), 1) == iota((n, n * SLOT), 0) * SLOT + CAP)
    return mm(pick, first).astype(BF)


def tag_lanes(tags, n, k):
    spread = onehot(iota((128, n * SLOT), 0) == (iota((128, n * SLOT), 1) & 15) + 16 * k)
    wide = mm(tags, spread)
    own = iota((n, n * SLOT), 0) == lax.shift_right_logical(iota((n, n * SLOT), 1), 4)
    return jnp.sum(jnp.where(own, wide, 0.0), axis=0, keepdims=True)


def tag_columns(tags, n, ks):
    spread = onehot(lax.shift_right_logical(iota((n * SLOT, n), 0), 4) == iota((n * SLOT, n), 1))
    wide = mm(spread, tags)
    shape = (n * SLOT, 128)
    own = iota(shape, 0) & 15
    return [jnp.sum(jnp.where(iota(shape, 1) == own + 16 * k, wide, 0.0), axis=1, keepdims=True) for k in ks]


def source_of(chip, core):
    return lax.shift_right_logical(chip, 4) * 32 + core * 16 + (chip & 15)


def main_order(shape, dim, core):
    slot = iota(shape, dim)
    return (source_of(lax.shift_right_logical(slot, 4), core) * 256 + (slot & 15)).astype(F32)


def away_order(source, turn, at):
    return (source * 256 + 16 + (CAP - 1 - at) * 8 + turn).astype(F32)


def fix_order(shape, dim, core, chip, at):
    holder = lax.shift_right_logical(iota(shape, dim), 4)
    chip = chip.astype(I32)
    return away_order(source_of(chip, core), (holder - chip) & 7, at.astype(I32))


def fix_kernel(ids_ref, main_ref, out_ref, flag_ref):
    own = ids_ref[1].astype(F32)
    tags = tag_rows(main_ref[:, 0:128], CHIPS)
    label = tag_lanes(tags, CHIPS, 0)
    dest = tag_lanes(tags, CHIPS, 1)
    moved = (label > 0.5) & (label != own + 1.0)
    member = moved & (iota((LABELS, MAIN), 0).astype(F32) == label - 1.0)
    before = onehot(iota((MAIN, MAIN), 0) < iota((MAIN, MAIN), 1))
    hot = jnp.concatenate([jnp.where(member, 1.0, 0.0), jnp.zeros((LABELS, MAIN), F32)], axis=0).astype(BF)
    ranks = mm(hot, before)[0:LABELS]
    rank = jnp.sum(jnp.where(member, ranks, 0.0), axis=0, keepdims=True)
    code = jnp.where(moved & (rank < CAP), (label - 1.0) * 16.0 + rank, -1.0)
    pick = onehot(iota((FIX, MAIN), 0).astype(F32) == code)
    slot = iota((1, MAIN), 1)
    lane = iota((128, MAIN), 0)
    kind = lax.shift_right_logical(lane, 4)
    vals = jnp.where(kind == 0, 1.0, jnp.where(kind == 1, lax.shift_right_logical(slot, 4).astype(F32), jnp.where(kind == 2, (slot & 15).astype(F32), jnp.where(kind == 3, dest, 0.0)))).astype(BF)
    fixed = (FIX, 128)
    tag = jnp.where((iota(fixed, 1) & 15) == (iota(fixed, 0) & 15), mm_t(pick, vals), 0.0)
    tag = jnp.broadcast_to(jnp.sum(tag.reshape(LABELS, SLOT, 128), axis=1, keepdims=True), (LABELS, SLOT, 128)).reshape(fixed)
    for b in range(0, D, 256):
        part = mm(pick, main_ref[:, b:b + 256])
        if b == 0:
            out_ref[:, 0:128] = jnp.where((iota(fixed, 0) & 15) == CAP, tag, part[:, 0:128]).astype(BF)
            out_ref[:, 128:256] = part[:, 128:256].astype(BF)
        else:
            out_ref[:, b:b + 256] = part.astype(BF)
    worst = jnp.max(jnp.where(moved, rank, 0.0), axis=1, keepdims=True)
    flag_ref[...] = jnp.broadcast_to(jnp.where(worst >= CAP, 1.0, 0.0), (8, 128))


def lanes_to_rows(row):
    return jnp.concatenate([row[:, i * 128:(i + 1) * 128] for i in range(row.shape[1] // 128)], axis=0)


def score_kernel(ids_ref, flag_ref, own_ref, twin_ref, fix_ref, fix_twin_ref, out_ref):
    core = ids_ref[0]
    mine = ids_ref[1].astype(F32) + 1.0
    tags = tag_rows(own_ref[:, 0:128], CHIPS)
    twin_tags = tag_rows(twin_ref[:, 0:128], CHIPS)
    fix_tags = tag_rows(fix_ref[:, 0:128], LABELS)
    fix_twin_tags = tag_rows(fix_twin_ref[:, 0:128], LABELS)

    def main_key(t, c):
        (label,) = tag_columns(t, CHIPS, (0,))
        return jnp.where(label == mine, main_order((MAIN, 1), 0, c), NEVER)

    def fix_key(t, c):
        valid, chip, at = tag_columns(t, LABELS, (0, 1, 2))
        return jnp.where(valid > 0.5, fix_order((FIX, 1), 0, c, chip, at), NEVER)

    keys = (
        (own_ref, main_key(tags, core)),
        (twin_ref, main_key(twin_tags, 1 - core)),
        (fix_ref, fix_key(fix_tags, core)),
        (fix_twin_ref, fix_key(fix_twin_tags, 1 - core)),
    )
    valid = tag_lanes(tags, CHIPS, 0) == mine
    query = jnp.where(valid, main_order((1, MAIN), 1, core), -1.0)
    code = jnp.where(valid, tag_lanes(tags, CHIPS, 1), -1.0)
    fix_valid = tag_lanes(fix_tags, LABELS, 0) > 0.5
    fix_chip = tag_lanes(fix_tags, LABELS, 1)
    fix_query = jnp.where(fix_valid, fix_order((1, FIX), 1, core, fix_chip, tag_lanes(fix_tags, LABELS, 2)), -1.0)
    fix_source = source_of(fix_chip.astype(I32), core).astype(F32)
    fix_code = jnp.where(fix_valid, fix_source * 128.0 + tag_lanes(fix_tags, LABELS, 3), -1.0)

    def best(q_rows, q_order, limits):
        found = jnp.full((1, q_rows.shape[0]), -1.0, F32)
        for (ref, order), limit in zip(keys, limits):
            for k in range(0, limit, 256):
                e = min(k + 256, limit)
                scores = mm_t(ref[k:e, :], q_rows)
                scores = jnp.where(order[k:e] < q_order, scores, -1.0)
                found = jnp.maximum(found, jnp.max(scores, axis=0, keepdims=True))
        return found

    rows = []
    for q in range(0, MAIN, 256):
        rows.append(lanes_to_rows(best(own_ref[q:q + 256, :], query[:, q:q + 256], (q + 256, q + 256, FIX, FIX))))
    found = jnp.concatenate(rows, axis=0)
    fix_found = best(fix_ref[...], fix_query, (MAIN, MAIN, FIX, FIX))
    table = jnp.concatenate([found, lanes_to_rows(code), fix_found, fix_code, flag_ref[0:1, :], jnp.zeros((5, 128), F32)], axis=0)
    for i in range(32):
        out_ref[i] = table


def split3(v):
    a = v.astype(BF)
    r = v - a.astype(F32)
    b = r.astype(BF)
    return a, b, (r - b.astype(F32)).astype(BF)


def place_kernel(ids_ref, in_ref, out_ref, flag_ref):
    core = ids_ref[0]
    base = (ids_ref[3] * 6).astype(F32)
    wide = (128, 128)
    outs = []
    spread = [onehot(iota(wide, 1) == lax.shift_right_logical(iota(wide, 0), 4) * 6 + q) for q in range(6)]
    fix_val, fix_code = [], []
    for c in range(2):
        acc = [jnp.zeros((8, 128), F32) for _ in range(6)]
        for k in range(LABELS):
            dev = c * 16 + core * 8 + k
            val = in_ref[dev, 0:8, :]
            code = in_ref[dev, 8:16, :]
            for q in range(6):
                acc[q] = acc[q] + jnp.where(code == base + q, val, 0.0)
            fix_val.append(in_ref[dev, 16:17, :])
            fix_code.append(in_ref[dev, 17:18, :])
        total = jnp.zeros((8, 128), F32)
        for q in range(6):
            for part in split3(acc[q]):
                total = total + mm(part, spread[q])
        outs.append(total)
    main = jnp.concatenate([outs[c][2 * x:2 * x + 2] for x in range(4) for c in range(2)], axis=0)
    val = jnp.concatenate(fix_val, axis=1)
    code = jnp.concatenate(fix_code, axis=1).astype(I32)
    source = lax.shift_right_arithmetic(code, 7)
    q = (code & 127).astype(F32) - base
    ok = (code >= 0) & (q >= 0.0) & (q < 6.0)
    n = val.shape[1]
    left = jnp.where(ok & (iota((16, n), 0) == lax.shift_right_arithmetic(source, 3)), val, 0.0)
    right = onehot(iota((128, n), 0).astype(F32) == (source & 7).astype(F32) * 6.0 + q)
    for part in split3(left):
        main = main + mm_t(part, right)
    out_ref[...] = jnp.maximum(main, -1.0)
    flag = in_ref[0, 16:24, :]
    for i in range(1, 32):
        flag = jnp.maximum(flag, in_ref[i, 16:24, :])
    flag_ref[...] = flag


def call(kernel, shapes, args, flops):
    specs = [pl.BlockSpec(memory_space=pltpu.SMEM)] + [pl.BlockSpec(memory_space=pltpu.VMEM)] * (len(args) - 1)
    return pl.pallas_call(
        kernel,
        out_shape=shapes,
        in_specs=specs,
        out_specs=jax.tree.map(lambda _: pl.BlockSpec(memory_space=pltpu.VMEM), shapes),
        compiler_params=pltpu.CompilerParams(vmem_limit_bytes=VMEM),
        cost_estimate=pl.CostEstimate(flops=flops, bytes_accessed=4 << 20, transcendentals=0),
    )(*args)


def struct(shape, dtype):
    return jax.ShapeDtypeStruct(shape, dtype)


def place(table, ids):
    back = lax.all_to_all(table, PLANE, split_axis=0, concat_axis=0, tiled=True)
    out, flag = call(place_kernel, (struct((16, 128), F32), struct((8, 128), F32)), (ids, back), 1 << 27)
    return out[:, :48].reshape(ROWS), flag


def general_path(main, ids, label_of_chip, core):
    tags = main.reshape(CHIPS, SLOT, D)[:, CAP, :32].astype(F32)
    label = tags[:, 0:16].reshape(MAIN)
    dest = tags[:, 16:32].reshape(MAIN)
    slot = jnp.arange(MAIN, dtype=I32)
    chip = slot // 16
    home = main_order((MAIN,), 0, core)
    away = away_order(source_of(chip, core), (label_of_chip - chip) & 7, slot & 15)
    order = jnp.where(label == (label_of_chip + 1).astype(F32), home, away)
    key_order = jnp.where(label > 0.5, order, NEVER)
    axes = ("core", "yl", "z")
    ring = [(i, (i + 1) % 16) for i in range(16)]

    def step(_, state):
        found, rows, tag = state
        scores = mm_t(main, rows)
        ok = (tag[0:1] == label[:, None]) & (tag[1:2] < order[:, None])
        found = jnp.maximum(found, jnp.max(jnp.where(ok, scores, -1.0), axis=1))
        return found, lax.ppermute(rows, axes, ring), lax.ppermute(tag, axes, ring)

    tag = jnp.stack([label, key_order])
    found, _, _ = lax.fori_loop(0, 16, step, (jnp.full((MAIN,), -1.0, F32), main, tag))
    code = jnp.where(label > 0.5, dest, -1.0)
    none = jnp.full((8, 128), -1.0, F32)
    table = jnp.concatenate([found.reshape(8, 128), code.reshape(8, 128), none], axis=0)
    out, _ = place(jnp.broadcast_to(table, (32, 24, 128)), ids)
    return out


def body(embeddings, labels, send_list):
    core = lax.axis_index("core").astype(I32)
    member = lax.axis_index(("yh", "yl", "z")).astype(I32)
    label_of_chip = member & 7
    ids = jnp.stack([core, label_of_chip, label_of_chip, member])
    packed = call(
        pack_kernel, struct((MAIN, D), BF), (ids, embeddings, labels.reshape(1, ROWS), send_list), 3 << 30
    )
    main = lax.all_to_all(
        packed.reshape(CHIPS, SLOT, D), CHIP_AXES, split_axis=0, concat_axis=0, tiled=True
    ).reshape(MAIN, D)
    swap = [(0, 1), (1, 0)]
    twin = lax.ppermute(main, "core", swap)
    fix, flag = call(fix_kernel, (struct((FIX, D), BF), struct((8, 128), F32)), (ids, main), 1 << 30)
    fix = lax.all_to_all(
        fix.reshape(LABELS, SLOT, D), GROUP_CHIPS, split_axis=0, concat_axis=0, tiled=True
    ).reshape(FIX, D)
    fix_twin = lax.ppermute(fix, "core", swap)
    table = call(score_kernel, struct((32, 24, 128), F32), (ids, flag, main, twin, fix, fix_twin), 4 << 30)
    out, flag = place(table, ids)
    return lax.cond(
        jnp.max(flag[2, 0]) > 0.0,
        lambda: general_path(main, ids, label_of_chip, core),
        lambda: out,
    )


def solution(mesh):
    fine = Mesh(mesh.devices.reshape(4, 2, 2, 2, 4), ALL)
    return jax.shard_map(body, mesh=fine, in_specs=(P(ALL, None), P(ALL), P(ALL, None)), out_specs=P(ALL), check_vma=False)
```

```python
import functools

import jax
import jax.numpy as jnp
from jax import lax
from jax.experimental import pallas as pl
from jax.experimental.pallas import tpu as pltpu
from jax.sharding import Mesh, PartitionSpec as P

F32 = jnp.float32
BF = jnp.bfloat16
I32 = jnp.int32

D = 1024
ROWS = 768
CHIPS = 64
LABELS = 8
CAP = 15
SLOT = 16
MAIN = CHIPS * SLOT
FIX = LABELS * SLOT
ALL = ("x", "core", "yh", "yl", "z")
CHIP_AXES = ("x", "yh", "yl", "z")
GROUP_CHIPS = ("yl", "z")
PLANE = ("core", "yh", "yl", "z")
NEVER = 1.0e9
VMEM = 48 * 1024 * 1024


def iota(shape, dim):
    return lax.broadcasted_iota(I32, shape, dim)


def onehot(cond):
    return jnp.where(cond, 1.0, 0.0).astype(BF)


def mm(a, b):
    return lax.dot_general(a, b, (((1,), (0,)), ((), ())), preferred_element_type=F32)


def mm_t(a, b):
    return lax.dot_general(a, b, (((1,), (1,)), ((), ())), preferred_element_type=F32)


def pack_kernel(ids_ref, emb_hbm, lab_hbm, list_hbm, out_hbm, emb_ref, lab_ref, list_ref, out_ref, sems, out_sems):
    copies = [
        pltpu.make_async_copy(src, dst, sems.at[i])
        for i, (src, dst) in enumerate(((list_hbm, list_ref), (lab_hbm, lab_ref), (emb_hbm, emb_ref)))
    ]
    for copy in copies:
        copy.start()
    rot = ids_ref[2]
    copies[0].wait()
    copies[1].wait()
    listed = onehot(iota((ROWS, ROWS), 0) == list_ref[...])
    pos = iota((16, ROWS), 1)
    group_of = lax.shift_right_logical(pos * 683, 16)
    sel = iota((16, ROWS), 0)
    vals = jnp.where(sel == 0, group_of, jnp.where(sel == 1, pos - group_of * 96, 0)).astype(F32).astype(BF)
    gd = mm_t(vals, listed)
    group = gd[0:1]
    dest = gd[1:2]
    label = lab_ref[...].reshape(1, ROWS).astype(F32)
    cluster = group * 8.0 + label
    member = iota((CHIPS, ROWS), 0).astype(F32) == cluster
    before = onehot(iota((ROWS, ROWS), 0) < iota((ROWS, ROWS), 1))
    ranks = mm(onehot(member), before)
    rank = jnp.sum(jnp.where(member, ranks, 0.0), axis=0, keepdims=True)
    count = jnp.broadcast_to(jnp.sum(jnp.where(member, 1.0, 0.0), axis=1, keepdims=True), (CHIPS, 128))
    over = jnp.maximum(count - CAP, 0.0).astype(BF)
    free = jnp.maximum(CAP - count, 0.0)
    c0, c1 = iota((CHIPS, CHIPS), 0), iota((CHIPS, CHIPS), 1)
    same = lax.shift_right_logical(c0, 3) == lax.shift_right_logical(c1, 3)
    over_pre = mm(onehot(same & (c1 < c0)), over)
    above = (CAP - 1 - (iota((CHIPS, 128), 1) & 15)).astype(F32)
    higher = jnp.clip(free, 0.0, jnp.maximum(above, 0.0)).astype(BF)
    level = onehot(free > above)
    free_pre = mm(onehot(same), higher) + mm(onehot(same & (((c1 - rot) & 7) < ((c0 - rot) & 7))), level)
    over_at = jnp.sum(jnp.where(member, over_pre[:, 0:1], 0.0), axis=0, keepdims=True) + rank - CAP
    row_code = jnp.where(rank < CAP, cluster * 16.0 + rank, 2048.0 + group * 128.0 + over_at)
    slot = iota((MAIN, 128), 0)
    at = (slot & 15).astype(F32)
    chip_hot = onehot(lax.shift_right_logical(iota((MAIN, CHIPS), 0), 4) == iota((MAIN, CHIPS), 1))
    slot_count = mm(chip_hot, count.astype(BF))
    slot_free = jnp.where(iota((MAIN, 128), 1) == (slot & 15), mm(chip_hot, free_pre.astype(BF)), 0.0)
    slot_free = jnp.sum(slot_free, axis=1, keepdims=True)
    spare = 2048.0 + (lax.shift_right_logical(slot, 7) * 128).astype(F32) + slot_free
    slot_code = jnp.where(at >= CAP, -1.0, jnp.where(at < slot_count, slot.astype(F32), spare))
    pick = jnp.concatenate([onehot(slot_code == row_code[:, b * 128:(b + 1) * 128]) for b in range(ROWS // 128)], axis=1)
    copies[2].wait()
    values = emb_ref[...].astype(F32)
    scale = lax.rsqrt(jnp.sum(values * values, axis=1, keepdims=True) + 1e-06)
    unit = (values * scale).astype(BF)
    lane = iota((128, ROWS), 0)
    tags = jnp.where(lane < 16, label + 1.0, jnp.where(lane < 32, dest, 0.0)).astype(BF)
    tag = jnp.where((iota((MAIN, 128), 1) & 15) == (slot & 15), mm_t(pick, tags), 0.0)
    tag = jnp.broadcast_to(jnp.sum(tag.reshape(CHIPS, SLOT, 128), axis=1, keepdims=True), (CHIPS, SLOT, 128)).reshape(MAIN, 128)
    copies = []
    for i, b in enumerate(range(0, D, 256)):
        part = mm(pick, unit[:, b:b + 256])
        if b == 0:
            out_ref[:, 0:128] = jnp.where(at >= CAP, tag, part[:, 0:128]).astype(BF)
            out_ref[:, 128:256] = part[:, 128:256].astype(BF)
        else:
            out_ref[:, b:b + 256] = part.astype(BF)
        copies.append(pltpu.make_async_copy(out_ref.at[:, b:b + 256], out_hbm.at[:, b:b + 256], out_sems.at[i]))
        copies[-1].start()
    for copy in copies:
        copy.wait()


def tag_rows(first, n):
    pick = onehot(iota((n, n * SLOT), 1) == iota((n, n * SLOT), 0) * SLOT + CAP)
    return mm(pick, first).astype(BF)


def tag_lanes(tags, n, k):
    spread = onehot(iota((128, n * SLOT), 0) == (iota((128, n * SLOT), 1) & 15) + 16 * k)
    wide = mm(tags, spread)
    own = iota((n, n * SLOT), 0) == lax.shift_right_logical(iota((n, n * SLOT), 1), 4)
    return jnp.sum(jnp.where(own, wide, 0.0), axis=0, keepdims=True)


def tag_columns(tags, n, ks):
    spread = onehot(lax.shift_right_logical(iota((n * SLOT, n), 0), 4) == iota((n * SLOT, n), 1))
    wide = mm(spread, tags)
    shape = (n * SLOT, 128)
    own = iota(shape, 0) & 15
    return [jnp.sum(jnp.where(iota(shape, 1) == own + 16 * k, wide, 0.0), axis=1, keepdims=True) for k in ks]


def source_of(chip, core):
    return lax.shift_right_logical(chip, 4) * 32 + core * 16 + (chip & 15)


def main_order(shape, dim, core):
    slot = iota(shape, dim)
    return (source_of(lax.shift_right_logical(slot, 4), core) * 256 + (slot & 15)).astype(F32)


def away_order(source, turn, at):
    return (source * 256 + 16 + (CAP - 1 - at) * 8 + turn).astype(F32)


def fix_order(shape, dim, core, chip, at):
    holder = lax.shift_right_logical(iota(shape, dim), 4)
    chip = chip.astype(I32)
    return away_order(source_of(chip, core), (holder - chip) & 7, at.astype(I32))


def fix_kernel(ids_ref, main_ref, out_ref, flag_ref):
    own = ids_ref[1].astype(F32)
    tags = tag_rows(main_ref[:, 0:128], CHIPS)
    label = tag_lanes(tags, CHIPS, 0)
    dest = tag_lanes(tags, CHIPS, 1)
    moved = (label > 0.5) & (label != own + 1.0)
    member = moved & (iota((LABELS, MAIN), 0).astype(F32) == label - 1.0)
    before = onehot(iota((MAIN, MAIN), 0) < iota((MAIN, MAIN), 1))
    hot = jnp.concatenate([jnp.where(member, 1.0, 0.0), jnp.zeros((LABELS, MAIN), F32)], axis=0).astype(BF)
    ranks = mm(hot, before)[0:LABELS]
    rank = jnp.sum(jnp.where(member, ranks, 0.0), axis=0, keepdims=True)
    code = jnp.where(moved & (rank < CAP), (label - 1.0) * 16.0 + rank, -1.0)
    pick = onehot(iota((FIX, MAIN), 0).astype(F32) == code)
    slot = iota((1, MAIN), 1)
    lane = iota((128, MAIN), 0)
    kind = lax.shift_right_logical(lane, 4)
    vals = jnp.where(kind == 0, 1.0, jnp.where(kind == 1, lax.shift_right_logical(slot, 4).astype(F32), jnp.where(kind == 2, (slot & 15).astype(F32), jnp.where(kind == 3, dest, 0.0)))).astype(BF)
    fixed = (FIX, 128)
    tag = jnp.where((iota(fixed, 1) & 15) == (iota(fixed, 0) & 15), mm_t(pick, vals), 0.0)
    tag = jnp.broadcast_to(jnp.sum(tag.reshape(LABELS, SLOT, 128), axis=1, keepdims=True), (LABELS, SLOT, 128)).reshape(fixed)
    for b in range(0, D, 256):
        part = mm(pick, main_ref[:, b:b + 256])
        if b == 0:
            out_ref[:, 0:128] = jnp.where((iota(fixed, 0) & 15) == CAP, tag, part[:, 0:128]).astype(BF)
            out_ref[:, 128:256] = part[:, 128:256].astype(BF)
        else:
            out_ref[:, b:b + 256] = part.astype(BF)
    worst = jnp.max(jnp.where(moved, rank, 0.0), axis=1, keepdims=True)
    flag_ref[...] = jnp.broadcast_to(jnp.where(worst >= CAP, 1.0, 0.0), (8, 128))


def lanes_to_rows(row):
    return jnp.concatenate([row[:, i * 128:(i + 1) * 128] for i in range(row.shape[1] // 128)], axis=0)


def best(keys, q_rows, q_order):
    found = jnp.full((1, q_rows.shape[0]), -1.0, F32)
    for rows, order in keys:
        scores = jnp.where(order[:, 0:1] < q_order, mm_t(rows[...], q_rows), -1.0)
        found = jnp.maximum(found, jnp.max(scores, axis=0, keepdims=True))
    return found


def main_kernel(ids_ref, own_ref, twin_ref, rows_ref, own_key_ref, twin_key_ref, code_ref):
    core = ids_ref[0]
    mine = ids_ref[1].astype(F32) + 1.0
    tags = tag_rows(own_ref[:, 0:128], CHIPS)
    twin_tags = tag_rows(twin_ref[:, 0:128], CHIPS)

    def main_key(t, c):
        (label,) = tag_columns(t, CHIPS, (0,))
        return jnp.broadcast_to(jnp.where(label == mine, main_order((MAIN, 1), 0, c), NEVER), (MAIN, 128))

    own_key_ref[...] = main_key(tags, core)
    twin_key_ref[...] = main_key(twin_tags, 1 - core)
    valid = tag_lanes(tags, CHIPS, 0) == mine
    query = jnp.where(valid, main_order((1, MAIN), 1, core), -1.0)
    dest = tag_lanes(tags, CHIPS, 1).astype(I32)
    home = lax.shift_right_logical(dest * 43, 8)
    member = valid & (iota((16, MAIN), 0) == home)
    before = onehot(iota((MAIN, MAIN), 0) < iota((MAIN, MAIN), 1))
    ranks = mm(onehot(member), before)
    rank = jnp.sum(jnp.where(member, ranks, 0.0), axis=0, keepdims=True)
    rank = jnp.where(valid, rank, -1.0)
    hot = onehot(iota((128, MAIN), 0).astype(F32) == rank)
    source = source_of(lax.shift_right_logical(iota((1, MAIN), 1), 4), core)
    at = source * 6 + dest - home * 6 + 1
    high = lax.shift_right_logical(at, 4)
    parts = [jnp.where(member, part.astype(F32), 0.0).astype(BF) for part in (high, at - high * 16)]
    code_ref[...] = mm_t(parts[0], hot) * 16.0 + mm_t(parts[1], hot) - 1.0
    worst = jnp.max(rank, axis=1, keepdims=True)
    found = [
        best(
            ((own_ref[0:q + 256, :], own_key_ref[0:q + 256, :]), (twin_ref[0:q + 256, :], twin_key_ref[0:q + 256, :])),
            own_ref[q:q + 256, :],
            query[:, q:q + 256],
        )
        for q in range(0, MAIN, 256)
    ]
    found = jnp.concatenate(found, axis=1)
    worst = jnp.broadcast_to(worst, (1, MAIN))
    rows = jnp.concatenate([query, found, home.astype(F32), worst, rank, jnp.zeros((3, MAIN), F32)], axis=0)
    rows_ref[...] = rows


def last_kernel(ids_ref, flag_ref, rows_ref, own_key_ref, twin_key_ref, code_ref, own_ref, twin_ref, fix_ref, fix_twin_ref, out_ref):
    core = ids_ref[0]
    fix_tags = tag_rows(fix_ref[:, 0:128], LABELS)
    fix_twin_tags = tag_rows(fix_twin_ref[:, 0:128], LABELS)

    def fix_key(t, c):
        valid, chip, at = tag_columns(t, LABELS, (0, 1, 2))
        return jnp.where(valid > 0.5, fix_order((FIX, 1), 0, c, chip, at), NEVER)

    fix_rows = jnp.concatenate([fix_ref[...], fix_twin_ref[...]], axis=0)
    fix_keys = ((fix_rows, jnp.concatenate([fix_key(fix_tags, core), fix_key(fix_twin_tags, 1 - core)], axis=0)),)
    fix_valid = tag_lanes(fix_tags, LABELS, 0) > 0.5
    fix_chip = tag_lanes(fix_tags, LABELS, 1)
    fix_query = jnp.where(fix_valid, fix_order((1, FIX), 1, core, fix_chip, tag_lanes(fix_tags, LABELS, 2)), -1.0)
    fix_source = source_of(fix_chip.astype(I32), core).astype(F32)
    fix_code = jnp.where(fix_valid, fix_source * 128.0 + tag_lanes(fix_tags, LABELS, 3), -1.0)
    fix_found = best(((own_ref, own_key_ref), (twin_ref, twin_key_ref)) + fix_keys, fix_ref[...], fix_query)
    found = jnp.maximum(best(fix_keys, own_ref[...], rows_ref[0:1, :]), rows_ref[1:2, :])
    here = iota((16, MAIN), 0).astype(F32) == rows_ref[2:3, :]
    value = jnp.concatenate([jnp.where(here, part.astype(F32), 0.0).astype(BF) for part in split3(found)], axis=0)
    value = mm_t(value, onehot(iota((128, MAIN), 0).astype(F32) == rows_ref[4:5, :]))
    value = value[0:16] + value[16:32] + value[32:48]
    flag = jnp.maximum(flag_ref[0:1, :], jnp.where(rows_ref[3:4, 0:128] >= 128.0, 1.0, 0.0))
    common = jnp.concatenate([fix_found, fix_code, flag, jnp.zeros((3, 128), F32)], axis=0)
    for m in range(16):
        table = jnp.concatenate([value[m:m + 1], code_ref[m:m + 1], common], axis=0)
        out_ref[m] = table
        out_ref[16 + m] = table


def split3(v):
    a = v.astype(BF)
    r = v - a.astype(F32)
    b = r.astype(BF)
    return a, b, (r - b.astype(F32)).astype(BF)


def place_kernel(ids_ref, in_ref, out_ref):
    core = ids_ref[0]
    base = (ids_ref[3] * 6).astype(F32)
    wide = (128, 128)
    outs = []
    spread = [onehot(iota(wide, 1) == lax.shift_right_logical(iota(wide, 0), 4) * 6 + q) for q in range(6)]
    fix_val, fix_code = [], []
    for c in range(2):
        acc = [jnp.zeros((8, 128), F32) for _ in range(6)]
        for k in range(LABELS):
            dev = c * 16 + core * 8 + k
            val = in_ref[dev, 0:8, :]
            code = in_ref[dev, 8:16, :]
            for q in range(6):
                acc[q] = acc[q] + jnp.where(code == base + q, val, 0.0)
            fix_val.append(in_ref[dev, 16:17, :])
            fix_code.append(in_ref[dev, 17:18, :])
        total = jnp.zeros((8, 128), F32)
        for q in range(6):
            for part in split3(acc[q]):
                total = total + mm(part, spread[q])
        outs.append(total)
    main = jnp.concatenate([outs[c][2 * x:2 * x + 2] for x in range(4) for c in range(2)], axis=0)
    val = jnp.concatenate(fix_val, axis=1)
    code = jnp.concatenate(fix_code, axis=1).astype(I32)
    source = lax.shift_right_arithmetic(code, 7)
    q = (code & 127).astype(F32) - base
    ok = (code >= 0) & (q >= 0.0) & (q < 6.0)
    n = val.shape[1]
    left = jnp.where(ok & (iota((16, n), 0) == lax.shift_right_arithmetic(source, 3)), val, 0.0)
    right = onehot(iota((128, n), 0).astype(F32) == (source & 7).astype(F32) * 6.0 + q)
    for part in split3(left):
        main = main + mm_t(part, right)
    out_ref[...] = jnp.maximum(main, -1.0)


def put_kernel(ids_ref, in_ref, out_ref, flag_ref):
    core = ids_ref[0]
    base = ids_ref[3] * 6
    val, at = [], []
    for c in range(2):
        for k in range(LABELS):
            block = in_ref[c * 16 + core * 8 + k]
            val.append(block[0:1])
            at.append(block[1:2].astype(I32))
            val.append(block[2:3])
            code = block[3:4].astype(I32)
            q = (code & 127) - base
            ok = (code >= 0) & (q >= 0) & (q < 6)
            at.append(jnp.where(ok, lax.shift_right_arithmetic(code, 7) * 6 + q, -1))
    val = jnp.concatenate(val, axis=1)
    at = jnp.concatenate(at, axis=1)
    n = val.shape[1]
    left = jnp.where(iota((8, n), 0) == lax.shift_right_arithmetic(at, 7), val, 0.0)
    right = onehot(iota((128, n), 0) == (at & 127))
    out = jnp.zeros((8, 128), F32)
    for part in split3(left):
        out = out + mm_t(part, right)
    out_ref[...] = jnp.maximum(out, -1.0)[0:6]
    flag = in_ref[0]
    for i in range(1, 32):
        flag = jnp.maximum(flag, in_ref[i])
    flag_ref[...] = flag


def call(kernel, shapes, args, flops, memory=pltpu.VMEM, scratch=(), vmem=VMEM, out_memory=pltpu.VMEM):
    specs = [pl.BlockSpec(memory_space=pltpu.SMEM)] + [pl.BlockSpec(memory_space=memory)] * (len(args) - 1)
    return pl.pallas_call(
        kernel,
        out_shape=shapes,
        in_specs=specs,
        out_specs=jax.tree.map(lambda _: pl.BlockSpec(memory_space=out_memory), shapes),
        scratch_shapes=scratch,
        compiler_params=pltpu.CompilerParams(vmem_limit_bytes=vmem),
        cost_estimate=pl.CostEstimate(flops=flops, bytes_accessed=4 << 20, transcendentals=0),
    )(*args)


def struct(shape, dtype):
    return jax.ShapeDtypeStruct(shape, dtype)


def place(table, ids):
    back = lax.all_to_all(table, PLANE, split_axis=0, concat_axis=0, tiled=True)
    out = call(place_kernel, struct((16, 128), F32), (ids, back), 1 << 27)
    return out[:, :48].reshape(ROWS)


def general_path(main, ids, label_of_chip, core):
    tags = main.reshape(CHIPS, SLOT, D)[:, CAP, :32].astype(F32)
    label = tags[:, 0:16].reshape(MAIN)
    dest = tags[:, 16:32].reshape(MAIN)
    slot = jnp.arange(MAIN, dtype=I32)
    chip = slot // 16
    home = main_order((MAIN,), 0, core)
    away = away_order(source_of(chip, core), (label_of_chip - chip) & 7, slot & 15)
    order = jnp.where(label == (label_of_chip + 1).astype(F32), home, away)
    key_order = jnp.where(label > 0.5, order, NEVER)
    axes = ("core", "yl", "z")
    ring = [(i, (i + 1) % 16) for i in range(16)]

    def step(_, state):
        found, rows, tag = state
        scores = mm_t(main, rows)
        ok = (tag[0:1] == label[:, None]) & (tag[1:2] < order[:, None])
        found = jnp.maximum(found, jnp.max(jnp.where(ok, scores, -1.0), axis=1))
        return found, lax.ppermute(rows, axes, ring), lax.ppermute(tag, axes, ring)

    tag = jnp.stack([label, key_order])
    found, _, _ = lax.fori_loop(0, 16, step, (jnp.full((MAIN,), -1.0, F32), main, tag))
    code = jnp.where(label > 0.5, dest, -1.0)
    none = jnp.full((8, 128), -1.0, F32)
    table = jnp.concatenate([found.reshape(8, 128), code.reshape(8, 128), none], axis=0)
    return place(jnp.broadcast_to(table, (32, 24, 128)), ids)


def body(embeddings, labels, send_list):
    core = lax.axis_index("core").astype(I32)
    member = lax.axis_index(("yh", "yl", "z")).astype(I32)
    label_of_chip = member & 7
    ids = jnp.stack([core, label_of_chip, label_of_chip, member])
    packed = call(
        pack_kernel,
        struct((MAIN, D), BF),
        (ids, embeddings, labels, send_list),
        3 << 30,
        pltpu.HBM,
        (
            pltpu.VMEM((ROWS, D), BF),
            pltpu.VMEM((ROWS,), I32),
            pltpu.VMEM((1, ROWS), I32),
            pltpu.VMEM((MAIN, D), BF),
            pltpu.SemaphoreType.DMA((3,)),
            pltpu.SemaphoreType.DMA((4,)),
        ),
        56 * 1024 * 1024,
        pltpu.HBM,
    )
    main = lax.all_to_all(
        packed.reshape(CHIPS, SLOT, D), CHIP_AXES, split_axis=0, concat_axis=0, tiled=True
    ).reshape(MAIN, D)
    swap = [(0, 1), (1, 0)]
    twin = lax.ppermute(main, "core", swap)
    fix, flag = call(fix_kernel, (struct((FIX, D), BF), struct((8, 128), F32)), (ids, main), 1 << 30)
    fix = lax.all_to_all(
        fix.reshape(LABELS, SLOT, D), GROUP_CHIPS, split_axis=0, concat_axis=0, tiled=True
    ).reshape(FIX, D)
    wide = struct((MAIN, 128), F32)
    shapes = (struct((8, MAIN), F32), wide, wide, struct((16, 128), F32))
    parts = call(main_kernel, shapes, (ids, main, twin), 3 << 30)
    fix, code = lax.optimization_barrier((fix, parts[3]))
    fix_twin = lax.ppermute(fix, "core", swap)
    table = call(last_kernel, struct((32, 8, 128), F32), (ids, flag, *parts[:3], code, main, twin, fix, fix_twin), 1 << 30)
    back = lax.all_to_all(table, PLANE, split_axis=0, concat_axis=0, tiled=True)
    out, flag = call(put_kernel, (struct((6, 128), F32), struct((8, 128), F32)), (ids, back), 1 << 27)
    return lax.cond(
        flag[4, 0] > 0.0,
        lambda: general_path(main, ids, label_of_chip, core),
        lambda: out.reshape(ROWS),
    )


def solution(mesh):
    fine = Mesh(mesh.devices.reshape(4, 2, 2, 2, 4), ALL)
    return jax.shard_map(body, mesh=fine, in_specs=(P(ALL, None), P(ALL), P(ALL, None)), out_specs=P(ALL), check_vma=False)
```

```python
import functools

import jax
import jax.numpy as jnp
from jax import lax
from jax.experimental import pallas as pl
from jax.experimental.pallas import tpu as pltpu
from jax.sharding import Mesh, PartitionSpec as P

F32 = jnp.float32
BF = jnp.bfloat16
I32 = jnp.int32

D = 1024
ROWS = 768
CHIPS = 64
LABELS = 8
CAP = 15
SLOT = 16
MAIN = CHIPS * SLOT
FIX = LABELS * SLOT
ALL = ("x", "core", "yh", "yl", "z")
CHIP_AXES = ("x", "yh", "yl", "z")
GROUP_CHIPS = ("yl", "z")
PLANE = ("core", "yh", "yl", "z")
NEVER = 1.0e9
VMEM = 24 * 1024 * 1024


def iota(shape, dim):
    return lax.broadcasted_iota(I32, shape, dim)


def onehot(cond):
    return jnp.where(cond, 1.0, 0.0).astype(BF)


def mm(a, b):
    return lax.dot_general(a, b, (((1,), (0,)), ((), ())), preferred_element_type=F32)


def mm_t(a, b):
    return lax.dot_general(a, b, (((1,), (1,)), ((), ())), preferred_element_type=F32)


def earlier(hot):
    n, width = hot.shape
    parts = width // 128
    rows = jnp.concatenate([hot[:, i * 128:(i + 1) * 128] for i in range(parts)], axis=0)
    inside = mm(rows.astype(BF), onehot(iota((128, 128), 0) < iota((128, 128), 1)))
    total = jnp.broadcast_to(jnp.sum(rows, axis=1, keepdims=True), rows.shape).astype(BF)
    m = parts * n
    a, b = iota((m, m), 0), iota((m, m), 1)
    inside = inside + mm(onehot(((a & (n - 1)) == (b & (n - 1))) & (b < a)), total)
    return jnp.concatenate([inside[i * n:(i + 1) * n] for i in range(parts)], axis=1)


def pack_kernel(ids_ref, emb_hbm, lab_hbm, list_hbm, out_hbm, emb_ref, lab_ref, list_ref, out_ref, sems, out_sems):
    copies = [
        pltpu.make_async_copy(src, dst, sems.at[i])
        for i, (src, dst) in enumerate(((list_hbm, list_ref), (lab_hbm, lab_ref), (emb_hbm, emb_ref)))
    ]
    for copy in copies:
        copy.start()
    rot = ids_ref[2]
    copies[0].wait()
    copies[1].wait()
    listed = onehot(iota((ROWS, ROWS), 0) == list_ref[...])
    pos = iota((16, ROWS), 1)
    group_of = lax.shift_right_logical(pos * 683, 16)
    sel = iota((16, ROWS), 0)
    vals = jnp.where(sel == 0, group_of, jnp.where(sel == 1, pos - group_of * 96, 0)).astype(F32).astype(BF)
    gd = mm_t(vals, listed)
    group = gd[0:1]
    dest = gd[1:2]
    label = lab_ref[...].reshape(1, ROWS).astype(F32)
    cluster = group * 8.0 + label
    member = iota((CHIPS, ROWS), 0).astype(F32) == cluster
    ranks = earlier(jnp.where(member, 1.0, 0.0))
    rank = jnp.sum(jnp.where(member, ranks, 0.0), axis=0, keepdims=True)
    count = jnp.broadcast_to(jnp.sum(jnp.where(member, 1.0, 0.0), axis=1, keepdims=True), (CHIPS, 128))
    over = jnp.maximum(count - CAP, 0.0).astype(BF)
    free = jnp.maximum(CAP - count, 0.0)
    c0, c1 = iota((CHIPS, CHIPS), 0), iota((CHIPS, CHIPS), 1)
    same = lax.shift_right_logical(c0, 3) == lax.shift_right_logical(c1, 3)
    over_pre = mm(onehot(same & (c1 < c0)), over)
    above = (CAP - 1 - (iota((CHIPS, 128), 1) & 15)).astype(F32)
    higher = jnp.clip(free, 0.0, jnp.maximum(above, 0.0)).astype(BF)
    level = onehot(free > above)
    free_pre = mm(onehot(same), higher) + mm(onehot(same & (((c1 - rot) & 7) < ((c0 - rot) & 7))), level)
    over_at = jnp.sum(jnp.where(member, over_pre[:, 0:1], 0.0), axis=0, keepdims=True) + rank - CAP
    row_code = jnp.where(rank < CAP, cluster * 16.0 + rank, 2048.0 + group * 128.0 + over_at)
    slot = iota((MAIN, 128), 0)
    at = (slot & 15).astype(F32)
    chip_hot = onehot(lax.shift_right_logical(iota((MAIN, CHIPS), 0), 4) == iota((MAIN, CHIPS), 1))
    slot_count = mm(chip_hot, count.astype(BF))
    slot_free = jnp.where(iota((MAIN, 128), 1) == (slot & 15), mm(chip_hot, free_pre.astype(BF)), 0.0)
    slot_free = jnp.sum(slot_free, axis=1, keepdims=True)
    spare = 2048.0 + (lax.shift_right_logical(slot, 7) * 128).astype(F32) + slot_free
    slot_code = jnp.where(at >= CAP, -1.0, jnp.where(at < slot_count, slot.astype(F32), spare))
    pick = jnp.concatenate([onehot(slot_code == row_code[:, b * 128:(b + 1) * 128]) for b in range(ROWS // 128)], axis=1)
    copies[2].wait()
    values = emb_ref[...].astype(F32)
    scale = lax.rsqrt(jnp.sum(values * values, axis=1, keepdims=True) + 1e-06)
    unit = (values * scale).astype(BF)
    lane = iota((128, ROWS), 0)
    tags = jnp.where(lane < 16, label + 1.0, jnp.where(lane < 32, dest, 0.0)).astype(BF)
    tag = jnp.where((iota((MAIN, 128), 1) & 15) == (slot & 15), mm_t(pick, tags), 0.0)
    tag = jnp.broadcast_to(jnp.sum(tag.reshape(CHIPS, SLOT, 128), axis=1, keepdims=True), (CHIPS, SLOT, 128)).reshape(MAIN, 128)
    copies = []
    for i, b in enumerate(range(0, D, 256)):
        part = mm(pick, unit[:, b:b + 256])
        if b == 0:
            out_ref[:, 0:128] = jnp.where(at >= CAP, tag, part[:, 0:128]).astype(BF)
            out_ref[:, 128:256] = part[:, 128:256].astype(BF)
        else:
            out_ref[:, b:b + 256] = part.astype(BF)
        copies.append(pltpu.make_async_copy(out_ref.at[:, b:b + 256], out_hbm.at[:, b:b + 256], out_sems.at[i]))
        copies[-1].start()
    for copy in copies:
        copy.wait()


def tag_rows(first, n):
    pick = onehot(iota((n, n * SLOT), 1) == iota((n, n * SLOT), 0) * SLOT + CAP)
    return mm(pick, first).astype(BF)


def tag_lanes(tags, n, k):
    spread = onehot(iota((128, n * SLOT), 0) == (iota((128, n * SLOT), 1) & 15) + 16 * k)
    wide = mm(tags, spread)
    own = iota((n, n * SLOT), 0) == lax.shift_right_logical(iota((n, n * SLOT), 1), 4)
    return jnp.sum(jnp.where(own, wide, 0.0), axis=0, keepdims=True)


def tag_columns(tags, n, ks):
    spread = onehot(lax.shift_right_logical(iota((n * SLOT, n), 0), 4) == iota((n * SLOT, n), 1))
    wide = mm(spread, tags)
    shape = (n * SLOT, 128)
    own = iota(shape, 0) & 15
    return [jnp.sum(jnp.where(iota(shape, 1) == own + 16 * k, wide, 0.0), axis=1, keepdims=True) for k in ks]


def source_of(chip, core):
    return lax.shift_right_logical(chip, 4) * 32 + core * 16 + (chip & 15)


def main_order(shape, dim, core):
    slot = iota(shape, dim)
    return (source_of(lax.shift_right_logical(slot, 4), core) * 256 + (slot & 15)).astype(F32)


def away_order(source, turn, at):
    return (source * 256 + 16 + (CAP - 1 - at) * 8 + turn).astype(F32)


def fix_order(shape, dim, core, chip, at):
    holder = lax.shift_right_logical(iota(shape, dim), 4)
    chip = chip.astype(I32)
    return away_order(source_of(chip, core), (holder - chip) & 7, at.astype(I32))


def fix_kernel(ids_ref, main_ref, out_ref, flag_ref):
    own = ids_ref[1].astype(F32)
    tags = tag_rows(main_ref[:, 0:128], CHIPS)
    label = tag_lanes(tags, CHIPS, 0)
    dest = tag_lanes(tags, CHIPS, 1)
    moved = (label > 0.5) & (label != own + 1.0)
    member = moved & (iota((LABELS, MAIN), 0).astype(F32) == label - 1.0)
    ranks = earlier(jnp.where(member, 1.0, 0.0))
    rank = jnp.sum(jnp.where(member, ranks, 0.0), axis=0, keepdims=True)
    code = jnp.where(moved & (rank < CAP), (label - 1.0) * 16.0 + rank, -1.0)
    pick = onehot(iota((FIX, MAIN), 0).astype(F32) == code)
    slot = iota((1, MAIN), 1)
    lane = iota((128, MAIN), 0)
    kind = lax.shift_right_logical(lane, 4)
    vals = jnp.where(kind == 0, 1.0, jnp.where(kind == 1, lax.shift_right_logical(slot, 4).astype(F32), jnp.where(kind == 2, (slot & 15).astype(F32), jnp.where(kind == 3, dest, 0.0)))).astype(BF)
    fixed = (FIX, 128)
    tag = jnp.where((iota(fixed, 1) & 15) == (iota(fixed, 0) & 15), mm_t(pick, vals), 0.0)
    tag = jnp.broadcast_to(jnp.sum(tag.reshape(LABELS, SLOT, 128), axis=1, keepdims=True), (LABELS, SLOT, 128)).reshape(fixed)
    for b in range(0, D, 256):
        part = mm(pick, main_ref[:, b:b + 256])
        if b == 0:
            out_ref[:, 0:128] = jnp.where((iota(fixed, 0) & 15) == CAP, tag, part[:, 0:128]).astype(BF)
            out_ref[:, 128:256] = part[:, 128:256].astype(BF)
        else:
            out_ref[:, b:b + 256] = part.astype(BF)
    worst = jnp.max(jnp.where(moved, rank, 0.0), axis=1, keepdims=True)
    flag_ref[...] = jnp.broadcast_to(jnp.where(worst >= CAP, 1.0, 0.0), (8, 128))


def lanes_to_rows(row):
    return jnp.concatenate([row[:, i * 128:(i + 1) * 128] for i in range(row.shape[1] // 128)], axis=0)


def best(keys, q_rows, q_order):
    found = jnp.full((1, q_rows.shape[0]), -1.0, F32)
    for rows, order in keys:
        scores = jnp.where(order[:, 0:1] < q_order, mm_t(rows[...], q_rows), -1.0)
        found = jnp.maximum(found, jnp.max(scores, axis=0, keepdims=True))
    return found


def main_kernel(ids_ref, own_ref, twin_ref, rows_ref, own_key_ref, code_ref, keep_hbm, sem):
    keep = pltpu.make_async_copy(own_ref, keep_hbm, sem)
    keep.start()
    core = ids_ref[0]
    mine = ids_ref[1].astype(F32) + 1.0
    tags = tag_rows(own_ref[:, 0:128], CHIPS)
    twin_tags = tag_rows(twin_ref[:, 0:128], CHIPS)

    def main_key(t, c):
        (label,) = tag_columns(t, CHIPS, (0,))
        return jnp.broadcast_to(jnp.where(label == mine, main_order((MAIN, 1), 0, c), NEVER), (MAIN, 128))

    own_key_ref[...] = main_key(tags, core)
    twin_key = main_key(twin_tags, 1 - core)
    valid = tag_lanes(tags, CHIPS, 0) == mine
    query = jnp.where(valid, main_order((1, MAIN), 1, core), -1.0)
    dest = tag_lanes(tags, CHIPS, 1).astype(I32)
    home = lax.shift_right_logical(dest * 43, 8)
    member = valid & (iota((16, MAIN), 0) == home)
    ranks = earlier(jnp.where(member, 1.0, 0.0))
    rank = jnp.sum(jnp.where(member, ranks, 0.0), axis=0, keepdims=True)
    rank = jnp.where(valid, rank, -1.0)
    hot = onehot(iota((128, MAIN), 0).astype(F32) == rank)
    source = source_of(lax.shift_right_logical(iota((1, MAIN), 1), 4), core)
    at = source * 6 + dest - home * 6 + 1
    high = lax.shift_right_logical(at, 4)
    parts = [jnp.where(member, part.astype(F32), 0.0).astype(BF) for part in (high, at - high * 16)]
    code_ref[...] = mm_t(parts[0], hot) * 16.0 + mm_t(parts[1], hot) - 1.0
    worst = jnp.max(rank, axis=1, keepdims=True)
    found = [
        best(
            ((own_ref[0:q + 256, :], own_key_ref[0:q + 256, :]), (twin_ref[0:q + 256, :], twin_key[0:q + 256, :])),
            own_ref[q:q + 256, :],
            query[:, q:q + 256],
        )
        for q in range(0, MAIN, 256)
    ]
    found = jnp.concatenate(found, axis=1)
    worst = jnp.broadcast_to(worst, (1, MAIN))
    rows = jnp.concatenate([query, found, home.astype(F32), worst, rank, jnp.zeros((3, MAIN), F32)], axis=0)
    rows_ref[...] = rows
    keep.wait()


def last_kernel(ids_ref, flag_ref, rows_ref, own_key_ref, code_ref, own_ref, fix_ref, fix_twin_ref, out_ref):
    core = ids_ref[0]
    fix_rows = jnp.concatenate([fix_ref[...], fix_twin_ref[...]], axis=0)
    orders, queries, codes = [], [], []
    for ref, c in ((fix_ref, core), (fix_twin_ref, 1 - core)):
        tags = tag_rows(ref[:, 0:128], LABELS)
        valid, chip, at = tag_columns(tags, LABELS, (0, 1, 2))
        orders.append(jnp.where(valid > 0.5, fix_order((FIX, 1), 0, c, chip, at), NEVER))
        valid = tag_lanes(tags, LABELS, 0) > 0.5
        chip = tag_lanes(tags, LABELS, 1)
        queries.append(jnp.where(valid, fix_order((1, FIX), 1, c, chip, tag_lanes(tags, LABELS, 2)), -1.0))
        source = source_of(chip.astype(I32), c).astype(F32)
        codes.append(jnp.where(valid, source * 128.0 + tag_lanes(tags, LABELS, 3), -1.0))
    fix_keys = ((fix_rows, jnp.concatenate(orders, axis=0)),)
    fix_found = best(((own_ref, own_key_ref),) + fix_keys, fix_rows, jnp.concatenate(queries, axis=1))
    found = jnp.maximum(best(fix_keys, own_ref[...], rows_ref[0:1, :]), rows_ref[1:2, :])
    here = iota((16, MAIN), 0).astype(F32) == rows_ref[2:3, :]
    value = jnp.concatenate([jnp.where(here, part.astype(F32), 0.0).astype(BF) for part in split3(found)], axis=0)
    value = mm_t(value, onehot(iota((128, MAIN), 0).astype(F32) == rows_ref[4:5, :]))
    value = value[0:16] + value[16:32] + value[32:48]
    flag = jnp.maximum(flag_ref[0:1, :], jnp.where(rows_ref[3:4, 0:128] >= 128.0, 1.0, 0.0))
    common = jnp.concatenate([lanes_to_rows(fix_found)] + codes + [flag, jnp.zeros((1, 128), F32)], axis=0)
    for m in range(16):
        table = jnp.concatenate([value[m:m + 1], code_ref[m:m + 1], common], axis=0)
        out_ref[m] = table
        out_ref[16 + m] = table


def split3(v):
    a = v.astype(BF)
    r = v - a.astype(F32)
    b = r.astype(BF)
    return a, b, (r - b.astype(F32)).astype(BF)


def place_kernel(ids_ref, in_ref, out_ref):
    core = ids_ref[0]
    base = (ids_ref[3] * 6).astype(F32)
    wide = (128, 128)
    outs = []
    spread = [onehot(iota(wide, 1) == lax.shift_right_logical(iota(wide, 0), 4) * 6 + q) for q in range(6)]
    fix_val, fix_code = [], []
    for c in range(2):
        acc = [jnp.zeros((8, 128), F32) for _ in range(6)]
        for k in range(LABELS):
            dev = c * 16 + core * 8 + k
            val = in_ref[dev, 0:8, :]
            code = in_ref[dev, 8:16, :]
            for q in range(6):
                acc[q] = acc[q] + jnp.where(code == base + q, val, 0.0)
            fix_val.append(in_ref[dev, 16:17, :])
            fix_code.append(in_ref[dev, 17:18, :])
        total = jnp.zeros((8, 128), F32)
        for q in range(6):
            for part in split3(acc[q]):
                total = total + mm(part, spread[q])
        outs.append(total)
    main = jnp.concatenate([outs[c][2 * x:2 * x + 2] for x in range(4) for c in range(2)], axis=0)
    val = jnp.concatenate(fix_val, axis=1)
    code = jnp.concatenate(fix_code, axis=1).astype(I32)
    source = lax.shift_right_arithmetic(code, 7)
    q = (code & 127).astype(F32) - base
    ok = (code >= 0) & (q >= 0.0) & (q < 6.0)
    n = val.shape[1]
    left = jnp.where(ok & (iota((16, n), 0) == lax.shift_right_arithmetic(source, 3)), val, 0.0)
    right = onehot(iota((128, n), 0).astype(F32) == (source & 7).astype(F32) * 6.0 + q)
    for part in split3(left):
        main = main + mm_t(part, right)
    out_ref[...] = jnp.maximum(main, -1.0)


def put_kernel(ids_ref, in_ref, out_ref, flag_ref):
    core = ids_ref[0]
    base = ids_ref[3] * 6
    outs = []
    for c in range(2):
        val, at = [], []
        for k in range(LABELS):
            block = in_ref[c * 16 + core * 8 + k]
            val += [block[0:1], block[2:3], block[3:4]]
            code = block[4:6].astype(I32)
            q = (code & 127) - base
            ok = (code >= 0) & (q >= 0) & (q < 6)
            fix_at = jnp.where(ok, lax.shift_right_arithmetic(code, 7) * 6 + q, -1)
            at += [block[1:2].astype(I32), fix_at[0:1], fix_at[1:2]]
        val = jnp.concatenate(val, axis=1) + 2.0
        at = jnp.concatenate(at, axis=1)
        n = val.shape[1]
        left = jnp.where(iota((8, n), 0) == lax.shift_right_arithmetic(at, 7), val, 0.0)
        out = mm_t(jnp.concatenate(split3(left), axis=0), onehot(iota((128, n), 0) == (at & 127)))
        outs.append(out[0:8] + out[8:16] + out[16:24])
    out_ref[...] = jnp.maximum(jnp.maximum(outs[0], outs[1]) - 2.0, -1.0)[0:6]
    flag_ref[0] = jnp.max(jnp.max(in_ref[...], axis=0)[6:7]).astype(I32)


def call(kernel, shapes, args, flops, memory=pltpu.VMEM, scratch=(), vmem=VMEM, out_memory=pltpu.VMEM, out_specs=None):
    specs = [pl.BlockSpec(memory_space=pltpu.SMEM)] + [pl.BlockSpec(memory_space=memory)] * (len(args) - 1)
    return pl.pallas_call(
        kernel,
        out_shape=shapes,
        in_specs=specs,
        out_specs=out_specs or jax.tree.map(lambda _: pl.BlockSpec(memory_space=out_memory), shapes),
        scratch_shapes=scratch,
        compiler_params=pltpu.CompilerParams(vmem_limit_bytes=vmem),
        cost_estimate=pl.CostEstimate(flops=flops, bytes_accessed=4 << 20, transcendentals=0),
    )(*args)


def struct(shape, dtype):
    return jax.ShapeDtypeStruct(shape, dtype)


def place(table, ids):
    back = lax.all_to_all(table, PLANE, split_axis=0, concat_axis=0, tiled=True)
    out = call(place_kernel, struct((16, 128), F32), (ids, back), 1 << 27)
    return out[:, :48].reshape(ROWS)


def general_path(main, ids, label_of_chip, core):
    tags = main[CAP::SLOT, :32].astype(F32)
    label = tags[:, 0:16].reshape(MAIN)
    dest = tags[:, 16:32].reshape(MAIN)
    slot = jnp.arange(MAIN, dtype=I32)
    chip = slot // 16
    home = main_order((MAIN,), 0, core)
    away = away_order(source_of(chip, core), (label_of_chip - chip) & 7, slot & 15)
    order = jnp.where(label == (label_of_chip + 1).astype(F32), home, away)
    key_order = jnp.where(label > 0.5, order, NEVER)
    axes = ("core", "yl", "z")
    ring = [(i, (i + 1) % 16) for i in range(16)]

    def step(_, state):
        found, rows, tag = state
        scores = mm_t(main, rows)
        ok = (tag[0:1] == label[:, None]) & (tag[1:2] < order[:, None])
        found = jnp.maximum(found, jnp.max(jnp.where(ok, scores, -1.0), axis=1))
        return found, lax.ppermute(rows, axes, ring), lax.ppermute(tag, axes, ring)

    tag = jnp.stack([label, key_order])
    found, _, _ = lax.fori_loop(0, 16, step, (jnp.full((MAIN,), -1.0, F32), main, tag))
    code = jnp.where(label > 0.5, dest, -1.0)
    none = jnp.full((8, 128), -1.0, F32)
    table = jnp.concatenate([found.reshape(8, 128), code.reshape(8, 128), none], axis=0)
    return place(jnp.broadcast_to(table, (32, 24, 128)), ids)


def pack_call(ids, embeddings, labels, send_list):
    return call(
        pack_kernel,
        struct((MAIN, D), BF),
        (ids, embeddings, labels, send_list),
        3 << 30,
        pltpu.HBM,
        (
            pltpu.VMEM((ROWS, D), BF),
            pltpu.VMEM((ROWS,), I32),
            pltpu.VMEM((1, ROWS), I32),
            pltpu.VMEM((MAIN, D), BF),
            pltpu.SemaphoreType.DMA((3,)),
            pltpu.SemaphoreType.DMA((4,)),
        ),
        56 * 1024 * 1024,
        pltpu.HBM,
    )


def fix_call(ids, main):
    return call(fix_kernel, (struct((FIX, D), BF), struct((8, 128), F32)), (ids, main), 1 << 30)


def main_call(ids, main, twin):
    wide = struct((MAIN, 128), F32)
    shapes = (struct((8, MAIN), F32), wide, struct((16, 128), F32), struct((MAIN, D), BF))
    specs = tuple(pl.BlockSpec(memory_space=pltpu.VMEM) for _ in range(3)) + (pl.BlockSpec(memory_space=pltpu.HBM),)
    return call(main_kernel, shapes, (ids, main, twin), 3 << 30, scratch=(pltpu.SemaphoreType.DMA,), out_specs=specs)


def last_call(*args):
    return call(last_kernel, struct((32, 8, 128), F32), args, 1 << 30)


def put_call(ids, back):
    specs = (pl.BlockSpec(memory_space=pltpu.VMEM), pl.BlockSpec(memory_space=pltpu.SMEM))
    return call(put_kernel, (struct((6, 128), F32), struct((1,), I32)), (ids, back), 1 << 27, out_specs=specs)


def body(embeddings, labels, send_list):
    core = lax.axis_index("core").astype(I32)
    member = lax.axis_index(("yh", "yl", "z")).astype(I32)
    label_of_chip = member & 7
    ids = jnp.stack([core, label_of_chip, label_of_chip, member])
    packed = pack_call(ids, embeddings, labels, send_list)
    main = lax.all_to_all(
        packed.reshape(CHIPS, SLOT, D), CHIP_AXES, split_axis=0, concat_axis=0, tiled=True
    ).reshape(MAIN, D)
    swap = [(0, 1), (1, 0)]
    twin = lax.ppermute(main, "core", swap)
    fix, flag = fix_call(ids, main)
    fix = lax.all_to_all(
        fix.reshape(LABELS, SLOT, D), GROUP_CHIPS, split_axis=0, concat_axis=0, tiled=True
    ).reshape(FIX, D)
    parts = main_call(ids, main, twin)
    fix, code = lax.optimization_barrier((fix, parts[2]))
    fix_twin = lax.ppermute(fix, "core", swap)
    table = last_call(ids, flag, *parts[:2], code, main, fix, fix_twin)
    back = lax.all_to_all(table, PLANE, split_axis=0, concat_axis=0, tiled=True)
    out, flag = put_call(ids, back)
    _, out = lax.while_loop(
        lambda state: state[0] > 0,
        lambda state: (state[0] * 0, general_path(parts[3], ids, label_of_chip, core)),
        (flag[0], out.reshape(ROWS)),
    )
    return out


def solution(mesh):
    fine = Mesh(mesh.devices.reshape(4, 2, 2, 2, 4), ALL)
    return jax.shard_map(body, mesh=fine, in_specs=(P(ALL, None), P(ALL), P(ALL, None)), out_specs=P(ALL), check_vma=False)
```

```python
import functools

import jax
import jax.numpy as jnp
from jax import lax
from jax.experimental import pallas as pl
from jax.experimental.pallas import tpu as pltpu
from jax.sharding import Mesh, PartitionSpec as P

F32 = jnp.float32
BF = jnp.bfloat16
I32 = jnp.int32

D = 1024
ROWS = 768
CHIPS = 64
LABELS = 8
CAP = 15
SLOT = 16
MAIN = CHIPS * SLOT
FIX = LABELS * SLOT
ALL = ("x", "core", "yh", "yl", "z")
CHIP_AXES = ("x", "yh", "yl", "z")
GROUP_CHIPS = ("yl", "z")
PLANE = ("core", "yh", "yl", "z")
NEVER = 1.0e9
VMEM = 24 * 1024 * 1024


def iota(shape, dim):
    return lax.broadcasted_iota(I32, shape, dim)


def onehot(cond):
    return jnp.where(cond, 1.0, 0.0).astype(BF)


def mm(a, b):
    return lax.dot_general(a, b, (((1,), (0,)), ((), ())), preferred_element_type=F32)


def mm_t(a, b):
    return lax.dot_general(a, b, (((1,), (1,)), ((), ())), preferred_element_type=F32)


def earlier(hot):
    n, width = hot.shape
    parts = width // 128
    rows = jnp.concatenate([hot[:, i * 128:(i + 1) * 128] for i in range(parts)], axis=0)
    inside = mm(rows.astype(BF), onehot(iota((128, 128), 0) < iota((128, 128), 1)))
    total = jnp.broadcast_to(jnp.sum(rows, axis=1, keepdims=True), rows.shape).astype(BF)
    m = parts * n
    a, b = iota((m, m), 0), iota((m, m), 1)
    inside = inside + mm(onehot(((a & (n - 1)) == (b & (n - 1))) & (b < a)), total)
    return jnp.concatenate([inside[i * n:(i + 1) * n] for i in range(parts)], axis=1)


def pack_kernel(ids_ref, emb_hbm, lab_hbm, list_hbm, out_ref, emb_ref, lab_ref, list_ref, sems):
    copies = [
        pltpu.make_async_copy(src, dst, sems.at[i])
        for i, (src, dst) in enumerate(((list_hbm, list_ref), (lab_hbm, lab_ref), (emb_hbm, emb_ref)))
    ]
    for copy in copies:
        copy.start()
    rot = ids_ref[2]
    copies[0].wait()
    copies[1].wait()
    listed = onehot(iota((ROWS, ROWS), 0) == list_ref[...])
    pos = iota((16, ROWS), 1)
    group_of = lax.shift_right_logical(pos * 683, 16)
    sel = iota((16, ROWS), 0)
    vals = jnp.where(sel == 0, group_of, jnp.where(sel == 1, pos - group_of * 96, 0)).astype(F32).astype(BF)
    gd = mm_t(vals, listed)
    group = gd[0:1]
    dest = gd[1:2]
    label = lab_ref[...].reshape(1, ROWS).astype(F32)
    cluster = group * 8.0 + label
    member = iota((CHIPS, ROWS), 0).astype(F32) == cluster
    ranks = earlier(jnp.where(member, 1.0, 0.0))
    rank = jnp.sum(jnp.where(member, ranks, 0.0), axis=0, keepdims=True)
    count = jnp.broadcast_to(jnp.sum(jnp.where(member, 1.0, 0.0), axis=1, keepdims=True), (CHIPS, 128))
    over = jnp.maximum(count - CAP, 0.0).astype(BF)
    free = jnp.maximum(CAP - count, 0.0)
    c0, c1 = iota((CHIPS, CHIPS), 0), iota((CHIPS, CHIPS), 1)
    same = lax.shift_right_logical(c0, 3) == lax.shift_right_logical(c1, 3)
    over_pre = mm(onehot(same & (c1 < c0)), over)
    above = (CAP - 1 - (iota((CHIPS, 128), 1) & 15)).astype(F32)
    higher = jnp.clip(free, 0.0, jnp.maximum(above, 0.0)).astype(BF)
    level = onehot(free > above)
    free_pre = mm(onehot(same), higher) + mm(onehot(same & (((c1 - rot) & 7) < ((c0 - rot) & 7))), level)
    over_at = jnp.sum(jnp.where(member, over_pre[:, 0:1], 0.0), axis=0, keepdims=True) + rank - CAP
    row_code = jnp.where(rank < CAP, cluster * 16.0 + rank, 2048.0 + group * 128.0 + over_at)
    slot = iota((MAIN, 128), 0)
    at = (slot & 15).astype(F32)
    chip_hot = onehot(lax.shift_right_logical(iota((MAIN, CHIPS), 0), 4) == iota((MAIN, CHIPS), 1))
    slot_count = mm(chip_hot, count.astype(BF))
    slot_free = jnp.where(iota((MAIN, 128), 1) == (slot & 15), mm(chip_hot, free_pre.astype(BF)), 0.0)
    slot_free = jnp.sum(slot_free, axis=1, keepdims=True)
    spare = 2048.0 + (lax.shift_right_logical(slot, 7) * 128).astype(F32) + slot_free
    slot_code = jnp.where(at >= CAP, -1.0, jnp.where(at < slot_count, slot.astype(F32), spare))
    pick = jnp.concatenate([onehot(slot_code == row_code[:, b * 128:(b + 1) * 128]) for b in range(ROWS // 128)], axis=1)
    copies[2].wait()
    values = emb_ref[...].astype(F32)
    scale = lax.rsqrt(jnp.sum(values * values, axis=1, keepdims=True) + 1e-06)
    unit = (values * scale).astype(BF)
    lane = iota((128, ROWS), 0)
    tags = jnp.where(lane < 16, label + 1.0, jnp.where(lane < 32, dest, 0.0)).astype(BF)
    tag = jnp.where((iota((MAIN, 128), 1) & 15) == (slot & 15), mm_t(pick, tags), 0.0)
    tag = jnp.broadcast_to(jnp.sum(tag.reshape(CHIPS, SLOT, 128), axis=1, keepdims=True), (CHIPS, SLOT, 128)).reshape(MAIN, 128)
    for r in range(0, MAIN, 256):
        part = mm(pick[r:r + 256], unit)
        out_ref[r:r + 256, 0:128] = jnp.where(at[r:r + 256] >= CAP, tag[r:r + 256], part[:, 0:128]).astype(BF)
        out_ref[r:r + 256, 128:D] = part[:, 128:D].astype(BF)


def tag_rows(first, n):
    pick = onehot(iota((n, n * SLOT), 1) == iota((n, n * SLOT), 0) * SLOT + CAP)
    return mm(pick, first).astype(BF)


def tag_lanes(tags, n, k):
    spread = onehot(iota((128, n * SLOT), 0) == (iota((128, n * SLOT), 1) & 15) + 16 * k)
    wide = mm(tags, spread)
    own = iota((n, n * SLOT), 0) == lax.shift_right_logical(iota((n, n * SLOT), 1), 4)
    return jnp.sum(jnp.where(own, wide, 0.0), axis=0, keepdims=True)


def tag_columns(tags, n, ks):
    spread = onehot(lax.shift_right_logical(iota((n * SLOT, n), 0), 4) == iota((n * SLOT, n), 1))
    wide = mm(spread, tags)
    shape = (n * SLOT, 128)
    own = iota(shape, 0) & 15
    return [jnp.sum(jnp.where(iota(shape, 1) == own + 16 * k, wide, 0.0), axis=1, keepdims=True) for k in ks]


def source_of(chip, core):
    return lax.shift_right_logical(chip, 4) * 32 + core * 16 + (chip & 15)


def main_order(shape, dim, core):
    slot = iota(shape, dim)
    return (source_of(lax.shift_right_logical(slot, 4), core) * 256 + (slot & 15)).astype(F32)


def away_order(source, turn, at):
    return (source * 256 + 16 + (CAP - 1 - at) * 8 + turn).astype(F32)


def fix_order(shape, dim, core, chip, at):
    holder = lax.shift_right_logical(iota(shape, dim), 4)
    chip = chip.astype(I32)
    return away_order(source_of(chip, core), (holder - chip) & 7, at.astype(I32))


def fix_kernel(ids_ref, main_ref, out_ref, flag_ref, tags_ref, lanes_ref):
    own = ids_ref[1].astype(F32)
    tags = tag_rows(main_ref[:, 0:128], CHIPS)
    label = tag_lanes(tags, CHIPS, 0)
    dest = tag_lanes(tags, CHIPS, 1)
    tags_ref[...] = tags
    lanes_ref[...] = jnp.concatenate([label, dest, jnp.zeros((6, MAIN), F32)], axis=0)
    moved = (label > 0.5) & (label != own + 1.0)
    member = moved & (iota((LABELS, MAIN), 0).astype(F32) == label - 1.0)
    ranks = earlier(jnp.where(member, 1.0, 0.0))
    rank = jnp.sum(jnp.where(member, ranks, 0.0), axis=0, keepdims=True)
    code = jnp.where(moved & (rank < CAP), (label - 1.0) * 16.0 + rank, -1.0)
    pick = onehot(iota((FIX, MAIN), 0).astype(F32) == code)
    slot = iota((1, MAIN), 1)
    lane = iota((128, MAIN), 0)
    kind = lax.shift_right_logical(lane, 4)
    vals = jnp.where(kind == 0, 1.0, jnp.where(kind == 1, lax.shift_right_logical(slot, 4).astype(F32), jnp.where(kind == 2, (slot & 15).astype(F32), jnp.where(kind == 3, dest, 0.0)))).astype(BF)
    fixed = (FIX, 128)
    tag = jnp.where((iota(fixed, 1) & 15) == (iota(fixed, 0) & 15), mm_t(pick, vals), 0.0)
    tag = jnp.broadcast_to(jnp.sum(tag.reshape(LABELS, SLOT, 128), axis=1, keepdims=True), (LABELS, SLOT, 128)).reshape(fixed)
    for b in range(0, D, 256):
        part = mm(pick, main_ref[:, b:b + 256])
        if b == 0:
            out_ref[:, 0:128] = jnp.where((iota(fixed, 0) & 15) == CAP, tag, part[:, 0:128]).astype(BF)
            out_ref[:, 128:256] = part[:, 128:256].astype(BF)
        else:
            out_ref[:, b:b + 256] = part.astype(BF)
    worst = jnp.max(jnp.where(moved, rank, 0.0), axis=1, keepdims=True)
    flag_ref[...] = jnp.broadcast_to(jnp.where(worst >= CAP, 1.0, 0.0), (8, 128))


def lanes_to_rows(row):
    return jnp.concatenate([row[:, i * 128:(i + 1) * 128] for i in range(row.shape[1] // 128)], axis=0)


def best(keys, q_rows, q_order):
    found = jnp.full((1, q_rows.shape[0]), -1.0, F32)
    for rows, order in keys:
        scores = jnp.where(order[:, 0:1] < q_order, mm_t(rows[...], q_rows), -1.0)
        found = jnp.maximum(found, jnp.max(scores, axis=0, keepdims=True))
    return found


def main_kernel(ids_ref, tags_ref, lanes_ref, own_ref, twin_ref, rows_ref, own_key_ref, code_ref):
    core = ids_ref[0]
    mine = ids_ref[1].astype(F32) + 1.0
    twin_tags = tag_rows(twin_ref[:, 0:128], CHIPS)

    def main_key(t, c):
        (label,) = tag_columns(t, CHIPS, (0,))
        return jnp.broadcast_to(jnp.where(label == mine, main_order((MAIN, 1), 0, c), NEVER), (MAIN, 128))

    own_key_ref[...] = main_key(tags_ref[...], core)
    twin_key = main_key(twin_tags, 1 - core)
    valid = lanes_ref[0:1, :] == mine
    query = jnp.where(valid, main_order((1, MAIN), 1, core), -1.0)
    dest = lanes_ref[1:2, :].astype(I32)
    home = lax.shift_right_logical(dest * 43, 8)
    member = valid & (iota((16, MAIN), 0) == home)
    ranks = earlier(jnp.where(member, 1.0, 0.0))
    rank = jnp.sum(jnp.where(member, ranks, 0.0), axis=0, keepdims=True)
    rank = jnp.where(valid, rank, -1.0)
    hot = onehot(iota((128, MAIN), 0).astype(F32) == rank)
    source = source_of(lax.shift_right_logical(iota((1, MAIN), 1), 4), core)
    at = source * 6 + dest - home * 6 + 1
    high = lax.shift_right_logical(at, 4)
    parts = [jnp.where(member, part.astype(F32), 0.0).astype(BF) for part in (high, at - high * 16)]
    code_ref[...] = mm_t(parts[0], hot) * 16.0 + mm_t(parts[1], hot) - 1.0
    worst = jnp.max(rank, axis=1, keepdims=True)
    found = [
        best(
            ((own_ref[0:q + 256, :], own_key_ref[0:q + 256, :]), (twin_ref[0:q + 256, :], twin_key[0:q + 256, :])),
            own_ref[q:q + 256, :],
            query[:, q:q + 256],
        )
        for q in range(0, MAIN, 256)
    ]
    found = jnp.concatenate(found, axis=1)
    worst = jnp.broadcast_to(worst, (1, MAIN))
    rows = jnp.concatenate([query, found, home.astype(F32), worst, rank, jnp.zeros((3, MAIN), F32)], axis=0)
    rows_ref[...] = rows


def last_kernel(ids_ref, flag_ref, rows_ref, own_key_ref, code_ref, own_ref, fix_ref, fix_twin_ref, out_ref):
    core = ids_ref[0]
    fix_rows = jnp.concatenate([fix_ref[...], fix_twin_ref[...]], axis=0)
    orders, queries, codes = [], [], []
    for ref, c in ((fix_ref, core), (fix_twin_ref, 1 - core)):
        tags = tag_rows(ref[:, 0:128], LABELS)
        valid, chip, at = tag_columns(tags, LABELS, (0, 1, 2))
        orders.append(jnp.where(valid > 0.5, fix_order((FIX, 1), 0, c, chip, at), NEVER))
        valid = tag_lanes(tags, LABELS, 0) > 0.5
        chip = tag_lanes(tags, LABELS, 1)
        queries.append(jnp.where(valid, fix_order((1, FIX), 1, c, chip, tag_lanes(tags, LABELS, 2)), -1.0))
        source = source_of(chip.astype(I32), c).astype(F32)
        codes.append(jnp.where(valid, source * 128.0 + tag_lanes(tags, LABELS, 3), -1.0))
    fix_keys = ((fix_rows, jnp.concatenate(orders, axis=0)),)
    fix_found = best(((own_ref, own_key_ref),) + fix_keys, fix_rows, jnp.concatenate(queries, axis=1))
    found = jnp.maximum(best(fix_keys, own_ref[...], rows_ref[0:1, :]), rows_ref[1:2, :])
    here = iota((16, MAIN), 0).astype(F32) == rows_ref[2:3, :]
    value = jnp.concatenate([jnp.where(here, part.astype(F32), 0.0).astype(BF) for part in split3(found)], axis=0)
    value = mm_t(value, onehot(iota((128, MAIN), 0).astype(F32) == rows_ref[4:5, :]))
    value = value[0:16] + value[16:32] + value[32:48]
    flag = jnp.maximum(flag_ref[0:1, :], jnp.where(rows_ref[3:4, 0:128] >= 128.0, 1.0, 0.0))
    common = jnp.concatenate([lanes_to_rows(fix_found)] + codes + [flag, jnp.zeros((1, 128), F32)], axis=0)
    for m in range(16):
        table = jnp.concatenate([value[m:m + 1], code_ref[m:m + 1], common], axis=0)
        out_ref[m] = table
        out_ref[16 + m] = table


def split3(v):
    a = v.astype(BF)
    r = v - a.astype(F32)
    b = r.astype(BF)
    return a, b, (r - b.astype(F32)).astype(BF)


def place_kernel(ids_ref, in_ref, out_ref):
    core = ids_ref[0]
    base = (ids_ref[3] * 6).astype(F32)
    wide = (128, 128)
    outs = []
    spread = [onehot(iota(wide, 1) == lax.shift_right_logical(iota(wide, 0), 4) * 6 + q) for q in range(6)]
    fix_val, fix_code = [], []
    for c in range(2):
        acc = [jnp.zeros((8, 128), F32) for _ in range(6)]
        for k in range(LABELS):
            dev = c * 16 + core * 8 + k
            val = in_ref[dev, 0:8, :]
            code = in_ref[dev, 8:16, :]
            for q in range(6):
                acc[q] = acc[q] + jnp.where(code == base + q, val, 0.0)
            fix_val.append(in_ref[dev, 16:17, :])
            fix_code.append(in_ref[dev, 17:18, :])
        total = jnp.zeros((8, 128), F32)
        for q in range(6):
            for part in split3(acc[q]):
                total = total + mm(part, spread[q])
        outs.append(total)
    main = jnp.concatenate([outs[c][2 * x:2 * x + 2] for x in range(4) for c in range(2)], axis=0)
    val = jnp.concatenate(fix_val, axis=1)
    code = jnp.concatenate(fix_code, axis=1).astype(I32)
    source = lax.shift_right_arithmetic(code, 7)
    q = (code & 127).astype(F32) - base
    ok = (code >= 0) & (q >= 0.0) & (q < 6.0)
    n = val.shape[1]
    left = jnp.where(ok & (iota((16, n), 0) == lax.shift_right_arithmetic(source, 3)), val, 0.0)
    right = onehot(iota((128, n), 0).astype(F32) == (source & 7).astype(F32) * 6.0 + q)
    for part in split3(left):
        main = main + mm_t(part, right)
    out_ref[...] = jnp.maximum(main, -1.0)


def put_kernel(ids_ref, in_ref, out_ref, flag_ref):
    core = ids_ref[0]
    base = ids_ref[3] * 6
    outs = []
    for c in range(2):
        val, at = [], []
        for k in range(LABELS):
            block = in_ref[c * 16 + core * 8 + k]
            val += [block[0:1], block[2:3], block[3:4]]
            code = block[4:6].astype(I32)
            q = (code & 127) - base
            ok = (code >= 0) & (q >= 0) & (q < 6)
            fix_at = jnp.where(ok, lax.shift_right_arithmetic(code, 7) * 6 + q, -1)
            at += [block[1:2].astype(I32), fix_at[0:1], fix_at[1:2]]
        val = jnp.concatenate(val, axis=1) + 2.0
        at = jnp.concatenate(at, axis=1)
        n = val.shape[1]
        left = jnp.where(iota((8, n), 0) == lax.shift_right_arithmetic(at, 7), val, 0.0)
        out = mm_t(jnp.concatenate(split3(left), axis=0), onehot(iota((128, n), 0) == (at & 127)))
        outs.append(out[0:8] + out[8:16] + out[16:24])
    out_ref[...] = jnp.maximum(jnp.maximum(outs[0], outs[1]) - 2.0, -1.0)[0:6]
    flag_ref[0] = jnp.max(jnp.max(in_ref[...], axis=0)[6:7]).astype(I32)


def call(kernel, shapes, args, flops, memory=pltpu.VMEM, scratch=(), vmem=VMEM, out_memory=pltpu.VMEM, out_specs=None):
    specs = [pl.BlockSpec(memory_space=pltpu.SMEM)] + [pl.BlockSpec(memory_space=memory)] * (len(args) - 1)
    return pl.pallas_call(
        kernel,
        out_shape=shapes,
        in_specs=specs,
        out_specs=out_specs or jax.tree.map(lambda _: pl.BlockSpec(memory_space=out_memory), shapes),
        scratch_shapes=scratch,
        compiler_params=pltpu.CompilerParams(vmem_limit_bytes=vmem),
        cost_estimate=pl.CostEstimate(flops=flops, bytes_accessed=4 << 20, transcendentals=0),
    )(*args)


def struct(shape, dtype):
    return jax.ShapeDtypeStruct(shape, dtype)


def place(table, ids):
    back = lax.all_to_all(table, PLANE, split_axis=0, concat_axis=0, tiled=True)
    out = call(place_kernel, struct((16, 128), F32), (ids, back), 1 << 27)
    return out[:, :48].reshape(ROWS)


def general_path(main, ids, label_of_chip, core):
    tags = main[CAP::SLOT, :32].astype(F32)
    label = tags[:, 0:16].reshape(MAIN)
    dest = tags[:, 16:32].reshape(MAIN)
    slot = jnp.arange(MAIN, dtype=I32)
    chip = slot // 16
    home = main_order((MAIN,), 0, core)
    away = away_order(source_of(chip, core), (label_of_chip - chip) & 7, slot & 15)
    order = jnp.where(label == (label_of_chip + 1).astype(F32), home, away)
    key_order = jnp.where(label > 0.5, order, NEVER)
    axes = ("core", "yl", "z")
    ring = [(i, (i + 1) % 16) for i in range(16)]

    def step(_, state):
        found, rows, tag = state
        scores = mm_t(main, rows)
        ok = (tag[0:1] == label[:, None]) & (tag[1:2] < order[:, None])
        found = jnp.maximum(found, jnp.max(jnp.where(ok, scores, -1.0), axis=1))
        return found, lax.ppermute(rows, axes, ring), lax.ppermute(tag, axes, ring)

    tag = jnp.stack([label, key_order])
    found, _, _ = lax.fori_loop(0, 16, step, (jnp.full((MAIN,), -1.0, F32), main, tag))
    code = jnp.where(label > 0.5, dest, -1.0)
    none = jnp.full((8, 128), -1.0, F32)
    table = jnp.concatenate([found.reshape(8, 128), code.reshape(8, 128), none], axis=0)
    return place(jnp.broadcast_to(table, (32, 24, 128)), ids)


def pack_call(ids, *arrays):
    arrays = [pltpu.with_memory_space_constraint(array, pltpu.HBM) for array in arrays]
    return call(
        pack_kernel,
        struct((MAIN, D), BF),
        (ids, *arrays),
        3 << 30,
        pl.ANY,
        (
            pltpu.VMEM((ROWS, D), BF),
            pltpu.VMEM((ROWS,), I32),
            pltpu.VMEM((1, ROWS), I32),
            pltpu.SemaphoreType.DMA((3,)),
        ),
    )


def fix_call(ids, main):
    shapes = (struct((FIX, D), BF), struct((8, 128), F32), struct((CHIPS, 128), BF), struct((8, MAIN), F32))
    return call(fix_kernel, shapes, (ids, main), 1 << 30)


def main_call(*args):
    wide = struct((MAIN, 128), F32)
    shapes = (struct((8, MAIN), F32), wide, struct((16, 128), F32))
    return call(main_kernel, shapes, args, 3 << 30)


def last_call(*args):
    return call(last_kernel, struct((32, 8, 128), F32), args, 1 << 30)


def put_call(ids, back):
    specs = (pl.BlockSpec(memory_space=pltpu.VMEM), pl.BlockSpec(memory_space=pltpu.SMEM))
    return call(put_kernel, (struct((6, 128), F32), struct((1,), I32)), (ids, back), 1 << 27, out_specs=specs)


def body(embeddings, labels, send_list):
    core = lax.axis_index("core").astype(I32)
    member = lax.axis_index(("yh", "yl", "z")).astype(I32)
    label_of_chip = member & 7
    ids = jnp.stack([core, label_of_chip, label_of_chip, member])
    packed = pack_call(ids, embeddings, labels, send_list)
    main = lax.all_to_all(
        packed.reshape(CHIPS, SLOT, D), CHIP_AXES, split_axis=0, concat_axis=0, tiled=True
    ).reshape(MAIN, D)
    swap = [(0, 1), (1, 0)]
    twin = lax.ppermute(main, "core", swap)
    fix, flag, tags, lanes = fix_call(ids, main)
    fix = lax.all_to_all(
        fix.reshape(LABELS, SLOT, D), GROUP_CHIPS, split_axis=0, concat_axis=0, tiled=True
    ).reshape(FIX, D)
    parts = main_call(ids, tags, lanes, main, twin)
    fix, code = lax.optimization_barrier((fix, parts[2]))
    fix_twin = lax.ppermute(fix, "core", swap)
    table = last_call(ids, flag, *parts[:2], code, main, fix, fix_twin)
    back = lax.all_to_all(table, PLANE, split_axis=0, concat_axis=0, tiled=True)
    out, flag = put_call(ids, back)
    _, out = lax.while_loop(
        lambda state: state[0] > 0,
        lambda state: (state[0] * 0, general_path(lax.ppermute(twin, "core", swap), ids, label_of_chip, core)),
        (flag[0], out.reshape(ROWS)),
    )
    return out


def solution(mesh):
    fine = Mesh(mesh.devices.reshape(4, 2, 2, 2, 4), ALL)
    return jax.shard_map(body, mesh=fine, in_specs=(P(ALL, None), P(ALL), P(ALL, None)), out_specs=P(ALL), check_vma=False)
```

```python
import functools

import jax
import jax.numpy as jnp
from jax import lax
from jax.experimental import pallas as pl
from jax.experimental.pallas import tpu as pltpu
from jax.sharding import Mesh, PartitionSpec as P

F32 = jnp.float32
BF = jnp.bfloat16
I32 = jnp.int32

D = 1024
ROWS = 768
CHIPS = 64
LABELS = 8
CAP = 15
SLOT = 16
MAIN = CHIPS * SLOT
FIX = LABELS * SLOT
ALL = ("x", "core", "yh", "yl", "z")
CHIP_AXES = ("x", "yh", "yl", "z")
GROUP_CHIPS = ("yl", "z")
PLANE = ("core", "yh", "yl", "z")
NEVER = 1.0e9
VMEM = 24 * 1024 * 1024


def iota(shape, dim):
    return lax.broadcasted_iota(I32, shape, dim)


def onehot(cond):
    return jnp.where(cond, 1.0, 0.0).astype(BF)


def mm(a, b):
    return lax.dot_general(a, b, (((1,), (0,)), ((), ())), preferred_element_type=F32)


def mm_t(a, b):
    return lax.dot_general(a, b, (((1,), (1,)), ((), ())), preferred_element_type=F32)


def earlier(hot):
    n, width = hot.shape
    parts = width // 128
    rows = jnp.concatenate([hot[:, i * 128:(i + 1) * 128] for i in range(parts)], axis=0)
    inside = mm(rows.astype(BF), onehot(iota((128, 128), 0) < iota((128, 128), 1)))
    total = jnp.broadcast_to(jnp.sum(rows, axis=1, keepdims=True), rows.shape).astype(BF)
    m = parts * n
    a, b = iota((m, m), 0), iota((m, m), 1)
    inside = inside + mm(onehot(((a & (n - 1)) == (b & (n - 1))) & (b < a)), total)
    return jnp.concatenate([inside[i * n:(i + 1) * n] for i in range(parts)], axis=1)


def pack_kernel(ids_ref, emb_hbm, lab_hbm, list_hbm, out_ref, emb_ref, lab_ref, list_ref, sems):
    copies = [
        pltpu.make_async_copy(src, dst, sems.at[i])
        for i, (src, dst) in enumerate(((list_hbm, list_ref), (lab_hbm, lab_ref), (emb_hbm, emb_ref)))
    ]
    for copy in copies:
        copy.start()
    rot = ids_ref[2]
    copies[0].wait()
    copies[1].wait()
    listed = onehot(iota((ROWS, ROWS), 0) == list_ref[...])
    pos = iota((16, ROWS), 1)
    group_of = lax.shift_right_logical(pos * 683, 16)
    sel = iota((16, ROWS), 0)
    vals = jnp.where(sel == 0, group_of, jnp.where(sel == 1, pos - group_of * 96, 0)).astype(F32).astype(BF)
    gd = mm_t(vals, listed)
    group = gd[0:1]
    dest = gd[1:2]
    label = lab_ref[...].reshape(1, ROWS).astype(F32)
    cluster = group * 8.0 + label
    member = iota((CHIPS, ROWS), 0).astype(F32) == cluster
    ranks = earlier(jnp.where(member, 1.0, 0.0))
    rank = jnp.sum(jnp.where(member, ranks, 0.0), axis=0, keepdims=True)
    count = jnp.broadcast_to(jnp.sum(jnp.where(member, 1.0, 0.0), axis=1, keepdims=True), (CHIPS, 128))
    over = jnp.maximum(count - CAP, 0.0).astype(BF)
    free = jnp.maximum(CAP - count, 0.0)
    c0, c1 = iota((CHIPS, CHIPS), 0), iota((CHIPS, CHIPS), 1)
    same = lax.shift_right_logical(c0, 3) == lax.shift_right_logical(c1, 3)
    over_pre = mm(onehot(same & (c1 < c0)), over)
    above = (CAP - 1 - (iota((CHIPS, 128), 1) & 15)).astype(F32)
    higher = jnp.clip(free, 0.0, jnp.maximum(above, 0.0)).astype(BF)
    level = onehot(free > above)
    free_pre = mm(onehot(same), higher) + mm(onehot(same & (((c1 - rot) & 7) < ((c0 - rot) & 7))), level)
    over_at = jnp.sum(jnp.where(member, over_pre[:, 0:1], 0.0), axis=0, keepdims=True) + rank - CAP
    row_code = jnp.where(rank < CAP, cluster * 16.0 + rank, 2048.0 + group * 128.0 + over_at)
    slot = iota((MAIN, 128), 0)
    at = (slot & 15).astype(F32)
    chip_hot = onehot(lax.shift_right_logical(iota((MAIN, CHIPS), 0), 4) == iota((MAIN, CHIPS), 1))
    slot_count = mm(chip_hot, count.astype(BF))
    slot_free = jnp.where(iota((MAIN, 128), 1) == (slot & 15), mm(chip_hot, free_pre.astype(BF)), 0.0)
    slot_free = jnp.sum(slot_free, axis=1, keepdims=True)
    spare = 2048.0 + (lax.shift_right_logical(slot, 7) * 128).astype(F32) + slot_free
    slot_code = jnp.where(at >= CAP, -1.0, jnp.where(at < slot_count, slot.astype(F32), spare))
    pick = jnp.concatenate([onehot(slot_code == row_code[:, b * 128:(b + 1) * 128]) for b in range(ROWS // 128)], axis=1)
    copies[2].wait()
    values = emb_ref[...].astype(F32)
    scale = lax.rsqrt(jnp.sum(values * values, axis=1, keepdims=True) + 1e-06)
    unit = (values * scale).astype(BF)
    lane = iota((128, ROWS), 0)
    tags = jnp.where(lane < 16, label + 1.0, jnp.where(lane < 32, dest, 0.0)).astype(BF)
    tag = jnp.where((iota((MAIN, 128), 1) & 15) == (slot & 15), mm_t(pick, tags), 0.0)
    tag = jnp.broadcast_to(jnp.sum(tag.reshape(CHIPS, SLOT, 128), axis=1, keepdims=True), (CHIPS, SLOT, 128)).reshape(MAIN, 128)
    for r in range(0, MAIN, 256):
        part = mm(pick[r:r + 256], unit)
        out_ref[r:r + 256, 0:128] = jnp.where(at[r:r + 256] >= CAP, tag[r:r + 256], part[:, 0:128]).astype(BF)
        out_ref[r:r + 256, 128:D] = part[:, 128:D].astype(BF)


def tag_rows(first, n):
    pick = onehot(iota((n, n * SLOT), 1) == iota((n, n * SLOT), 0) * SLOT + CAP)
    return mm(pick, first).astype(BF)


def tag_lanes(tags, n, k):
    spread = onehot(iota((128, n * SLOT), 0) == (iota((128, n * SLOT), 1) & 15) + 16 * k)
    wide = mm(tags, spread)
    own = iota((n, n * SLOT), 0) == lax.shift_right_logical(iota((n, n * SLOT), 1), 4)
    return jnp.sum(jnp.where(own, wide, 0.0), axis=0, keepdims=True)


def tag_columns(tags, n, ks):
    spread = onehot(lax.shift_right_logical(iota((n * SLOT, n), 0), 4) == iota((n * SLOT, n), 1))
    wide = mm(spread, tags)
    shape = (n * SLOT, 128)
    own = iota(shape, 0) & 15
    return [jnp.sum(jnp.where(iota(shape, 1) == own + 16 * k, wide, 0.0), axis=1, keepdims=True) for k in ks]


def source_of(chip, core):
    return lax.shift_right_logical(chip, 4) * 32 + core * 16 + (chip & 15)


def main_order(shape, dim, core):
    slot = iota(shape, dim)
    return (source_of(lax.shift_right_logical(slot, 4), core) * 256 + (slot & 15)).astype(F32)


def away_order(source, turn, at):
    return (source * 256 + 16 + (CAP - 1 - at) * 8 + turn).astype(F32)


def fix_order(shape, dim, core, chip, at):
    holder = lax.shift_right_logical(iota(shape, dim), 4)
    chip = chip.astype(I32)
    return away_order(source_of(chip, core), (holder - chip) & 7, at.astype(I32))


def fix_kernel(ids_ref, main_ref, out_ref, flag_ref, tags_ref, lanes_ref):
    own = ids_ref[1].astype(F32)
    tags = tag_rows(main_ref[:, 0:128], CHIPS)
    label = tag_lanes(tags, CHIPS, 0)
    dest = tag_lanes(tags, CHIPS, 1)
    tags_ref[...] = tags
    lanes_ref[...] = jnp.concatenate([label, dest, jnp.zeros((6, MAIN), F32)], axis=0)
    moved = (label > 0.5) & (label != own + 1.0)
    member = moved & (iota((LABELS, MAIN), 0).astype(F32) == label - 1.0)
    ranks = earlier(jnp.where(member, 1.0, 0.0))
    rank = jnp.sum(jnp.where(member, ranks, 0.0), axis=0, keepdims=True)
    code = jnp.where(moved & (rank < CAP), (label - 1.0) * 16.0 + rank, -1.0)
    pick = onehot(iota((FIX, MAIN), 0).astype(F32) == code)
    slot = iota((1, MAIN), 1)
    lane = iota((128, MAIN), 0)
    kind = lax.shift_right_logical(lane, 4)
    vals = jnp.where(kind == 0, 1.0, jnp.where(kind == 1, lax.shift_right_logical(slot, 4).astype(F32), jnp.where(kind == 2, (slot & 15).astype(F32), jnp.where(kind == 3, dest, 0.0)))).astype(BF)
    fixed = (FIX, 128)
    tag = jnp.where((iota(fixed, 1) & 15) == (iota(fixed, 0) & 15), mm_t(pick, vals), 0.0)
    tag = jnp.broadcast_to(jnp.sum(tag.reshape(LABELS, SLOT, 128), axis=1, keepdims=True), (LABELS, SLOT, 128)).reshape(fixed)
    for b in range(0, D, 256):
        part = mm(pick, main_ref[:, b:b + 256])
        if b == 0:
            out_ref[:, 0:128] = jnp.where((iota(fixed, 0) & 15) == CAP, tag, part[:, 0:128]).astype(BF)
            out_ref[:, 128:256] = part[:, 128:256].astype(BF)
        else:
            out_ref[:, b:b + 256] = part.astype(BF)
    worst = jnp.max(jnp.where(moved, rank, 0.0), axis=1, keepdims=True)
    flag_ref[...] = jnp.broadcast_to(jnp.where(worst >= CAP, 1.0, 0.0), (8, 128))


def lanes_to_rows(row):
    return jnp.concatenate([row[:, i * 128:(i + 1) * 128] for i in range(row.shape[1] // 128)], axis=0)


def best(keys, q_rows, q_order):
    found = jnp.full((1, q_rows.shape[0]), -1.0, F32)
    for rows, order in keys:
        scores = jnp.where(order[:, 0:1] < q_order, mm_t(rows[...], q_rows), -1.0)
        found = jnp.maximum(found, jnp.max(scores, axis=0, keepdims=True))
    return found


def main_kernel(ids_ref, tags_ref, lanes_ref, own_ref, twin_ref, rows_ref, own_key_ref, code_ref):
    core = ids_ref[0]
    mine = ids_ref[1].astype(F32) + 1.0
    twin_tags = tag_rows(twin_ref[:, 0:128], CHIPS)

    def main_key(t, c):
        (label,) = tag_columns(t, CHIPS, (0,))
        return jnp.broadcast_to(jnp.where(label == mine, main_order((MAIN, 1), 0, c), NEVER), (MAIN, 128))

    own_key_ref[...] = main_key(tags_ref[...], core)
    twin_key = main_key(twin_tags, 1 - core)
    valid = lanes_ref[0:1, :] == mine
    query = jnp.where(valid, main_order((1, MAIN), 1, core), -1.0)
    dest = lanes_ref[1:2, :].astype(I32)
    home = lax.shift_right_logical(dest * 43, 8)
    member = valid & (iota((16, MAIN), 0) == home)
    ranks = earlier(jnp.where(member, 1.0, 0.0))
    rank = jnp.sum(jnp.where(member, ranks, 0.0), axis=0, keepdims=True)
    rank = jnp.where(valid, rank, -1.0)
    hot = onehot(iota((128, MAIN), 0).astype(F32) == rank)
    source = source_of(lax.shift_right_logical(iota((1, MAIN), 1), 4), core)
    at = source * 6 + dest - home * 6 + 1
    high = lax.shift_right_logical(at, 4)
    parts = [jnp.where(member, part.astype(F32), 0.0).astype(BF) for part in (high, at - high * 16)]
    code_ref[...] = mm_t(parts[0], hot) * 16.0 + mm_t(parts[1], hot) - 1.0
    worst = jnp.max(rank, axis=1, keepdims=True)
    found = [
        best(
            ((own_ref[0:q + 256, :], own_key_ref[0:q + 256, :]), (twin_ref[0:q + 256, :], twin_key[0:q + 256, :])),
            own_ref[q:q + 256, :],
            query[:, q:q + 256],
        )
        for q in range(0, MAIN, 256)
    ]
    found = jnp.concatenate(found, axis=1)
    worst = jnp.broadcast_to(worst, (1, MAIN))
    rows = jnp.concatenate([query, found, home.astype(F32), worst, rank, jnp.zeros((3, MAIN), F32)], axis=0)
    rows_ref[...] = rows


def last_kernel(ids_ref, flag_ref, rows_ref, own_key_ref, code_ref, own_ref, fix_ref, fix_twin_ref, out_ref):
    core = ids_ref[0]
    fix_rows = jnp.concatenate([fix_ref[...], fix_twin_ref[...]], axis=0)
    tags = tag_rows(fix_rows[:, 0:128], 2 * LABELS)

    def side(shape, dim):
        return core ^ lax.shift_right_logical(iota(shape, dim), 7)

    tall, wide = (2 * FIX, 1), (1, 2 * FIX)
    valid, chip, at = tag_columns(tags, 2 * LABELS, (0, 1, 2))
    fix_keys = ((fix_rows, jnp.where(valid > 0.5, fix_order(tall, 0, side(tall, 0), chip, at), NEVER)),)
    valid, chip, at, dest = (tag_lanes(tags, 2 * LABELS, k) for k in range(4))
    source = source_of(chip.astype(I32), side(wide, 1)).astype(F32)
    fix_query = jnp.where(valid > 0.5, fix_order(wide, 1, side(wide, 1), chip, at), -1.0)
    fix_code = jnp.where(valid > 0.5, source * 128.0 + dest, -1.0)
    fix_found = best(((own_ref, own_key_ref),) + fix_keys, fix_rows, fix_query)
    found = jnp.maximum(best(fix_keys, own_ref[...], rows_ref[0:1, :]), rows_ref[1:2, :])
    here = iota((16, MAIN), 0).astype(F32) == rows_ref[2:3, :]
    value = jnp.concatenate([jnp.where(here, part.astype(F32), 0.0).astype(BF) for part in split3(found)], axis=0)
    value = mm_t(value, onehot(iota((128, MAIN), 0).astype(F32) == rows_ref[4:5, :]))
    value = value[0:16] + value[16:32] + value[32:48]
    flag = jnp.maximum(flag_ref[0:1, :], jnp.where(rows_ref[3:4, 0:128] >= 128.0, 1.0, 0.0))
    common = [lanes_to_rows(fix_found), lanes_to_rows(fix_code), flag, jnp.zeros((1, 128), F32)]
    common = jnp.concatenate(common, axis=0)
    shape = (16, 8, 128)
    row = iota(shape, 1)
    table = jnp.broadcast_to(jnp.concatenate([jnp.zeros((2, 128), F32), common], axis=0)[None], shape)
    table = jnp.where(row == 0, value[:, None, :], jnp.where(row == 1, code_ref[...][:, None, :], table))
    out_ref[0:16] = table
    out_ref[16:32] = table


def split3(v):
    a = v.astype(BF)
    r = v - a.astype(F32)
    b = r.astype(BF)
    return a, b, (r - b.astype(F32)).astype(BF)


def place_kernel(ids_ref, in_ref, out_ref):
    core = ids_ref[0]
    base = (ids_ref[3] * 6).astype(F32)
    wide = (128, 128)
    outs = []
    spread = [onehot(iota(wide, 1) == lax.shift_right_logical(iota(wide, 0), 4) * 6 + q) for q in range(6)]
    fix_val, fix_code = [], []
    for c in range(2):
        acc = [jnp.zeros((8, 128), F32) for _ in range(6)]
        for k in range(LABELS):
            dev = c * 16 + core * 8 + k
            val = in_ref[dev, 0:8, :]
            code = in_ref[dev, 8:16, :]
            for q in range(6):
                acc[q] = acc[q] + jnp.where(code == base + q, val, 0.0)
            fix_val.append(in_ref[dev, 16:17, :])
            fix_code.append(in_ref[dev, 17:18, :])
        total = jnp.zeros((8, 128), F32)
        for q in range(6):
            for part in split3(acc[q]):
                total = total + mm(part, spread[q])
        outs.append(total)
    main = jnp.concatenate([outs[c][2 * x:2 * x + 2] for x in range(4) for c in range(2)], axis=0)
    val = jnp.concatenate(fix_val, axis=1)
    code = jnp.concatenate(fix_code, axis=1).astype(I32)
    source = lax.shift_right_arithmetic(code, 7)
    q = (code & 127).astype(F32) - base
    ok = (code >= 0) & (q >= 0.0) & (q < 6.0)
    n = val.shape[1]
    left = jnp.where(ok & (iota((16, n), 0) == lax.shift_right_arithmetic(source, 3)), val, 0.0)
    right = onehot(iota((128, n), 0).astype(F32) == (source & 7).astype(F32) * 6.0 + q)
    for part in split3(left):
        main = main + mm_t(part, right)
    out_ref[...] = jnp.maximum(main, -1.0)


def put_kernel(ids_ref, in_ref, out_ref, flag_ref):
    core = ids_ref[0]
    base = ids_ref[3] * 6
    outs = []
    for c in range(2):
        val, at = [], []
        for k in range(LABELS):
            block = in_ref[c * 16 + core * 8 + k]
            val += [block[0:1], block[2:3], block[3:4]]
            code = block[4:6].astype(I32)
            q = (code & 127) - base
            ok = (code >= 0) & (q >= 0) & (q < 6)
            fix_at = jnp.where(ok, lax.shift_right_arithmetic(code, 7) * 6 + q, -1)
            at += [block[1:2].astype(I32), fix_at[0:1], fix_at[1:2]]
        val = jnp.concatenate(val, axis=1) + 2.0
        at = jnp.concatenate(at, axis=1)
        n = val.shape[1]
        left = jnp.where(iota((8, n), 0) == lax.shift_right_arithmetic(at, 7), val, 0.0)
        out = mm_t(jnp.concatenate(split3(left), axis=0), onehot(iota((128, n), 0) == (at & 127)))
        outs.append(out[0:8] + out[8:16] + out[16:24])
    out_ref[...] = jnp.maximum(jnp.maximum(outs[0], outs[1]) - 2.0, -1.0)[0:6]
    flag_ref[0] = jnp.max(jnp.max(in_ref[...], axis=0)[6:7]).astype(I32)


def call(kernel, shapes, args, flops, memory=pltpu.VMEM, scratch=(), vmem=VMEM, out_memory=pltpu.VMEM, out_specs=None):
    specs = [pl.BlockSpec(memory_space=pltpu.SMEM)] + [pl.BlockSpec(memory_space=memory)] * (len(args) - 1)
    return pl.pallas_call(
        kernel,
        out_shape=shapes,
        in_specs=specs,
        out_specs=out_specs or jax.tree.map(lambda _: pl.BlockSpec(memory_space=out_memory), shapes),
        scratch_shapes=scratch,
        compiler_params=pltpu.CompilerParams(vmem_limit_bytes=vmem),
        cost_estimate=pl.CostEstimate(flops=flops, bytes_accessed=4 << 20, transcendentals=0),
    )(*args)


def struct(shape, dtype):
    return jax.ShapeDtypeStruct(shape, dtype)


def place(table, ids):
    back = lax.all_to_all(table, PLANE, split_axis=0, concat_axis=0, tiled=True)
    out = call(place_kernel, struct((16, 128), F32), (ids, back), 1 << 27)
    return out[:, :48].reshape(ROWS)


def general_path(main, ids, label_of_chip, core):
    tags = main[CAP::SLOT, :32].astype(F32)
    label = tags[:, 0:16].reshape(MAIN)
    dest = tags[:, 16:32].reshape(MAIN)
    slot = jnp.arange(MAIN, dtype=I32)
    chip = slot // 16
    home = main_order((MAIN,), 0, core)
    away = away_order(source_of(chip, core), (label_of_chip - chip) & 7, slot & 15)
    order = jnp.where(label == (label_of_chip + 1).astype(F32), home, away)
    key_order = jnp.where(label > 0.5, order, NEVER)
    axes = ("core", "yl", "z")
    ring = [(i, (i + 1) % 16) for i in range(16)]

    def step(_, state):
        found, rows, tag = state
        scores = mm_t(main, rows)
        ok = (tag[0:1] == label[:, None]) & (tag[1:2] < order[:, None])
        found = jnp.maximum(found, jnp.max(jnp.where(ok, scores, -1.0), axis=1))
        return found, lax.ppermute(rows, axes, ring), lax.ppermute(tag, axes, ring)

    tag = jnp.stack([label, key_order])
    found, _, _ = lax.fori_loop(0, 16, step, (jnp.full((MAIN,), -1.0, F32), main, tag))
    code = jnp.where(label > 0.5, dest, -1.0)
    none = jnp.full((8, 128), -1.0, F32)
    table = jnp.concatenate([found.reshape(8, 128), code.reshape(8, 128), none], axis=0)
    return place(jnp.broadcast_to(table, (32, 24, 128)), ids)


def pack_call(ids, *arrays):
    arrays = [pltpu.with_memory_space_constraint(array, pltpu.HBM) for array in arrays]
    return call(
        pack_kernel,
        struct((MAIN, D), BF),
        (ids, *arrays),
        3 << 30,
        pl.ANY,
        (
            pltpu.VMEM((ROWS, D), BF),
            pltpu.VMEM((ROWS,), I32),
            pltpu.VMEM((1, ROWS), I32),
            pltpu.SemaphoreType.DMA((3,)),
        ),
    )


def fix_call(ids, main):
    shapes = (struct((FIX, D), BF), struct((8, 128), F32), struct((CHIPS, 128), BF), struct((8, MAIN), F32))
    return call(fix_kernel, shapes, (ids, main), 1 << 30)


def main_call(*args):
    wide = struct((MAIN, 128), F32)
    shapes = (struct((8, MAIN), F32), wide, struct((16, 128), F32))
    return call(main_kernel, shapes, args, 3 << 30)


def last_call(*args):
    return call(last_kernel, struct((32, 8, 128), F32), args, 1 << 30)


def put_call(ids, back):
    specs = (pl.BlockSpec(memory_space=pltpu.VMEM), pl.BlockSpec(memory_space=pltpu.SMEM))
    return call(put_kernel, (struct((6, 128), F32), struct((1,), I32)), (ids, back), 1 << 27, out_specs=specs)


def body(embeddings, labels, send_list):
    core = lax.axis_index("core").astype(I32)
    member = lax.axis_index(("yh", "yl", "z")).astype(I32)
    label_of_chip = member & 7
    ids = jnp.stack([core, label_of_chip, label_of_chip, member])
    packed = pack_call(ids, embeddings, labels, send_list)
    main = lax.all_to_all(
        packed.reshape(CHIPS, SLOT, D), CHIP_AXES, split_axis=0, concat_axis=0, tiled=True
    ).reshape(MAIN, D)
    swap = [(0, 1), (1, 0)]
    twin = lax.ppermute(main, "core", swap)
    fix, flag, tags, lanes = fix_call(ids, main)
    fix = lax.all_to_all(
        fix.reshape(LABELS, SLOT, D), GROUP_CHIPS, split_axis=0, concat_axis=0, tiled=True
    ).reshape(FIX, D)
    parts = main_call(ids, tags, lanes, main, twin)
    fix, code = lax.optimization_barrier((fix, parts[2]))
    fix_twin = lax.ppermute(fix, "core", swap)
    table = last_call(ids, flag, *parts[:2], code, main, fix, fix_twin)
    back = lax.all_to_all(table, PLANE, split_axis=0, concat_axis=0, tiled=True)
    out, flag = put_call(ids, back)
    _, out = lax.while_loop(
        lambda state: state[0] > 0,
        lambda state: (state[0] * 0, general_path(lax.ppermute(twin, "core", swap), ids, label_of_chip, core)),
        (flag[0], out.reshape(ROWS)),
    )
    return out


def solution(mesh):
    fine = Mesh(mesh.devices.reshape(4, 2, 2, 2, 4), ALL)
    return jax.shard_map(body, mesh=fine, in_specs=(P(ALL, None), P(ALL), P(ALL, None)), out_specs=P(ALL), check_vma=False)
```

```python
import functools

import jax
import jax.numpy as jnp
from jax import lax
from jax.experimental import pallas as pl
from jax.experimental.pallas import tpu as pltpu
from jax.sharding import Mesh, PartitionSpec as P

F32 = jnp.float32
BF = jnp.bfloat16
I32 = jnp.int32

D = 1024
ROWS = 768
CHIPS = 64
LABELS = 8
CAP = 15
SLOT = 16
MAIN = CHIPS * SLOT
FIX = LABELS * SLOT
ALL = ("x", "core", "yh", "yl", "z")
CHIP_AXES = ("x", "yh", "yl", "z")
GROUP_CORES = ("core", "yl", "z")
PLANE = ("core", "yh", "yl", "z")
NEVER = 1.0e9
VMEM = 24 * 1024 * 1024


def iota(shape, dim):
    return lax.broadcasted_iota(I32, shape, dim)


def onehot(cond):
    return jnp.where(cond, 1.0, 0.0).astype(BF)


def mm(a, b):
    return lax.dot_general(a, b, (((1,), (0,)), ((), ())), preferred_element_type=F32)


def mm_t(a, b):
    return lax.dot_general(a, b, (((1,), (1,)), ((), ())), preferred_element_type=F32)


def earlier(hot):
    n, width = hot.shape
    parts = width // 128
    rows = jnp.concatenate([hot[:, i * 128:(i + 1) * 128] for i in range(parts)], axis=0)
    inside = mm(rows.astype(BF), onehot(iota((128, 128), 0) < iota((128, 128), 1)))
    total = jnp.broadcast_to(jnp.sum(rows, axis=1, keepdims=True), rows.shape).astype(BF)
    m = parts * n
    a, b = iota((m, m), 0), iota((m, m), 1)
    inside = inside + mm(onehot(((a & (n - 1)) == (b & (n - 1))) & (b < a)), total)
    return jnp.concatenate([inside[i * n:(i + 1) * n] for i in range(parts)], axis=1)


def pack_kernel(ids_ref, emb_hbm, lab_hbm, list_hbm, out_ref, emb_ref, lab_ref, list_ref, sems):
    copies = [
        pltpu.make_async_copy(src, dst, sems.at[i])
        for i, (src, dst) in enumerate(((list_hbm, list_ref), (lab_hbm, lab_ref), (emb_hbm, emb_ref)))
    ]
    for copy in copies:
        copy.start()
    rot = ids_ref[2]
    copies[0].wait()
    copies[1].wait()
    listed = onehot(iota((ROWS, ROWS), 0) == list_ref[...])
    pos = iota((16, ROWS), 1)
    group_of = lax.shift_right_logical(pos * 683, 16)
    sel = iota((16, ROWS), 0)
    vals = jnp.where(sel == 0, group_of, jnp.where(sel == 1, pos - group_of * 96, 0)).astype(F32).astype(BF)
    gd = mm_t(vals, listed)
    group = gd[0:1]
    dest = gd[1:2]
    label = lab_ref[...].reshape(1, ROWS).astype(F32)
    cluster = group * 8.0 + label
    member = iota((CHIPS, ROWS), 0).astype(F32) == cluster
    ranks = earlier(jnp.where(member, 1.0, 0.0))
    rank = jnp.sum(jnp.where(member, ranks, 0.0), axis=0, keepdims=True)
    count = jnp.broadcast_to(jnp.sum(jnp.where(member, 1.0, 0.0), axis=1, keepdims=True), (CHIPS, 128))
    over = jnp.maximum(count - CAP, 0.0).astype(BF)
    free = jnp.maximum(CAP - count, 0.0)
    c0, c1 = iota((CHIPS, CHIPS), 0), iota((CHIPS, CHIPS), 1)
    same = lax.shift_right_logical(c0, 3) == lax.shift_right_logical(c1, 3)
    over_pre = mm(onehot(same & (c1 < c0)), over)
    above = (CAP - 1 - (iota((CHIPS, 128), 1) & 15)).astype(F32)
    higher = jnp.clip(free, 0.0, jnp.maximum(above, 0.0)).astype(BF)
    level = onehot(free > above)
    free_pre = mm(onehot(same), higher) + mm(onehot(same & (((c1 - rot) & 7) < ((c0 - rot) & 7))), level)
    over_at = jnp.sum(jnp.where(member, over_pre[:, 0:1], 0.0), axis=0, keepdims=True) + rank - CAP
    row_code = jnp.where(rank < CAP, cluster * 16.0 + rank, 2048.0 + group * 128.0 + over_at)
    slot = iota((MAIN, 128), 0)
    at = (slot & 15).astype(F32)
    chip_hot = onehot(lax.shift_right_logical(iota((MAIN, CHIPS), 0), 4) == iota((MAIN, CHIPS), 1))
    slot_count = mm(chip_hot, count.astype(BF))
    slot_free = jnp.where(iota((MAIN, 128), 1) == (slot & 15), mm(chip_hot, free_pre.astype(BF)), 0.0)
    slot_free = jnp.sum(slot_free, axis=1, keepdims=True)
    spare = 2048.0 + (lax.shift_right_logical(slot, 7) * 128).astype(F32) + slot_free
    slot_code = jnp.where(at >= CAP, -1.0, jnp.where(at < slot_count, slot.astype(F32), spare))
    pick = jnp.concatenate([onehot(slot_code == row_code[:, b * 128:(b + 1) * 128]) for b in range(ROWS // 128)], axis=1)
    copies[2].wait()
    values = emb_ref[...].astype(F32)
    scale = lax.rsqrt(jnp.sum(values * values, axis=1, keepdims=True) + 1e-06)
    unit = (values * scale).astype(BF)
    lane = iota((128, ROWS), 0)
    tags = jnp.where(lane < 16, label + 1.0, jnp.where(lane < 32, dest, 0.0)).astype(BF)
    tag = jnp.where((iota((MAIN, 128), 1) & 15) == (slot & 15), mm_t(pick, tags), 0.0)
    tag = jnp.broadcast_to(jnp.sum(tag.reshape(CHIPS, SLOT, 128), axis=1, keepdims=True), (CHIPS, SLOT, 128)).reshape(MAIN, 128)
    for r in range(0, MAIN, 256):
        part = mm(pick[r:r + 256], unit)
        out_ref[r:r + 256, 0:128] = jnp.where(at[r:r + 256] >= CAP, tag[r:r + 256], part[:, 0:128]).astype(BF)
        out_ref[r:r + 256, 128:D] = part[:, 128:D].astype(BF)


def tag_rows(first, n):
    pick = onehot(iota((n, n * SLOT), 1) == iota((n, n * SLOT), 0) * SLOT + CAP)
    return mm(pick, first).astype(BF)


def tag_lanes(tags, n, k):
    spread = onehot(iota((128, n * SLOT), 0) == (iota((128, n * SLOT), 1) & 15) + 16 * k)
    wide = mm(tags, spread)
    own = iota((n, n * SLOT), 0) == lax.shift_right_logical(iota((n, n * SLOT), 1), 4)
    return jnp.sum(jnp.where(own, wide, 0.0), axis=0, keepdims=True)


def tag_columns(tags, n, ks):
    spread = onehot(lax.shift_right_logical(iota((n * SLOT, n), 0), 4) == iota((n * SLOT, n), 1))
    wide = mm(spread, tags)
    shape = (n * SLOT, 128)
    own = iota(shape, 0) & 15
    return [jnp.sum(jnp.where(iota(shape, 1) == own + 16 * k, wide, 0.0), axis=1, keepdims=True) for k in ks]


def source_of(chip, core):
    return lax.shift_right_logical(chip, 4) * 32 + core * 16 + (chip & 15)


def main_order(shape, dim, core):
    slot = iota(shape, dim)
    return (source_of(lax.shift_right_logical(slot, 4), core) * 256 + (slot & 15)).astype(F32)


def away_order(source, turn, at):
    return (source * 256 + 16 + (CAP - 1 - at) * 8 + turn).astype(F32)


def fix_order(shape, dim, core, chip, at):
    holder = lax.shift_right_logical(iota(shape, dim), 4)
    chip = chip.astype(I32)
    return away_order(source_of(chip, core), (holder - chip) & 7, at.astype(I32))


def fix_kernel(ids_ref, main_ref, out_ref, flag_ref, tags_ref, lanes_ref):
    own = ids_ref[1].astype(F32)
    tags = tag_rows(main_ref[:, 0:128], CHIPS)
    label = tag_lanes(tags, CHIPS, 0)
    dest = tag_lanes(tags, CHIPS, 1)
    tags_ref[...] = tags
    lanes_ref[...] = jnp.concatenate([label, dest, jnp.zeros((6, MAIN), F32)], axis=0)
    moved = (label > 0.5) & (label != own + 1.0)
    member = moved & (iota((LABELS, MAIN), 0).astype(F32) == label - 1.0)
    ranks = earlier(jnp.where(member, 1.0, 0.0))
    rank = jnp.sum(jnp.where(member, ranks, 0.0), axis=0, keepdims=True)
    code = jnp.where(moved & (rank < CAP), (label - 1.0) * 16.0 + rank, -1.0)
    pick = onehot(iota((FIX, MAIN), 0).astype(F32) == code)
    slot = iota((1, MAIN), 1)
    lane = iota((128, MAIN), 0)
    kind = lax.shift_right_logical(lane, 4)
    vals = jnp.where(kind == 0, 1.0, jnp.where(kind == 1, lax.shift_right_logical(slot, 4).astype(F32), jnp.where(kind == 2, (slot & 15).astype(F32), jnp.where(kind == 3, dest, 0.0)))).astype(BF)
    fixed = (FIX, 128)
    tag = jnp.where((iota(fixed, 1) & 15) == (iota(fixed, 0) & 15), mm_t(pick, vals), 0.0)
    tag = jnp.broadcast_to(jnp.sum(tag.reshape(LABELS, SLOT, 128), axis=1, keepdims=True), (LABELS, SLOT, 128)).reshape(fixed)
    for b in range(0, D, 256):
        part = mm(pick, main_ref[:, b:b + 256])
        if b == 0:
            part = jnp.concatenate([jnp.where((iota(fixed, 0) & 15) == CAP, tag, part[:, 0:128]), part[:, 128:256]], axis=1)
            out_ref[0:FIX, 0:256] = part.astype(BF)
            out_ref[FIX:2 * FIX, 0:256] = part.astype(BF)
        else:
            out_ref[0:FIX, b:b + 256] = part.astype(BF)
            out_ref[FIX:2 * FIX, b:b + 256] = part.astype(BF)
    worst = jnp.max(jnp.where(moved, rank, 0.0), axis=1, keepdims=True)
    flag_ref[...] = jnp.broadcast_to(jnp.where(worst >= CAP, 1.0, 0.0), (8, 128))


def lanes_to_rows(row):
    return jnp.concatenate([row[:, i * 128:(i + 1) * 128] for i in range(row.shape[1] // 128)], axis=0)


def best(keys, q_rows, q_order):
    found = jnp.full((1, q_rows.shape[0]), -1.0, F32)
    for rows, order in keys:
        scores = jnp.where(order[:, 0:1] < q_order, mm_t(rows[...], q_rows), -1.0)
        found = jnp.maximum(found, jnp.max(scores, axis=0, keepdims=True))
    return found


def main_kernel(ids_ref, tags_ref, lanes_ref, own_ref, twin_ref, rows_ref, own_key_ref, code_ref):
    core = ids_ref[0]
    mine = ids_ref[1].astype(F32) + 1.0
    twin_tags = tag_rows(twin_ref[:, 0:128], CHIPS)

    def main_key(t, c):
        (label,) = tag_columns(t, CHIPS, (0,))
        return jnp.broadcast_to(jnp.where(label == mine, main_order((MAIN, 1), 0, c), NEVER), (MAIN, 128))

    own_key_ref[...] = main_key(tags_ref[...], core)
    twin_key = main_key(twin_tags, 1 - core)
    valid = lanes_ref[0:1, :] == mine
    query = jnp.where(valid, main_order((1, MAIN), 1, core), -1.0)
    dest = lanes_ref[1:2, :].astype(I32)
    home = lax.shift_right_logical(dest * 43, 8)
    member = valid & (iota((16, MAIN), 0) == home)
    ranks = earlier(jnp.where(member, 1.0, 0.0))
    rank = jnp.sum(jnp.where(member, ranks, 0.0), axis=0, keepdims=True)
    rank = jnp.where(valid, rank, -1.0)
    hot = onehot(iota((128, MAIN), 0).astype(F32) == rank)
    source = source_of(lax.shift_right_logical(iota((1, MAIN), 1), 4), core)
    at = source * 6 + dest - home * 6 + 1
    high = lax.shift_right_logical(at, 4)
    parts = [jnp.where(member, part.astype(F32), 0.0).astype(BF) for part in (high, at - high * 16)]
    code_ref[...] = mm_t(parts[0], hot) * 16.0 + mm_t(parts[1], hot) - 1.0
    worst = jnp.max(rank, axis=1, keepdims=True)
    found = [
        best(
            ((own_ref[0:q + 256, :], own_key_ref[0:q + 256, :]), (twin_ref[0:q + 256, :], twin_key[0:q + 256, :])),
            own_ref[q:q + 256, :],
            query[:, q:q + 256],
        )
        for q in range(0, MAIN, 256)
    ]
    found = jnp.concatenate(found, axis=1)
    worst = jnp.broadcast_to(worst, (1, MAIN))
    rows = jnp.concatenate([query, found, home.astype(F32), worst, rank, jnp.zeros((3, MAIN), F32)], axis=0)
    rows_ref[...] = rows


def last_kernel(ids_ref, flag_ref, rows_ref, own_key_ref, code_ref, own_ref, fix_ref, out_ref):
    core = ids_ref[0]
    fix_rows = fix_ref[...]
    tags = tag_rows(fix_rows[:, 0:128], 2 * LABELS)

    def side(shape, dim):
        return lax.shift_right_logical(iota(shape, dim), 7)

    tall, wide = (2 * FIX, 1), (1, 2 * FIX)
    valid, chip, at = tag_columns(tags, 2 * LABELS, (0, 1, 2))
    fix_keys = ((fix_rows, jnp.where(valid > 0.5, fix_order(tall, 0, side(tall, 0), chip, at), NEVER)),)
    valid, chip, at, dest = (tag_lanes(tags, 2 * LABELS, k) for k in range(4))
    source = source_of(chip.astype(I32), side(wide, 1)).astype(F32)
    fix_query = jnp.where(valid > 0.5, fix_order(wide, 1, side(wide, 1), chip, at), -1.0)
    fix_code = jnp.where(valid > 0.5, source * 128.0 + dest, -1.0)
    fix_found = best(((own_ref, own_key_ref),) + fix_keys, fix_rows, fix_query)
    found = jnp.maximum(best(fix_keys, own_ref[...], rows_ref[0:1, :]), rows_ref[1:2, :])
    here = iota((16, MAIN), 0).astype(F32) == rows_ref[2:3, :]
    value = jnp.concatenate([jnp.where(here, part.astype(F32), 0.0).astype(BF) for part in split3(found)], axis=0)
    value = mm_t(value, onehot(iota((128, MAIN), 0).astype(F32) == rows_ref[4:5, :]))
    value = value[0:16] + value[16:32] + value[32:48]
    flag = jnp.maximum(flag_ref[0:1, :], jnp.where(rows_ref[3:4, 0:128] >= 128.0, 1.0, 0.0))
    common = [lanes_to_rows(fix_found), lanes_to_rows(fix_code), flag, jnp.zeros((1, 128), F32)]
    common = jnp.concatenate(common, axis=0)
    shape = (16, 8, 128)
    row = iota(shape, 1)
    table = jnp.broadcast_to(jnp.concatenate([jnp.zeros((2, 128), F32), common], axis=0)[None], shape)
    table = jnp.where(row == 0, value[:, None, :], jnp.where(row == 1, code_ref[...][:, None, :], table))
    out_ref[0:16] = table
    out_ref[16:32] = table


def split3(v):
    a = v.astype(BF)
    r = v - a.astype(F32)
    b = r.astype(BF)
    return a, b, (r - b.astype(F32)).astype(BF)


def place_kernel(ids_ref, in_ref, out_ref):
    core = ids_ref[0]
    base = (ids_ref[3] * 6).astype(F32)
    wide = (128, 128)
    outs = []
    spread = [onehot(iota(wide, 1) == lax.shift_right_logical(iota(wide, 0), 4) * 6 + q) for q in range(6)]
    fix_val, fix_code = [], []
    for c in range(2):
        acc = [jnp.zeros((8, 128), F32) for _ in range(6)]
        for k in range(LABELS):
            dev = c * 16 + core * 8 + k
            val = in_ref[dev, 0:8, :]
            code = in_ref[dev, 8:16, :]
            for q in range(6):
                acc[q] = acc[q] + jnp.where(code == base + q, val, 0.0)
            fix_val.append(in_ref[dev, 16:17, :])
            fix_code.append(in_ref[dev, 17:18, :])
        total = jnp.zeros((8, 128), F32)
        for q in range(6):
            for part in split3(acc[q]):
                total = total + mm(part, spread[q])
        outs.append(total)
    main = jnp.concatenate([outs[c][2 * x:2 * x + 2] for x in range(4) for c in range(2)], axis=0)
    val = jnp.concatenate(fix_val, axis=1)
    code = jnp.concatenate(fix_code, axis=1).astype(I32)
    source = lax.shift_right_arithmetic(code, 7)
    q = (code & 127).astype(F32) - base
    ok = (code >= 0) & (q >= 0.0) & (q < 6.0)
    n = val.shape[1]
    left = jnp.where(ok & (iota((16, n), 0) == lax.shift_right_arithmetic(source, 3)), val, 0.0)
    right = onehot(iota((128, n), 0).astype(F32) == (source & 7).astype(F32) * 6.0 + q)
    for part in split3(left):
        main = main + mm_t(part, right)
    out_ref[...] = jnp.maximum(main, -1.0)


def put_kernel(ids_ref, in_ref, out_ref, flag_ref):
    core = ids_ref[0]
    base = ids_ref[3] * 6
    outs = []
    for c in range(2):
        val, at = [], []
        for k in range(LABELS):
            block = in_ref[c * 16 + core * 8 + k]
            val += [block[0:1], block[2:3], block[3:4]]
            code = block[4:6].astype(I32)
            q = (code & 127) - base
            ok = (code >= 0) & (q >= 0) & (q < 6)
            fix_at = jnp.where(ok, lax.shift_right_arithmetic(code, 7) * 6 + q, -1)
            at += [block[1:2].astype(I32), fix_at[0:1], fix_at[1:2]]
        val = jnp.concatenate(val, axis=1) + 2.0
        at = jnp.concatenate(at, axis=1)
        n = val.shape[1]
        left = jnp.where(iota((8, n), 0) == lax.shift_right_arithmetic(at, 7), val, 0.0)
        out = mm_t(jnp.concatenate(split3(left), axis=0), onehot(iota((128, n), 0) == (at & 127)))
        outs.append(out[0:8] + out[8:16] + out[16:24])
    out_ref[...] = jnp.maximum(jnp.maximum(outs[0], outs[1]) - 2.0, -1.0)[0:6]
    flag_ref[0] = jnp.max(jnp.max(in_ref[...], axis=0)[6:7]).astype(I32)


def call(kernel, shapes, args, flops, memory=pltpu.VMEM, scratch=(), vmem=VMEM, out_memory=pltpu.VMEM, out_specs=None):
    specs = [pl.BlockSpec(memory_space=pltpu.SMEM)] + [pl.BlockSpec(memory_space=memory)] * (len(args) - 1)
    return pl.pallas_call(
        kernel,
        out_shape=shapes,
        in_specs=specs,
        out_specs=out_specs or jax.tree.map(lambda _: pl.BlockSpec(memory_space=out_memory), shapes),
        scratch_shapes=scratch,
        compiler_params=pltpu.CompilerParams(vmem_limit_bytes=vmem),
        cost_estimate=pl.CostEstimate(flops=flops, bytes_accessed=4 << 20, transcendentals=0),
    )(*args)


def struct(shape, dtype):
    return jax.ShapeDtypeStruct(shape, dtype)


def place(table, ids):
    back = lax.all_to_all(table, PLANE, split_axis=0, concat_axis=0, tiled=True)
    out = call(place_kernel, struct((16, 128), F32), (ids, back), 1 << 27)
    return out[:, :48].reshape(ROWS)


def general_path(main, ids, label_of_chip, core):
    tags = main[CAP::SLOT, :32].astype(F32)
    label = tags[:, 0:16].reshape(MAIN)
    dest = tags[:, 16:32].reshape(MAIN)
    slot = jnp.arange(MAIN, dtype=I32)
    chip = slot // 16
    home = main_order((MAIN,), 0, core)
    away = away_order(source_of(chip, core), (label_of_chip - chip) & 7, slot & 15)
    order = jnp.where(label == (label_of_chip + 1).astype(F32), home, away)
    key_order = jnp.where(label > 0.5, order, NEVER)
    axes = ("core", "yl", "z")
    ring = [(i, (i + 1) % 16) for i in range(16)]

    def step(_, state):
        found, rows, tag = state
        scores = mm_t(main, rows)
        ok = (tag[0:1] == label[:, None]) & (tag[1:2] < order[:, None])
        found = jnp.maximum(found, jnp.max(jnp.where(ok, scores, -1.0), axis=1))
        return found, lax.ppermute(rows, axes, ring), lax.ppermute(tag, axes, ring)

    tag = jnp.stack([label, key_order])
    found, _, _ = lax.fori_loop(0, 16, step, (jnp.full((MAIN,), -1.0, F32), main, tag))
    code = jnp.where(label > 0.5, dest, -1.0)
    none = jnp.full((8, 128), -1.0, F32)
    table = jnp.concatenate([found.reshape(8, 128), code.reshape(8, 128), none], axis=0)
    return place(jnp.broadcast_to(table, (32, 24, 128)), ids)


def pack_call(ids, *arrays):
    arrays = [pltpu.with_memory_space_constraint(array, pltpu.HBM) for array in arrays]
    return call(
        pack_kernel,
        struct((MAIN, D), BF),
        (ids, *arrays),
        3 << 30,
        pl.ANY,
        (
            pltpu.VMEM((ROWS, D), BF),
            pltpu.VMEM((ROWS,), I32),
            pltpu.VMEM((1, ROWS), I32),
            pltpu.SemaphoreType.DMA((3,)),
        ),
    )


def fix_call(ids, main):
    shapes = (struct((2 * FIX, D), BF), struct((8, 128), F32), struct((CHIPS, 128), BF), struct((8, MAIN), F32))
    return call(fix_kernel, shapes, (ids, main), 1 << 30)


def main_call(*args):
    wide = struct((MAIN, 128), F32)
    shapes = (struct((8, MAIN), F32), wide, struct((16, 128), F32))
    return call(main_kernel, shapes, args, 3 << 30)


def last_call(*args):
    return call(last_kernel, struct((32, 8, 128), F32), args, 1 << 30)


def put_call(ids, back):
    specs = (pl.BlockSpec(memory_space=pltpu.VMEM), pl.BlockSpec(memory_space=pltpu.SMEM))
    return call(put_kernel, (struct((6, 128), F32), struct((1,), I32)), (ids, back), 1 << 27, out_specs=specs)


def body(embeddings, labels, send_list):
    core = lax.axis_index("core").astype(I32)
    member = lax.axis_index(("yh", "yl", "z")).astype(I32)
    label_of_chip = member & 7
    ids = jnp.stack([core, label_of_chip, label_of_chip, member])
    packed = pack_call(ids, embeddings, labels, send_list)
    main = lax.all_to_all(
        packed.reshape(CHIPS, SLOT, D), CHIP_AXES, split_axis=0, concat_axis=0, tiled=True
    ).reshape(MAIN, D)
    swap = [(0, 1), (1, 0)]
    twin = lax.ppermute(main, "core", swap)
    fix, flag, tags, lanes = fix_call(ids, main)
    fix = lax.all_to_all(
        fix.reshape(2 * LABELS, SLOT, D), GROUP_CORES, split_axis=0, concat_axis=0, tiled=True
    ).reshape(2 * FIX, D)
    parts = main_call(ids, tags, lanes, main, twin)
    fix, code = lax.optimization_barrier((fix, parts[2]))
    table = last_call(ids, flag, *parts[:2], code, main, fix)
    back = lax.all_to_all(table, PLANE, split_axis=0, concat_axis=0, tiled=True)
    out, flag = put_call(ids, back)
    _, out = lax.while_loop(
        lambda state: state[0] > 0,
        lambda state: (state[0] * 0, general_path(lax.ppermute(twin, "core", swap), ids, label_of_chip, core)),
        (flag[0], out.reshape(ROWS)),
    )
    return out


def solution(mesh):
    fine = Mesh(mesh.devices.reshape(4, 2, 2, 2, 4), ALL)
    return jax.shard_map(body, mesh=fine, in_specs=(P(ALL, None), P(ALL), P(ALL, None)), out_specs=P(ALL), check_vma=False)
```

```python
import functools

import jax
import jax.numpy as jnp
from jax import lax
from jax.experimental import pallas as pl
from jax.experimental.pallas import tpu as pltpu
from jax.sharding import Mesh, PartitionSpec as P

F32 = jnp.float32
BF = jnp.bfloat16
I32 = jnp.int32

D = 1024
ROWS = 768
CHIPS = 64
LABELS = 8
CAP = 15
SLOT = 16
MAIN = CHIPS * SLOT
FIX = LABELS * SLOT
ALL = ("x", "core", "yh", "yl", "z")
CHIP_AXES = ("x", "yh", "yl", "z")
GROUP_CHIPS = ("yl", "z")
PLANE = ("core", "yh", "yl", "z")
NEVER = 1.0e9
VMEM = 24 * 1024 * 1024


def iota(shape, dim):
    return lax.broadcasted_iota(I32, shape, dim)


def onehot(cond):
    return jnp.where(cond, 1.0, 0.0).astype(BF)


def mm(a, b):
    return lax.dot_general(a, b, (((1,), (0,)), ((), ())), preferred_element_type=F32)


def mm_t(a, b):
    return lax.dot_general(a, b, (((1,), (1,)), ((), ())), preferred_element_type=F32)


def earlier(hot):
    n, width = hot.shape
    parts = width // 128
    rows = jnp.concatenate([hot[:, i * 128:(i + 1) * 128] for i in range(parts)], axis=0)
    inside = mm(rows.astype(BF), onehot(iota((128, 128), 0) < iota((128, 128), 1)))
    total = jnp.broadcast_to(jnp.sum(rows, axis=1, keepdims=True), rows.shape).astype(BF)
    m = parts * n
    a, b = iota((m, m), 0), iota((m, m), 1)
    inside = inside + mm(onehot(((a & (n - 1)) == (b & (n - 1))) & (b < a)), total)
    return jnp.concatenate([inside[i * n:(i + 1) * n] for i in range(parts)], axis=1)


def pack_kernel(ids_ref, emb_hbm, lab_hbm, list_hbm, out_ref, emb_ref, lab_ref, list_ref, sems):
    copies = [
        pltpu.make_async_copy(src, dst, sems.at[i])
        for i, (src, dst) in enumerate(((list_hbm, list_ref), (lab_hbm, lab_ref), (emb_hbm, emb_ref)))
    ]
    for copy in copies:
        copy.start()
    rot = ids_ref[2]
    copies[0].wait()
    copies[1].wait()
    listed = onehot(iota((ROWS, ROWS), 0) == list_ref[...])
    pos = iota((16, ROWS), 1)
    group_of = lax.shift_right_logical(pos * 683, 16)
    sel = iota((16, ROWS), 0)
    vals = jnp.where(sel == 0, group_of, jnp.where(sel == 1, pos - group_of * 96, 0)).astype(F32).astype(BF)
    gd = mm_t(vals, listed)
    group = gd[0:1]
    dest = gd[1:2]
    label = lab_ref[...].reshape(1, ROWS).astype(F32)
    cluster = group * 8.0 + label
    member = iota((CHIPS, ROWS), 0).astype(F32) == cluster
    ranks = earlier(jnp.where(member, 1.0, 0.0))
    rank = jnp.sum(jnp.where(member, ranks, 0.0), axis=0, keepdims=True)
    count = jnp.broadcast_to(jnp.sum(jnp.where(member, 1.0, 0.0), axis=1, keepdims=True), (CHIPS, 128))
    over = jnp.maximum(count - CAP, 0.0).astype(BF)
    free = jnp.maximum(CAP - count, 0.0)
    c0, c1 = iota((CHIPS, CHIPS), 0), iota((CHIPS, CHIPS), 1)
    same = lax.shift_right_logical(c0, 3) == lax.shift_right_logical(c1, 3)
    over_pre = mm(onehot(same & (c1 < c0)), over)
    above = (CAP - 1 - (iota((CHIPS, 128), 1) & 15)).astype(F32)
    higher = jnp.clip(free, 0.0, jnp.maximum(above, 0.0)).astype(BF)
    level = onehot(free > above)
    free_pre = mm(onehot(same), higher) + mm(onehot(same & (((c1 - rot) & 7) < ((c0 - rot) & 7))), level)
    over_at = jnp.sum(jnp.where(member, over_pre[:, 0:1], 0.0), axis=0, keepdims=True) + rank - CAP
    row_code = jnp.where(rank < CAP, cluster * 16.0 + rank, 2048.0 + group * 128.0 + over_at)
    slot = iota((MAIN, 128), 0)
    at = (slot & 15).astype(F32)
    chip_hot = onehot(lax.shift_right_logical(iota((MAIN, CHIPS), 0), 4) == iota((MAIN, CHIPS), 1))
    slot_count = mm(chip_hot, count.astype(BF))
    slot_free = jnp.where(iota((MAIN, 128), 1) == (slot & 15), mm(chip_hot, free_pre.astype(BF)), 0.0)
    slot_free = jnp.sum(slot_free, axis=1, keepdims=True)
    spare = 2048.0 + (lax.shift_right_logical(slot, 7) * 128).astype(F32) + slot_free
    slot_code = jnp.where(at >= CAP, -1.0, jnp.where(at < slot_count, slot.astype(F32), spare))
    pick = jnp.concatenate([onehot(slot_code == row_code[:, b * 128:(b + 1) * 128]) for b in range(ROWS // 128)], axis=1)
    copies[2].wait()
    values = emb_ref[...].astype(F32)
    scale = lax.rsqrt(jnp.sum(values * values, axis=1, keepdims=True) + 1e-06)
    unit = (values * scale).astype(BF)
    lane = iota((128, ROWS), 0)
    tags = jnp.where(lane < 16, label + 1.0, jnp.where(lane < 32, dest, 0.0)).astype(BF)
    tag = jnp.where((iota((MAIN, 128), 1) & 15) == (slot & 15), mm_t(pick, tags), 0.0)
    tag = jnp.broadcast_to(jnp.sum(tag.reshape(CHIPS, SLOT, 128), axis=1, keepdims=True), (CHIPS, SLOT, 128)).reshape(MAIN, 128)
    for r in range(0, MAIN, 256):
        part = mm(pick[r:r + 256], unit)
        out_ref[r:r + 256, 0:128] = jnp.where(at[r:r + 256] >= CAP, tag[r:r + 256], part[:, 0:128]).astype(BF)
        out_ref[r:r + 256, 128:D] = part[:, 128:D].astype(BF)


def tag_rows(first, n):
    pick = onehot(iota((n, n * SLOT), 1) == iota((n, n * SLOT), 0) * SLOT + CAP)
    return mm(pick, first).astype(BF)


def tag_lanes(tags, n, k):
    spread = onehot(iota((128, n * SLOT), 0) == (iota((128, n * SLOT), 1) & 15) + 16 * k)
    wide = mm(tags, spread)
    own = iota((n, n * SLOT), 0) == lax.shift_right_logical(iota((n, n * SLOT), 1), 4)
    return jnp.sum(jnp.where(own, wide, 0.0), axis=0, keepdims=True)


def tag_columns(tags, n, ks):
    spread = onehot(lax.shift_right_logical(iota((n * SLOT, n), 0), 4) == iota((n * SLOT, n), 1))
    wide = mm(spread, tags)
    shape = (n * SLOT, 128)
    own = iota(shape, 0) & 15
    return [jnp.sum(jnp.where(iota(shape, 1) == own + 16 * k, wide, 0.0), axis=1, keepdims=True) for k in ks]


def source_of(chip, core):
    return lax.shift_right_logical(chip, 4) * 32 + core * 16 + (chip & 15)


def main_order(shape, dim, core):
    slot = iota(shape, dim)
    return (source_of(lax.shift_right_logical(slot, 4), core) * 256 + (slot & 15)).astype(F32)


def away_order(source, turn, at):
    return (source * 256 + 16 + (CAP - 1 - at) * 8 + turn).astype(F32)


def fix_order(shape, dim, core, chip, at):
    holder = lax.shift_right_logical(iota(shape, dim), 4)
    chip = chip.astype(I32)
    return away_order(source_of(chip, core), (holder - chip) & 7, at.astype(I32))


def fix_kernel(ids_ref, main_ref, out_hbm, flag_ref, tags_ref, lanes_ref, out_ref, sems):
    own = ids_ref[1].astype(F32)
    tags = tag_rows(main_ref[:, 0:128], CHIPS)
    label = tag_lanes(tags, CHIPS, 0)
    dest = tag_lanes(tags, CHIPS, 1)
    tags_ref[...] = tags
    lanes_ref[...] = jnp.concatenate([label, dest, jnp.zeros((6, MAIN), F32)], axis=0)
    moved = (label > 0.5) & (label != own + 1.0)
    member = moved & (iota((LABELS, MAIN), 0).astype(F32) == label - 1.0)
    ranks = earlier(jnp.where(member, 1.0, 0.0))
    rank = jnp.sum(jnp.where(member, ranks, 0.0), axis=0, keepdims=True)
    code = jnp.where(moved & (rank < CAP), (label - 1.0) * 16.0 + rank, -1.0)
    pick = onehot(iota((FIX, MAIN), 0).astype(F32) == code)
    slot = iota((1, MAIN), 1)
    lane = iota((128, MAIN), 0)
    kind = lax.shift_right_logical(lane, 4)
    vals = jnp.where(kind == 0, 1.0, jnp.where(kind == 1, lax.shift_right_logical(slot, 4).astype(F32), jnp.where(kind == 2, (slot & 15).astype(F32), jnp.where(kind == 3, dest, 0.0)))).astype(BF)
    fixed = (FIX, 128)
    tag = jnp.where((iota(fixed, 1) & 15) == (iota(fixed, 0) & 15), mm_t(pick, vals), 0.0)
    tag = jnp.broadcast_to(jnp.sum(tag.reshape(LABELS, SLOT, 128), axis=1, keepdims=True), (LABELS, SLOT, 128)).reshape(fixed)
    copies = []
    for i, b in enumerate(range(0, D, 256)):
        part = mm(pick, main_ref[:, b:b + 256])
        if b == 0:
            out_ref[:, 0:128] = jnp.where((iota(fixed, 0) & 15) == CAP, tag, part[:, 0:128]).astype(BF)
            out_ref[:, 128:256] = part[:, 128:256].astype(BF)
        else:
            out_ref[:, b:b + 256] = part.astype(BF)
        copies.append(pltpu.make_async_copy(out_ref.at[:, b:b + 256], out_hbm.at[:, b:b + 256], sems.at[i]))
        copies[-1].start()
    worst = jnp.max(jnp.where(moved, rank, 0.0), axis=1, keepdims=True)
    flag_ref[...] = jnp.broadcast_to(jnp.where(worst >= CAP, 1.0, 0.0), (8, 128))
    for copy in copies:
        copy.wait()


def lanes_to_rows(row):
    return jnp.concatenate([row[:, i * 128:(i + 1) * 128] for i in range(row.shape[1] // 128)], axis=0)


def best(keys, q_rows, q_order):
    found = jnp.full((1, q_rows.shape[0]), -1.0, F32)
    for rows, order in keys:
        scores = jnp.where(order[:, 0:1] < q_order, mm_t(rows[...], q_rows), -1.0)
        found = jnp.maximum(found, jnp.max(scores, axis=0, keepdims=True))
    return found


def main_kernel(ids_ref, tags_ref, lanes_ref, own_ref, twin_hbm, rows_ref, own_key_ref, code_ref, twin_ref, sems):
    fetch = [
        pltpu.make_async_copy(twin_hbm.at[r:r + 256], twin_ref.at[r:r + 256], sems.at[i])
        for i, r in enumerate(range(0, MAIN, 256))
    ]
    for copy in fetch:
        copy.start()
    core = ids_ref[0]
    mine = ids_ref[1].astype(F32) + 1.0

    def main_key(t, c):
        (label,) = tag_columns(t, CHIPS, (0,))
        return jnp.broadcast_to(jnp.where(label == mine, main_order((MAIN, 1), 0, c), NEVER), (MAIN, 128))

    own_key_ref[...] = main_key(tags_ref[...], core)
    valid = lanes_ref[0:1, :] == mine
    query = jnp.where(valid, main_order((1, MAIN), 1, core), -1.0)

    def score(ref, key, q):
        return best(((ref[0:q + 256, :], key[0:q + 256, :]),), own_ref[q:q + 256, :], query[:, q:q + 256])

    found = [score(own_ref, own_key_ref, 0), score(own_ref, own_key_ref, 256)]
    dest = lanes_ref[1:2, :].astype(I32)
    home = lax.shift_right_logical(dest * 43, 8)
    member = valid & (iota((16, MAIN), 0) == home)
    ranks = earlier(jnp.where(member, 1.0, 0.0))
    found.append(score(own_ref, own_key_ref, 512))
    rank = jnp.sum(jnp.where(member, ranks, 0.0), axis=0, keepdims=True)
    rank = jnp.where(valid, rank, -1.0)
    found.append(score(own_ref, own_key_ref, 768))
    hot = onehot(iota((128, MAIN), 0).astype(F32) == rank)
    source = source_of(lax.shift_right_logical(iota((1, MAIN), 1), 4), core)
    at = source * 6 + dest - home * 6 + 1
    high = lax.shift_right_logical(at, 4)
    parts = [jnp.where(member, part.astype(F32), 0.0).astype(BF) for part in (high, at - high * 16)]
    for copy in fetch:
        copy.wait()
    twin_key = main_key(tag_rows(twin_ref[:, 0:128], CHIPS), 1 - core)
    found[0] = jnp.maximum(found[0], score(twin_ref, twin_key, 0))
    found[1] = jnp.maximum(found[1], score(twin_ref, twin_key, 256))
    code_ref[...] = mm_t(parts[0], hot) * 16.0 + mm_t(parts[1], hot) - 1.0
    found[2] = jnp.maximum(found[2], score(twin_ref, twin_key, 512))
    found[3] = jnp.maximum(found[3], score(twin_ref, twin_key, 768))
    worst = jnp.broadcast_to(jnp.max(rank, axis=1, keepdims=True), (1, MAIN))
    found = jnp.concatenate(found, axis=1)
    rows = jnp.concatenate([query, found, home.astype(F32), worst, rank, jnp.zeros((3, MAIN), F32)], axis=0)
    rows_ref[...] = rows


def last_kernel(ids_ref, flag_ref, rows_ref, own_key_ref, code_ref, own_ref, fix_ref, fix_twin_ref, out_ref):
    core = ids_ref[0]
    fix_rows = jnp.concatenate([fix_ref[...], fix_twin_ref[...]], axis=0)
    tags = tag_rows(fix_rows[:, 0:128], 2 * LABELS)

    def side(shape, dim):
        return core ^ lax.shift_right_logical(iota(shape, dim), 7)

    tall, wide = (2 * FIX, 1), (1, 2 * FIX)
    valid, chip, at = tag_columns(tags, 2 * LABELS, (0, 1, 2))
    fix_keys = ((fix_rows, jnp.where(valid > 0.5, fix_order(tall, 0, side(tall, 0), chip, at), NEVER)),)
    valid, chip, at, dest = (tag_lanes(tags, 2 * LABELS, k) for k in range(4))
    source = source_of(chip.astype(I32), side(wide, 1)).astype(F32)
    fix_query = jnp.where(valid > 0.5, fix_order(wide, 1, side(wide, 1), chip, at), -1.0)
    fix_code = jnp.where(valid > 0.5, source * 128.0 + dest, -1.0)
    fix_found = best(((own_ref, own_key_ref),) + fix_keys, fix_rows, fix_query)
    found = jnp.maximum(best(fix_keys, own_ref[...], rows_ref[0:1, :]), rows_ref[1:2, :])
    here = iota((16, MAIN), 0).astype(F32) == rows_ref[2:3, :]
    value = jnp.concatenate([jnp.where(here, part.astype(F32), 0.0).astype(BF) for part in split3(found)], axis=0)
    value = mm_t(value, onehot(iota((128, MAIN), 0).astype(F32) == rows_ref[4:5, :]))
    value = value[0:16] + value[16:32] + value[32:48]
    flag = jnp.maximum(flag_ref[0:1, :], jnp.where(rows_ref[3:4, 0:128] >= 128.0, 1.0, 0.0))
    common = [lanes_to_rows(fix_found), lanes_to_rows(fix_code), flag, jnp.zeros((1, 128), F32)]
    common = jnp.concatenate(common, axis=0)
    shape = (16, 8, 128)
    row = iota(shape, 1)
    table = jnp.broadcast_to(jnp.concatenate([jnp.zeros((2, 128), F32), common], axis=0)[None], shape)
    table = jnp.where(row == 0, value[:, None, :], jnp.where(row == 1, code_ref[...][:, None, :], table))
    out_ref[0:16] = table
    out_ref[16:32] = table


def split3(v):
    a = v.astype(BF)
    r = v - a.astype(F32)
    b = r.astype(BF)
    return a, b, (r - b.astype(F32)).astype(BF)


def place_kernel(ids_ref, in_ref, out_ref):
    core = ids_ref[0]
    base = (ids_ref[3] * 6).astype(F32)
    wide = (128, 128)
    outs = []
    spread = [onehot(iota(wide, 1) == lax.shift_right_logical(iota(wide, 0), 4) * 6 + q) for q in range(6)]
    fix_val, fix_code = [], []
    for c in range(2):
        acc = [jnp.zeros((8, 128), F32) for _ in range(6)]
        for k in range(LABELS):
            dev = c * 16 + core * 8 + k
            val = in_ref[dev, 0:8, :]
            code = in_ref[dev, 8:16, :]
            for q in range(6):
                acc[q] = acc[q] + jnp.where(code == base + q, val, 0.0)
            fix_val.append(in_ref[dev, 16:17, :])
            fix_code.append(in_ref[dev, 17:18, :])
        total = jnp.zeros((8, 128), F32)
        for q in range(6):
            for part in split3(acc[q]):
                total = total + mm(part, spread[q])
        outs.append(total)
    main = jnp.concatenate([outs[c][2 * x:2 * x + 2] for x in range(4) for c in range(2)], axis=0)
    val = jnp.concatenate(fix_val, axis=1)
    code = jnp.concatenate(fix_code, axis=1).astype(I32)
    source = lax.shift_right_arithmetic(code, 7)
    q = (code & 127).astype(F32) - base
    ok = (code >= 0) & (q >= 0.0) & (q < 6.0)
    n = val.shape[1]
    left = jnp.where(ok & (iota((16, n), 0) == lax.shift_right_arithmetic(source, 3)), val, 0.0)
    right = onehot(iota((128, n), 0).astype(F32) == (source & 7).astype(F32) * 6.0 + q)
    for part in split3(left):
        main = main + mm_t(part, right)
    out_ref[...] = jnp.maximum(main, -1.0)


def put_kernel(ids_ref, in_ref, out_ref, flag_ref):
    core = ids_ref[0]
    base = ids_ref[3] * 6
    outs = []
    for c in range(2):
        val, at = [], []
        for k in range(LABELS):
            block = in_ref[c * 16 + core * 8 + k]
            val += [block[0:1], block[2:3], block[3:4]]
            code = block[4:6].astype(I32)
            q = (code & 127) - base
            ok = (code >= 0) & (q >= 0) & (q < 6)
            fix_at = jnp.where(ok, lax.shift_right_arithmetic(code, 7) * 6 + q, -1)
            at += [block[1:2].astype(I32), fix_at[0:1], fix_at[1:2]]
        val = jnp.concatenate(val, axis=1) + 2.0
        at = jnp.concatenate(at, axis=1)
        n = val.shape[1]
        left = jnp.where(iota((8, n), 0) == lax.shift_right_arithmetic(at, 7), val, 0.0)
        out = mm_t(jnp.concatenate(split3(left), axis=0), onehot(iota((128, n), 0) == (at & 127)))
        outs.append(out[0:8] + out[8:16] + out[16:24])
    out_ref[...] = jnp.maximum(jnp.maximum(outs[0], outs[1]) - 2.0, -1.0)[0:6]
    flag_ref[0] = jnp.max(jnp.max(in_ref[...], axis=0)[6:7]).astype(I32)


def call(kernel, shapes, args, flops, memory=pltpu.VMEM, scratch=(), vmem=VMEM, out_memory=pltpu.VMEM, out_specs=None):
    memory = memory if isinstance(memory, list) else [memory] * (len(args) - 1)
    specs = [pl.BlockSpec(memory_space=space) for space in [pltpu.SMEM] + memory]
    return pl.pallas_call(
        kernel,
        out_shape=shapes,
        in_specs=specs,
        out_specs=out_specs or jax.tree.map(lambda _: pl.BlockSpec(memory_space=out_memory), shapes),
        scratch_shapes=scratch,
        compiler_params=pltpu.CompilerParams(vmem_limit_bytes=vmem),
        cost_estimate=pl.CostEstimate(flops=flops, bytes_accessed=4 << 20, transcendentals=0),
    )(*args)


def struct(shape, dtype):
    return jax.ShapeDtypeStruct(shape, dtype)


def place(table, ids):
    back = lax.all_to_all(table, PLANE, split_axis=0, concat_axis=0, tiled=True)
    out = call(place_kernel, struct((16, 128), F32), (ids, back), 1 << 27)
    return out[:, :48].reshape(ROWS)


def general_path(main, ids, label_of_chip, core):
    tags = main[CAP::SLOT, :32].astype(F32)
    label = tags[:, 0:16].reshape(MAIN)
    dest = tags[:, 16:32].reshape(MAIN)
    slot = jnp.arange(MAIN, dtype=I32)
    chip = slot // 16
    home = main_order((MAIN,), 0, core)
    away = away_order(source_of(chip, core), (label_of_chip - chip) & 7, slot & 15)
    order = jnp.where(label == (label_of_chip + 1).astype(F32), home, away)
    key_order = jnp.where(label > 0.5, order, NEVER)
    axes = ("core", "yl", "z")
    ring = [(i, (i + 1) % 16) for i in range(16)]

    def step(_, state):
        found, rows, tag = state
        scores = mm_t(main, rows)
        ok = (tag[0:1] == label[:, None]) & (tag[1:2] < order[:, None])
        found = jnp.maximum(found, jnp.max(jnp.where(ok, scores, -1.0), axis=1))
        return found, lax.ppermute(rows, axes, ring), lax.ppermute(tag, axes, ring)

    tag = jnp.stack([label, key_order])
    found, _, _ = lax.fori_loop(0, 16, step, (jnp.full((MAIN,), -1.0, F32), main, tag))
    code = jnp.where(label > 0.5, dest, -1.0)
    none = jnp.full((8, 128), -1.0, F32)
    table = jnp.concatenate([found.reshape(8, 128), code.reshape(8, 128), none], axis=0)
    return place(jnp.broadcast_to(table, (32, 24, 128)), ids)


def pack_call(ids, *arrays):
    arrays = [pltpu.with_memory_space_constraint(array, pltpu.HBM) for array in arrays]
    return call(
        pack_kernel,
        struct((MAIN, D), BF),
        (ids, *arrays),
        3 << 30,
        pl.ANY,
        (
            pltpu.VMEM((ROWS, D), BF),
            pltpu.VMEM((ROWS,), I32),
            pltpu.VMEM((1, ROWS), I32),
            pltpu.SemaphoreType.DMA((3,)),
        ),
    )


def fix_call(ids, main):
    shapes = (struct((FIX, D), BF), struct((8, 128), F32), struct((CHIPS, 128), BF), struct((8, MAIN), F32))
    specs = tuple(pl.BlockSpec(memory_space=space) for space in (pltpu.HBM,) + (pltpu.VMEM,) * 3)
    scratch = (pltpu.VMEM((FIX, D), BF), pltpu.SemaphoreType.DMA((4,)))
    return call(fix_kernel, shapes, (ids, main), 1 << 30, scratch=scratch, out_specs=specs)


def main_call(*args):
    wide = struct((MAIN, 128), F32)
    shapes = (struct((8, MAIN), F32), wide, struct((16, 128), F32))
    memory = [pltpu.VMEM] * 3 + [pl.ANY]
    scratch = (pltpu.VMEM((MAIN, D), BF), pltpu.SemaphoreType.DMA((4,)))
    return call(main_kernel, shapes, args, 3 << 30, memory, scratch)


def last_call(*args):
    return call(last_kernel, struct((32, 8, 128), F32), args, 1 << 30)


def put_call(ids, back):
    specs = (pl.BlockSpec(memory_space=pltpu.VMEM), pl.BlockSpec(memory_space=pltpu.SMEM))
    return call(put_kernel, (struct((6, 128), F32), struct((1,), I32)), (ids, back), 1 << 27, out_specs=specs)


def body(embeddings, labels, send_list):
    core = lax.axis_index("core").astype(I32)
    member = lax.axis_index(("yh", "yl", "z")).astype(I32)
    label_of_chip = member & 7
    ids = jnp.stack([core, label_of_chip, label_of_chip, member])
    packed = pack_call(ids, embeddings, labels, send_list)
    main = lax.all_to_all(
        packed.reshape(CHIPS, SLOT, D), CHIP_AXES, split_axis=0, concat_axis=0, tiled=True
    ).reshape(MAIN, D)
    swap = [(0, 1), (1, 0)]
    twin = lax.ppermute(main, "core", swap)
    fix, flag, tags, lanes = fix_call(ids, main)
    fix = lax.all_to_all(
        fix.reshape(LABELS, SLOT, D), GROUP_CHIPS, split_axis=0, concat_axis=0, tiled=True
    ).reshape(FIX, D)
    parts = main_call(ids, tags, lanes, main, twin)
    fix, code = lax.optimization_barrier((fix, parts[2]))
    fix_twin = lax.ppermute(fix, "core", swap)
    table = last_call(ids, flag, *parts[:2], code, main, fix, fix_twin)
    back = lax.all_to_all(table, PLANE, split_axis=0, concat_axis=0, tiled=True)
    out, flag = put_call(ids, back)
    _, out = lax.while_loop(
        lambda state: state[0] > 0,
        lambda state: (state[0] * 0, general_path(lax.ppermute(twin, "core", swap), ids, label_of_chip, core)),
        (flag[0], out.reshape(ROWS)),
    )
    return out


def solution(mesh):
    fine = Mesh(mesh.devices.reshape(4, 2, 2, 2, 4), ALL)
    return jax.shard_map(body, mesh=fine, in_specs=(P(ALL, None), P(ALL), P(ALL, None)), out_specs=P(ALL), check_vma=False)
```

```python
import functools

import jax
import jax.numpy as jnp
from jax import lax
from jax.experimental import pallas as pl
from jax.experimental.pallas import tpu as pltpu
from jax.sharding import Mesh, PartitionSpec as P

F32 = jnp.float32
BF = jnp.bfloat16
I32 = jnp.int32

D = 1024
ROWS = 768
CHIPS = 64
LABELS = 8
CAP = 15
SLOT = 16
MAIN = CHIPS * SLOT
FIX = LABELS * SLOT
ALL = ("x", "core", "yh", "yl", "z")
CHIP_AXES = ("x", "yh", "yl", "z")
GROUP_CHIPS = ("yl", "z")
PLANE = ("core", "yh", "yl", "z")
NEVER = 1.0e9
VMEM = 24 * 1024 * 1024


def iota(shape, dim):
    return lax.broadcasted_iota(I32, shape, dim)


def onehot(cond):
    return jnp.where(cond, 1.0, 0.0).astype(BF)


def mm(a, b):
    return lax.dot_general(a, b, (((1,), (0,)), ((), ())), preferred_element_type=F32)


def mm_t(a, b):
    return lax.dot_general(a, b, (((1,), (1,)), ((), ())), preferred_element_type=F32)


def earlier(hot):
    n, width = hot.shape
    parts = width // 128
    rows = jnp.concatenate([hot[:, i * 128:(i + 1) * 128] for i in range(parts)], axis=0)
    inside = mm(rows.astype(BF), onehot(iota((128, 128), 0) < iota((128, 128), 1)))
    total = jnp.broadcast_to(jnp.sum(rows, axis=1, keepdims=True), rows.shape).astype(BF)
    m = parts * n
    a, b = iota((m, m), 0), iota((m, m), 1)
    inside = inside + mm(onehot(((a & (n - 1)) == (b & (n - 1))) & (b < a)), total)
    return jnp.concatenate([inside[i * n:(i + 1) * n] for i in range(parts)], axis=1)


def pack_kernel(ids_ref, emb_hbm, lab_hbm, list_hbm, out_ref, emb_ref, lab_ref, list_ref, sems):
    copies = [
        pltpu.make_async_copy(src, dst, sems.at[i])
        for i, (src, dst) in enumerate(((list_hbm, list_ref), (lab_hbm, lab_ref), (emb_hbm, emb_ref)))
    ]
    for copy in copies:
        copy.start()
    rot = ids_ref[2]
    before = onehot(iota((ROWS, ROWS), 0) < iota((ROWS, ROWS), 1))
    pos = iota((16, ROWS), 1)
    group_of = lax.shift_right_logical(pos * 683, 16)
    sel = iota((16, ROWS), 0)
    vals = jnp.where(sel == 0, group_of, jnp.where(sel == 1, pos - group_of * 96, 0)).astype(F32).astype(BF)
    slot = iota((MAIN, 128), 0)
    at = (slot & 15).astype(F32)
    chip_hot = onehot(lax.shift_right_logical(iota((MAIN, CHIPS), 0), 4) == iota((MAIN, CHIPS), 1))
    copies[0].wait()
    copies[1].wait()
    listed = onehot(iota((ROWS, ROWS), 0) == list_ref[...])
    gd = mm_t(vals, listed)
    group = gd[0:1]
    dest = gd[1:2]
    label = lab_ref[...].reshape(1, ROWS).astype(F32)
    cluster = group * 8.0 + label
    member = iota((CHIPS, ROWS), 0).astype(F32) == cluster
    ranks = mm(onehot(member), before)
    rank = jnp.sum(jnp.where(member, ranks, 0.0), axis=0, keepdims=True)
    count = jnp.broadcast_to(jnp.sum(jnp.where(member, 1.0, 0.0), axis=1, keepdims=True), (CHIPS, 128))
    over = jnp.maximum(count - CAP, 0.0).astype(BF)
    free = jnp.maximum(CAP - count, 0.0)
    c0, c1 = iota((CHIPS, CHIPS), 0), iota((CHIPS, CHIPS), 1)
    same = lax.shift_right_logical(c0, 3) == lax.shift_right_logical(c1, 3)
    over_pre = mm(onehot(same & (c1 < c0)), over)
    above = (CAP - 1 - (iota((CHIPS, 128), 1) & 15)).astype(F32)
    higher = jnp.clip(free, 0.0, jnp.maximum(above, 0.0)).astype(BF)
    level = onehot(free > above)
    free_pre = mm(onehot(same), higher) + mm(onehot(same & (((c1 - rot) & 7) < ((c0 - rot) & 7))), level)
    over_at = jnp.sum(jnp.where(member, over_pre[:, 0:1], 0.0), axis=0, keepdims=True) + rank - CAP
    row_code = jnp.where(rank < CAP, cluster * 16.0 + rank, 2048.0 + group * 128.0 + over_at)
    slot_count = mm(chip_hot, count.astype(BF))
    slot_free = jnp.where(iota((MAIN, 128), 1) == (slot & 15), mm(chip_hot, free_pre.astype(BF)), 0.0)
    slot_free = jnp.sum(slot_free, axis=1, keepdims=True)
    spare = 2048.0 + (lax.shift_right_logical(slot, 7) * 128).astype(F32) + slot_free
    slot_code = jnp.where(at >= CAP, -1.0, jnp.where(at < slot_count, slot.astype(F32), spare))
    pick = jnp.concatenate([onehot(slot_code == row_code[:, b * 128:(b + 1) * 128]) for b in range(ROWS // 128)], axis=1)
    copies[2].wait()
    values = emb_ref[...].astype(F32)
    scale = lax.rsqrt(jnp.sum(values * values, axis=1, keepdims=True) + 1e-06)
    unit = (values * scale).astype(BF)
    lane = iota((128, ROWS), 0)
    tags = jnp.where(lane < 16, label + 1.0, jnp.where(lane < 32, dest, 0.0)).astype(BF)
    tag = jnp.where((iota((MAIN, 128), 1) & 15) == (slot & 15), mm_t(pick, tags), 0.0)
    tag = jnp.broadcast_to(jnp.sum(tag.reshape(CHIPS, SLOT, 128), axis=1, keepdims=True), (CHIPS, SLOT, 128)).reshape(MAIN, 128)
    for r in range(0, MAIN, 256):
        part = mm(pick[r:r + 256], unit)
        out_ref[r:r + 256, 0:128] = jnp.where(at[r:r + 256] >= CAP, tag[r:r + 256], part[:, 0:128]).astype(BF)
        out_ref[r:r + 256, 128:D] = part[:, 128:D].astype(BF)


def tag_rows(first, n):
    pick = onehot(iota((n, n * SLOT), 1) == iota((n, n * SLOT), 0) * SLOT + CAP)
    return mm(pick, first).astype(BF)


def tag_lanes(tags, n, k):
    spread = onehot(iota((128, n * SLOT), 0) == (iota((128, n * SLOT), 1) & 15) + 16 * k)
    wide = mm(tags, spread)
    own = iota((n, n * SLOT), 0) == lax.shift_right_logical(iota((n, n * SLOT), 1), 4)
    return jnp.sum(jnp.where(own, wide, 0.0), axis=0, keepdims=True)


def tag_columns(tags, n, ks):
    spread = onehot(lax.shift_right_logical(iota((n * SLOT, n), 0), 4) == iota((n * SLOT, n), 1))
    wide = mm(spread, tags)
    shape = (n * SLOT, 128)
    own = iota(shape, 0) & 15
    return [jnp.sum(jnp.where(iota(shape, 1) == own + 16 * k, wide, 0.0), axis=1, keepdims=True) for k in ks]


def source_of(chip, core):
    return lax.shift_right_logical(chip, 4) * 32 + core * 16 + (chip & 15)


def main_order(shape, dim, core):
    slot = iota(shape, dim)
    return (source_of(lax.shift_right_logical(slot, 4), core) * 256 + (slot & 15)).astype(F32)


def away_order(source, turn, at):
    return (source * 256 + 16 + (CAP - 1 - at) * 8 + turn).astype(F32)


def fix_order(shape, dim, core, chip, at):
    holder = lax.shift_right_logical(iota(shape, dim), 4)
    chip = chip.astype(I32)
    return away_order(source_of(chip, core), (holder - chip) & 7, at.astype(I32))


def fix_kernel(ids_ref, main_ref, out_hbm, flag_ref, tags_ref, lanes_ref, out_ref, sems):
    own = ids_ref[1].astype(F32)
    tags = tag_rows(main_ref[:, 0:128], CHIPS)
    label = tag_lanes(tags, CHIPS, 0)
    dest = tag_lanes(tags, CHIPS, 1)
    tags_ref[...] = tags
    lanes_ref[...] = jnp.concatenate([label, dest, jnp.zeros((6, MAIN), F32)], axis=0)
    moved = (label > 0.5) & (label != own + 1.0)
    member = moved & (iota((LABELS, MAIN), 0).astype(F32) == label - 1.0)
    ranks = earlier(jnp.where(member, 1.0, 0.0))
    rank = jnp.sum(jnp.where(member, ranks, 0.0), axis=0, keepdims=True)
    code = jnp.where(moved & (rank < CAP), (label - 1.0) * 16.0 + rank, -1.0)
    pick = onehot(iota((FIX, MAIN), 0).astype(F32) == code)
    slot = iota((1, MAIN), 1)
    lane = iota((128, MAIN), 0)
    kind = lax.shift_right_logical(lane, 4)
    vals = jnp.where(kind == 0, 1.0, jnp.where(kind == 1, lax.shift_right_logical(slot, 4).astype(F32), jnp.where(kind == 2, (slot & 15).astype(F32), jnp.where(kind == 3, dest, 0.0)))).astype(BF)
    fixed = (FIX, 128)
    tag = jnp.where((iota(fixed, 1) & 15) == (iota(fixed, 0) & 15), mm_t(pick, vals), 0.0)
    tag = jnp.broadcast_to(jnp.sum(tag.reshape(LABELS, SLOT, 128), axis=1, keepdims=True), (LABELS, SLOT, 128)).reshape(fixed)
    copies = []
    for i, b in enumerate(range(0, D, 256)):
        part = mm(pick, main_ref[:, b:b + 256])
        if b == 0:
            out_ref[:, 0:128] = jnp.where((iota(fixed, 0) & 15) == CAP, tag, part[:, 0:128]).astype(BF)
            out_ref[:, 128:256] = part[:, 128:256].astype(BF)
        else:
            out_ref[:, b:b + 256] = part.astype(BF)
        copies.append(pltpu.make_async_copy(out_ref.at[:, b:b + 256], out_hbm.at[:, b:b + 256], sems.at[i]))
        copies[-1].start()
    worst = jnp.max(jnp.where(moved, rank, 0.0), axis=1, keepdims=True)
    flag_ref[...] = jnp.broadcast_to(jnp.where(worst >= CAP, 1.0, 0.0), (8, 128))
    for copy in copies:
        copy.wait()


def lanes_to_rows(row):
    return jnp.concatenate([row[:, i * 128:(i + 1) * 128] for i in range(row.shape[1] // 128)], axis=0)


def best(keys, q_rows, q_order):
    found = jnp.full((1, q_rows.shape[0]), -1.0, F32)
    for rows, order in keys:
        scores = jnp.where(order[:, 0:1] < q_order, mm_t(rows[...], q_rows), -1.0)
        found = jnp.maximum(found, jnp.max(scores, axis=0, keepdims=True))
    return found


def main_kernel(ids_ref, tags_ref, lanes_ref, own_ref, twin_hbm, rows_ref, own_key_ref, code_ref, twin_ref, sems):
    fetch = [
        pltpu.make_async_copy(twin_hbm.at[r:r + 256], twin_ref.at[r:r + 256], sems.at[i])
        for i, r in enumerate(range(0, MAIN, 256))
    ]
    for copy in fetch:
        copy.start()
    core = ids_ref[0]
    mine = ids_ref[1].astype(F32) + 1.0

    def main_key(t, c):
        (label,) = tag_columns(t, CHIPS, (0,))
        return jnp.broadcast_to(jnp.where(label == mine, main_order((MAIN, 1), 0, c), NEVER), (MAIN, 128))

    own_key_ref[...] = main_key(tags_ref[...], core)
    valid = lanes_ref[0:1, :] == mine
    query = jnp.where(valid, main_order((1, MAIN), 1, core), -1.0)

    def score(ref, key, q):
        return best(((ref[0:q + 256, :], key[0:q + 256, :]),), own_ref[q:q + 256, :], query[:, q:q + 256])

    found = [score(own_ref, own_key_ref, 0), score(own_ref, own_key_ref, 256)]
    dest = lanes_ref[1:2, :].astype(I32)
    home = lax.shift_right_logical(dest * 43, 8)
    member = valid & (iota((16, MAIN), 0) == home)
    ranks = earlier(jnp.where(member, 1.0, 0.0))
    found.append(score(own_ref, own_key_ref, 512))
    rank = jnp.sum(jnp.where(member, ranks, 0.0), axis=0, keepdims=True)
    rank = jnp.where(valid, rank, -1.0)
    found.append(score(own_ref, own_key_ref, 768))
    hot = onehot(iota((128, MAIN), 0).astype(F32) == rank)
    source = source_of(lax.shift_right_logical(iota((1, MAIN), 1), 4), core)
    at = source * 6 + dest - home * 6 + 1
    high = lax.shift_right_logical(at, 4)
    parts = [jnp.where(member, part.astype(F32), 0.0).astype(BF) for part in (high, at - high * 16)]
    for copy in fetch:
        copy.wait()
    twin_key = main_key(tag_rows(twin_ref[:, 0:128], CHIPS), 1 - core)
    found[0] = jnp.maximum(found[0], score(twin_ref, twin_key, 0))
    found[1] = jnp.maximum(found[1], score(twin_ref, twin_key, 256))
    code_ref[...] = mm_t(parts[0], hot) * 16.0 + mm_t(parts[1], hot) - 1.0
    found[2] = jnp.maximum(found[2], score(twin_ref, twin_key, 512))
    found[3] = jnp.maximum(found[3], score(twin_ref, twin_key, 768))
    worst = jnp.broadcast_to(jnp.max(rank, axis=1, keepdims=True), (1, MAIN))
    found = jnp.concatenate(found, axis=1)
    rows = jnp.concatenate([query, found, home.astype(F32), worst, rank, jnp.zeros((3, MAIN), F32)], axis=0)
    rows_ref[...] = rows


def last_kernel(ids_ref, flag_ref, rows_ref, own_key_ref, code_ref, own_ref, fix_ref, fix_twin_ref, out_ref):
    core = ids_ref[0]
    fix_rows = jnp.concatenate([fix_ref[...], fix_twin_ref[...]], axis=0)
    tags = tag_rows(fix_rows[:, 0:128], 2 * LABELS)

    def side(shape, dim):
        return core ^ lax.shift_right_logical(iota(shape, dim), 7)

    tall, wide = (2 * FIX, 1), (1, 2 * FIX)
    valid, chip, at = tag_columns(tags, 2 * LABELS, (0, 1, 2))
    fix_keys = ((fix_rows, jnp.where(valid > 0.5, fix_order(tall, 0, side(tall, 0), chip, at), NEVER)),)
    valid, chip, at, dest = (tag_lanes(tags, 2 * LABELS, k) for k in range(4))
    source = source_of(chip.astype(I32), side(wide, 1)).astype(F32)
    fix_query = jnp.where(valid > 0.5, fix_order(wide, 1, side(wide, 1), chip, at), -1.0)
    fix_code = jnp.where(valid > 0.5, source * 128.0 + dest, -1.0)
    fix_found = best(((own_ref, own_key_ref),) + fix_keys, fix_rows, fix_query)
    found = jnp.maximum(best(fix_keys, own_ref[...], rows_ref[0:1, :]), rows_ref[1:2, :])
    here = iota((16, MAIN), 0).astype(F32) == rows_ref[2:3, :]
    value = jnp.concatenate([jnp.where(here, part.astype(F32), 0.0).astype(BF) for part in split3(found)], axis=0)
    value = mm_t(value, onehot(iota((128, MAIN), 0).astype(F32) == rows_ref[4:5, :]))
    value = value[0:16] + value[16:32] + value[32:48]
    flag = jnp.maximum(flag_ref[0:1, :], jnp.where(rows_ref[3:4, 0:128] >= 128.0, 1.0, 0.0))
    common = [lanes_to_rows(fix_found), lanes_to_rows(fix_code), flag, jnp.zeros((1, 128), F32)]
    common = jnp.concatenate(common, axis=0)
    shape = (16, 8, 128)
    row = iota(shape, 1)
    table = jnp.broadcast_to(jnp.concatenate([jnp.zeros((2, 128), F32), common], axis=0)[None], shape)
    table = jnp.where(row == 0, value[:, None, :], jnp.where(row == 1, code_ref[...][:, None, :], table))
    out_ref[0:16] = table
    out_ref[16:32] = table


def split3(v):
    a = v.astype(BF)
    r = v - a.astype(F32)
    b = r.astype(BF)
    return a, b, (r - b.astype(F32)).astype(BF)


def place_kernel(ids_ref, in_ref, out_ref):
    core = ids_ref[0]
    base = (ids_ref[3] * 6).astype(F32)
    wide = (128, 128)
    outs = []
    spread = [onehot(iota(wide, 1) == lax.shift_right_logical(iota(wide, 0), 4) * 6 + q) for q in range(6)]
    fix_val, fix_code = [], []
    for c in range(2):
        acc = [jnp.zeros((8, 128), F32) for _ in range(6)]
        for k in range(LABELS):
            dev = c * 16 + core * 8 + k
            val = in_ref[dev, 0:8, :]
            code = in_ref[dev, 8:16, :]
            for q in range(6):
                acc[q] = acc[q] + jnp.where(code == base + q, val, 0.0)
            fix_val.append(in_ref[dev, 16:17, :])
            fix_code.append(in_ref[dev, 17:18, :])
        total = jnp.zeros((8, 128), F32)
        for q in range(6):
            for part in split3(acc[q]):
                total = total + mm(part, spread[q])
        outs.append(total)
    main = jnp.concatenate([outs[c][2 * x:2 * x + 2] for x in range(4) for c in range(2)], axis=0)
    val = jnp.concatenate(fix_val, axis=1)
    code = jnp.concatenate(fix_code, axis=1).astype(I32)
    source = lax.shift_right_arithmetic(code, 7)
    q = (code & 127).astype(F32) - base
    ok = (code >= 0) & (q >= 0.0) & (q < 6.0)
    n = val.shape[1]
    left = jnp.where(ok & (iota((16, n), 0) == lax.shift_right_arithmetic(source, 3)), val, 0.0)
    right = onehot(iota((128, n), 0).astype(F32) == (source & 7).astype(F32) * 6.0 + q)
    for part in split3(left):
        main = main + mm_t(part, right)
    out_ref[...] = jnp.maximum(main, -1.0)


def put_kernel(ids_ref, in_ref, out_ref, flag_ref):
    core = ids_ref[0]
    base = ids_ref[3] * 6
    outs = []
    for c in range(2):
        val, at = [], []
        for k in range(LABELS):
            block = in_ref[c * 16 + core * 8 + k]
            val += [block[0:1], block[2:3], block[3:4]]
            code = block[4:6].astype(I32)
            q = (code & 127) - base
            ok = (code >= 0) & (q >= 0) & (q < 6)
            fix_at = jnp.where(ok, lax.shift_right_arithmetic(code, 7) * 6 + q, -1)
            at += [block[1:2].astype(I32), fix_at[0:1], fix_at[1:2]]
        val = jnp.concatenate(val, axis=1) + 2.0
        at = jnp.concatenate(at, axis=1)
        n = val.shape[1]
        left = jnp.where(iota((8, n), 0) == lax.shift_right_arithmetic(at, 7), val, 0.0)
        out = mm_t(jnp.concatenate(split3(left), axis=0), onehot(iota((128, n), 0) == (at & 127)))
        outs.append(out[0:8] + out[8:16] + out[16:24])
    out_ref[...] = jnp.maximum(jnp.maximum(outs[0], outs[1]) - 2.0, -1.0)[0:6]
    flag_ref[0] = jnp.max(jnp.max(in_ref[...], axis=0)[6:7]).astype(I32)


def call(kernel, shapes, args, flops, memory=pltpu.VMEM, scratch=(), vmem=VMEM, out_memory=pltpu.VMEM, out_specs=None):
    memory = memory if isinstance(memory, list) else [memory] * (len(args) - 1)
    specs = [pl.BlockSpec(memory_space=space) for space in [pltpu.SMEM] + memory]
    return pl.pallas_call(
        kernel,
        out_shape=shapes,
        in_specs=specs,
        out_specs=out_specs or jax.tree.map(lambda _: pl.BlockSpec(memory_space=out_memory), shapes),
        scratch_shapes=scratch,
        compiler_params=pltpu.CompilerParams(vmem_limit_bytes=vmem),
        cost_estimate=pl.CostEstimate(flops=flops, bytes_accessed=4 << 20, transcendentals=0),
    )(*args)


def struct(shape, dtype):
    return jax.ShapeDtypeStruct(shape, dtype)


def place(table, ids):
    back = lax.all_to_all(table, PLANE, split_axis=0, concat_axis=0, tiled=True)
    out = call(place_kernel, struct((16, 128), F32), (ids, back), 1 << 27)
    return out[:, :48].reshape(ROWS)


def general_path(main, ids, label_of_chip, core):
    tags = main[CAP::SLOT, :32].astype(F32)
    label = tags[:, 0:16].reshape(MAIN)
    dest = tags[:, 16:32].reshape(MAIN)
    slot = jnp.arange(MAIN, dtype=I32)
    chip = slot // 16
    home = main_order((MAIN,), 0, core)
    away = away_order(source_of(chip, core), (label_of_chip - chip) & 7, slot & 15)
    order = jnp.where(label == (label_of_chip + 1).astype(F32), home, away)
    key_order = jnp.where(label > 0.5, order, NEVER)
    axes = ("core", "yl", "z")
    ring = [(i, (i + 1) % 16) for i in range(16)]

    def step(_, state):
        found, rows, tag = state
        scores = mm_t(main, rows)
        ok = (tag[0:1] == label[:, None]) & (tag[1:2] < order[:, None])
        found = jnp.maximum(found, jnp.max(jnp.where(ok, scores, -1.0), axis=1))
        return found, lax.ppermute(rows, axes, ring), lax.ppermute(tag, axes, ring)

    tag = jnp.stack([label, key_order])
    found, _, _ = lax.fori_loop(0, 16, step, (jnp.full((MAIN,), -1.0, F32), main, tag))
    code = jnp.where(label > 0.5, dest, -1.0)
    none = jnp.full((8, 128), -1.0, F32)
    table = jnp.concatenate([found.reshape(8, 128), code.reshape(8, 128), none], axis=0)
    return place(jnp.broadcast_to(table, (32, 24, 128)), ids)


def pack_call(ids, *arrays):
    arrays = [pltpu.with_memory_space_constraint(array, pltpu.HBM) for array in arrays]
    return call(
        pack_kernel,
        struct((MAIN, D), BF),
        (ids, *arrays),
        3 << 30,
        pl.ANY,
        (
            pltpu.VMEM((ROWS, D), BF),
            pltpu.VMEM((ROWS,), I32),
            pltpu.VMEM((1, ROWS), I32),
            pltpu.SemaphoreType.DMA((3,)),
        ),
    )


def fix_call(ids, main):
    shapes = (struct((FIX, D), BF), struct((8, 128), F32), struct((CHIPS, 128), BF), struct((8, MAIN), F32))
    specs = tuple(pl.BlockSpec(memory_space=space) for space in (pltpu.HBM,) + (pltpu.VMEM,) * 3)
    scratch = (pltpu.VMEM((FIX, D), BF), pltpu.SemaphoreType.DMA((4,)))
    return call(fix_kernel, shapes, (ids, main), 1 << 30, scratch=scratch, out_specs=specs)


def main_call(*args):
    wide = struct((MAIN, 128), F32)
    shapes = (struct((8, MAIN), F32), wide, struct((16, 128), F32))
    memory = [pltpu.VMEM] * 3 + [pl.ANY]
    scratch = (pltpu.VMEM((MAIN, D), BF), pltpu.SemaphoreType.DMA((4,)))
    return call(main_kernel, shapes, args, 3 << 30, memory, scratch)


def last_call(*args):
    return call(last_kernel, struct((32, 8, 128), F32), args, 1 << 30)


def put_call(ids, back):
    specs = (pl.BlockSpec(memory_space=pltpu.VMEM), pl.BlockSpec(memory_space=pltpu.SMEM))
    return call(put_kernel, (struct((6, 128), F32), struct((1,), I32)), (ids, back), 1 << 27, out_specs=specs)


def body(embeddings, labels, send_list):
    core = lax.axis_index("core").astype(I32)
    member = lax.axis_index(("yh", "yl", "z")).astype(I32)
    label_of_chip = member & 7
    ids = jnp.stack([core, label_of_chip, label_of_chip, member])
    packed = pack_call(ids, embeddings, labels, send_list)
    main = lax.all_to_all(
        packed.reshape(CHIPS, SLOT, D), CHIP_AXES, split_axis=0, concat_axis=0, tiled=True
    ).reshape(MAIN, D)
    swap = [(0, 1), (1, 0)]
    twin = lax.ppermute(main, "core", swap)
    fix, flag, tags, lanes = fix_call(ids, main)
    fix = lax.all_to_all(
        fix.reshape(LABELS, SLOT, D), GROUP_CHIPS, split_axis=0, concat_axis=0, tiled=True
    ).reshape(FIX, D)
    parts = main_call(ids, tags, lanes, main, twin)
    fix, code = lax.optimization_barrier((fix, parts[2]))
    fix_twin = lax.ppermute(fix, "core", swap)
    table = last_call(ids, flag, *parts[:2], code, main, fix, fix_twin)
    back = lax.all_to_all(table, PLANE, split_axis=0, concat_axis=0, tiled=True)
    out, flag = put_call(ids, back)
    _, out = lax.while_loop(
        lambda state: state[0] > 0,
        lambda state: (state[0] * 0, general_path(lax.ppermute(twin, "core", swap), ids, label_of_chip, core)),
        (flag[0], out.reshape(ROWS)),
    )
    return out


def solution(mesh):
    fine = Mesh(mesh.devices.reshape(4, 2, 2, 2, 4), ALL)
    return jax.shard_map(body, mesh=fine, in_specs=(P(ALL, None), P(ALL), P(ALL, None)), out_specs=P(ALL), check_vma=False)
```

```python
import functools

import jax
import jax.numpy as jnp
from jax import lax
from jax.experimental import pallas as pl
from jax.experimental.pallas import tpu as pltpu
from jax.sharding import Mesh, PartitionSpec as P

F32 = jnp.float32
BF = jnp.bfloat16
I32 = jnp.int32

D = 1024
ROWS = 768
CHIPS = 64
LABELS = 8
CAP = 15
SLOT = 16
MAIN = CHIPS * SLOT
FIX = LABELS * SLOT
ALL = ("x", "core", "yh", "yl", "z")
CHIP_AXES = ("x", "yh", "yl", "z")
GROUP_CHIPS = ("yl", "z")
PLANE = ("core", "yh", "yl", "z")
NEVER = 1.0e9
VMEM = 24 * 1024 * 1024


def iota(shape, dim):
    return lax.broadcasted_iota(I32, shape, dim)


def onehot(cond):
    return jnp.where(cond, 1.0, 0.0).astype(BF)


def mm(a, b):
    return lax.dot_general(a, b, (((1,), (0,)), ((), ())), preferred_element_type=F32)


def mm_t(a, b):
    return lax.dot_general(a, b, (((1,), (1,)), ((), ())), preferred_element_type=F32)


def earlier(hot):
    n, width = hot.shape
    parts = width // 128
    rows = jnp.concatenate([hot[:, i * 128:(i + 1) * 128] for i in range(parts)], axis=0)
    inside = mm(rows.astype(BF), onehot(iota((128, 128), 0) < iota((128, 128), 1)))
    total = jnp.broadcast_to(jnp.sum(rows, axis=1, keepdims=True), rows.shape).astype(BF)
    m = parts * n
    a, b = iota((m, m), 0), iota((m, m), 1)
    inside = inside + mm(onehot(((a & (n - 1)) == (b & (n - 1))) & (b < a)), total)
    return jnp.concatenate([inside[i * n:(i + 1) * n] for i in range(parts)], axis=1)


def pack_kernel(ids_ref, emb_hbm, lab_hbm, list_hbm, out_ref, emb_ref, lab_ref, list_ref, sems):
    copies = [
        pltpu.make_async_copy(src, dst, sems.at[i])
        for i, (src, dst) in enumerate(((list_hbm, list_ref), (lab_hbm, lab_ref), (emb_hbm, emb_ref)))
    ]
    for copy in copies:
        copy.start()
    rot = ids_ref[2]
    copies[0].wait()
    copies[1].wait()
    listed = onehot(iota((ROWS, ROWS), 0) == list_ref[...])
    pos = iota((16, ROWS), 1)
    group_of = lax.shift_right_logical(pos * 683, 16)
    sel = iota((16, ROWS), 0)
    vals = jnp.where(sel == 0, group_of, jnp.where(sel == 1, pos - group_of * 96, 0)).astype(F32).astype(BF)
    gd = mm_t(vals, listed)
    group = gd[0:1]
    dest = gd[1:2]
    label = lab_ref[...].reshape(1, ROWS).astype(F32)
    cluster = group * 8.0 + label
    member = iota((CHIPS, ROWS), 0).astype(F32) == cluster
    ranks = earlier(jnp.where(member, 1.0, 0.0))
    rank = jnp.sum(jnp.where(member, ranks, 0.0), axis=0, keepdims=True)
    count = jnp.broadcast_to(jnp.sum(jnp.where(member, 1.0, 0.0), axis=1, keepdims=True), (CHIPS, 128))
    over = jnp.maximum(count - CAP, 0.0).astype(BF)
    free = jnp.maximum(CAP - count, 0.0)
    c0, c1 = iota((CHIPS, CHIPS), 0), iota((CHIPS, CHIPS), 1)
    same = lax.shift_right_logical(c0, 3) == lax.shift_right_logical(c1, 3)
    over_pre = mm(onehot(same & (c1 < c0)), over)
    above = (CAP - 1 - (iota((CHIPS, 128), 1) & 15)).astype(F32)
    higher = jnp.clip(free, 0.0, jnp.maximum(above, 0.0)).astype(BF)
    level = onehot(free > above)
    free_pre = mm(onehot(same), higher) + mm(onehot(same & (((c1 - rot) & 7) < ((c0 - rot) & 7))), level)
    over_at = jnp.sum(jnp.where(member, over_pre[:, 0:1], 0.0), axis=0, keepdims=True) + rank - CAP
    row_code = jnp.where(rank < CAP, cluster * 16.0 + rank, 2048.0 + group * 128.0 + over_at)
    slot = iota((MAIN, 128), 0)
    at = (slot & 15).astype(F32)
    chip_hot = onehot(lax.shift_right_logical(iota((MAIN, CHIPS), 0), 4) == iota((MAIN, CHIPS), 1))
    slot_count = mm(chip_hot, count.astype(BF))
    slot_free = jnp.where(iota((MAIN, 128), 1) == (slot & 15), mm(chip_hot, free_pre.astype(BF)), 0.0)
    slot_free = jnp.sum(slot_free, axis=1, keepdims=True)
    spare = 2048.0 + (lax.shift_right_logical(slot, 7) * 128).astype(F32) + slot_free
    slot_code = jnp.where(at >= CAP, -1.0, jnp.where(at < slot_count, slot.astype(F32), spare))
    pick = jnp.concatenate([onehot(slot_code == row_code[:, b * 128:(b + 1) * 128]) for b in range(ROWS // 128)], axis=1)
    copies[2].wait()
    values = emb_ref[...].astype(F32)
    scale = lax.rsqrt(jnp.sum(values * values, axis=1, keepdims=True) + 1e-06)
    unit = (values * scale).astype(BF)
    lane = iota((128, ROWS), 0)
    tags = jnp.where(lane < 16, label + 1.0, jnp.where(lane < 32, dest, 0.0)).astype(BF)
    tag = jnp.where((iota((MAIN, 128), 1) & 15) == (slot & 15), mm_t(pick, tags), 0.0)
    tag = jnp.broadcast_to(jnp.sum(tag.reshape(CHIPS, SLOT, 128), axis=1, keepdims=True), (CHIPS, SLOT, 128)).reshape(MAIN, 128)
    for r in range(0, MAIN, 256):
        part = mm(pick[r:r + 256], unit)
        out_ref[r:r + 256, 0:128] = jnp.where(at[r:r + 256] >= CAP, tag[r:r + 256], part[:, 0:128]).astype(BF)
        out_ref[r:r + 256, 128:D] = part[:, 128:D].astype(BF)


def tag_rows(first, n):
    pick = onehot(iota((n, n * SLOT), 1) == iota((n, n * SLOT), 0) * SLOT + CAP)
    return mm(pick, first).astype(BF)


def tag_lanes(tags, n, k):
    spread = onehot(iota((128, n * SLOT), 0) == (iota((128, n * SLOT), 1) & 15) + 16 * k)
    wide = mm(tags, spread)
    own = iota((n, n * SLOT), 0) == lax.shift_right_logical(iota((n, n * SLOT), 1), 4)
    return jnp.sum(jnp.where(own, wide, 0.0), axis=0, keepdims=True)


def tag_columns(tags, n, ks):
    spread = onehot(lax.shift_right_logical(iota((n * SLOT, n), 0), 4) == iota((n * SLOT, n), 1))
    wide = mm(spread, tags)
    shape = (n * SLOT, 128)
    own = iota(shape, 0) & 15
    return [jnp.sum(jnp.where(iota(shape, 1) == own + 16 * k, wide, 0.0), axis=1, keepdims=True) for k in ks]


def source_of(chip, core):
    return lax.shift_right_logical(chip, 4) * 32 + core * 16 + (chip & 15)


def main_order(shape, dim, core):
    slot = iota(shape, dim)
    return (source_of(lax.shift_right_logical(slot, 4), core) * 256 + (slot & 15)).astype(F32)


def away_order(source, turn, at):
    return (source * 256 + 16 + (CAP - 1 - at) * 8 + turn).astype(F32)


def fix_order(shape, dim, core, chip, at):
    holder = lax.shift_right_logical(iota(shape, dim), 4)
    chip = chip.astype(I32)
    return away_order(source_of(chip, core), (holder - chip) & 7, at.astype(I32))


def fix_kernel(ids_ref, main_ref, out_hbm, flag_ref, tags_ref, lanes_ref, out_ref, sems):
    own = ids_ref[1].astype(F32)
    tags = tag_rows(main_ref[:, 0:128], CHIPS)
    label = tag_lanes(tags, CHIPS, 0)
    dest = tag_lanes(tags, CHIPS, 1)
    tags_ref[...] = tags
    lanes_ref[...] = jnp.concatenate([label, dest, jnp.zeros((6, MAIN), F32)], axis=0)
    moved = (label > 0.5) & (label != own + 1.0)
    member = moved & (iota((LABELS, MAIN), 0).astype(F32) == label - 1.0)
    ranks = earlier(jnp.where(member, 1.0, 0.0))
    rank = jnp.sum(jnp.where(member, ranks, 0.0), axis=0, keepdims=True)
    code = jnp.where(moved & (rank < CAP), (label - 1.0) * 16.0 + rank, -1.0)
    pick = onehot(iota((FIX, MAIN), 0).astype(F32) == code)
    slot = iota((1, MAIN), 1)
    lane = iota((128, MAIN), 0)
    kind = lax.shift_right_logical(lane, 4)
    vals = jnp.where(kind == 0, 1.0, jnp.where(kind == 1, lax.shift_right_logical(slot, 4).astype(F32), jnp.where(kind == 2, (slot & 15).astype(F32), jnp.where(kind == 3, dest, 0.0)))).astype(BF)
    fixed = (FIX, 128)
    tag = jnp.where((iota(fixed, 1) & 15) == (iota(fixed, 0) & 15), mm_t(pick, vals), 0.0)
    tag = jnp.broadcast_to(jnp.sum(tag.reshape(LABELS, SLOT, 128), axis=1, keepdims=True), (LABELS, SLOT, 128)).reshape(fixed)
    copies = []
    for i, b in enumerate(range(0, D, 512)):
        part = mm(pick, main_ref[:, b:b + 512])
        if b == 0:
            out_ref[:, 0:128] = jnp.where((iota(fixed, 0) & 15) == CAP, tag, part[:, 0:128]).astype(BF)
            out_ref[:, 128:512] = part[:, 128:512].astype(BF)
        else:
            out_ref[:, b:b + 512] = part.astype(BF)
        copies.append(pltpu.make_async_copy(out_ref.at[:, b:b + 512], out_hbm.at[:, b:b + 512], sems.at[i]))
        copies[-1].start()
    worst = jnp.max(jnp.where(moved, rank, 0.0), axis=1, keepdims=True)
    flag_ref[...] = jnp.broadcast_to(jnp.where(worst >= CAP, 1.0, 0.0), (8, 128))
    for copy in copies:
        copy.wait()


def lanes_to_rows(row):
    return jnp.concatenate([row[:, i * 128:(i + 1) * 128] for i in range(row.shape[1] // 128)], axis=0)


def best(keys, q_rows, q_order):
    found = jnp.full((1, q_rows.shape[0]), -1.0, F32)
    for rows, order in keys:
        scores = jnp.where(order[:, 0:1] < q_order, mm_t(rows[...], q_rows), -1.0)
        found = jnp.maximum(found, jnp.max(scores, axis=0, keepdims=True))
    return found


def main_kernel(ids_ref, tags_ref, lanes_ref, own_ref, twin_hbm, rows_ref, own_key_ref, code_ref, twin_ref, sems):
    fetch = [
        pltpu.make_async_copy(twin_hbm.at[r:r + 256], twin_ref.at[r:r + 256], sems.at[i])
        for i, r in enumerate(range(0, MAIN, 256))
    ]
    for copy in fetch:
        copy.start()
    core = ids_ref[0]
    mine = ids_ref[1].astype(F32) + 1.0

    def main_key(t, c):
        (label,) = tag_columns(t, CHIPS, (0,))
        return jnp.broadcast_to(jnp.where(label == mine, main_order((MAIN, 1), 0, c), NEVER), (MAIN, 128))

    own_key_ref[...] = main_key(tags_ref[...], core)
    valid = lanes_ref[0:1, :] == mine
    query = jnp.where(valid, main_order((1, MAIN), 1, core), -1.0)

    def score(ref, key, q):
        return best(((ref[0:q + 256, :], key[0:q + 256, :]),), own_ref[q:q + 256, :], query[:, q:q + 256])

    found = [score(own_ref, own_key_ref, 0), score(own_ref, own_key_ref, 256)]
    dest = lanes_ref[1:2, :].astype(I32)
    home = lax.shift_right_logical(dest * 43, 8)
    member = valid & (iota((16, MAIN), 0) == home)
    ranks = earlier(jnp.where(member, 1.0, 0.0))
    found.append(score(own_ref, own_key_ref, 512))
    rank = jnp.sum(jnp.where(member, ranks, 0.0), axis=0, keepdims=True)
    rank = jnp.where(valid, rank, -1.0)
    found.append(score(own_ref, own_key_ref, 768))
    hot = onehot(iota((128, MAIN), 0).astype(F32) == rank)
    source = source_of(lax.shift_right_logical(iota((1, MAIN), 1), 4), core)
    at = source * 6 + dest - home * 6 + 1
    high = lax.shift_right_logical(at, 4)
    parts = [jnp.where(member, part.astype(F32), 0.0).astype(BF) for part in (high, at - high * 16)]
    for copy in fetch:
        copy.wait()
    twin_key = main_key(tag_rows(twin_ref[:, 0:128], CHIPS), 1 - core)
    found[0] = jnp.maximum(found[0], score(twin_ref, twin_key, 0))
    found[1] = jnp.maximum(found[1], score(twin_ref, twin_key, 256))
    code_ref[...] = mm_t(parts[0], hot) * 16.0 + mm_t(parts[1], hot) - 1.0
    found[2] = jnp.maximum(found[2], score(twin_ref, twin_key, 512))
    found[3] = jnp.maximum(found[3], score(twin_ref, twin_key, 768))
    worst = jnp.broadcast_to(jnp.max(rank, axis=1, keepdims=True), (1, MAIN))
    found = jnp.concatenate(found, axis=1)
    rows = jnp.concatenate([query, found, home.astype(F32), worst, rank, jnp.zeros((3, MAIN), F32)], axis=0)
    rows_ref[...] = rows


def last_kernel(ids_ref, flag_ref, rows_ref, own_key_ref, code_ref, own_ref, fix_ref, fix_twin_ref, out_ref):
    core = ids_ref[0]
    fix_rows = jnp.concatenate([fix_ref[...], fix_twin_ref[...]], axis=0)
    tags = tag_rows(fix_rows[:, 0:128], 2 * LABELS)

    def side(shape, dim):
        return core ^ lax.shift_right_logical(iota(shape, dim), 7)

    tall, wide = (2 * FIX, 1), (1, 2 * FIX)
    valid, chip, at = tag_columns(tags, 2 * LABELS, (0, 1, 2))
    fix_keys = ((fix_rows, jnp.where(valid > 0.5, fix_order(tall, 0, side(tall, 0), chip, at), NEVER)),)
    valid, chip, at, dest = (tag_lanes(tags, 2 * LABELS, k) for k in range(4))
    source = source_of(chip.astype(I32), side(wide, 1)).astype(F32)
    fix_query = jnp.where(valid > 0.5, fix_order(wide, 1, side(wide, 1), chip, at), -1.0)
    fix_code = jnp.where(valid > 0.5, source * 128.0 + dest, -1.0)
    fix_found = best(((own_ref, own_key_ref),) + fix_keys, fix_rows, fix_query)
    found = jnp.maximum(best(fix_keys, own_ref[...], rows_ref[0:1, :]), rows_ref[1:2, :])
    here = iota((16, MAIN), 0).astype(F32) == rows_ref[2:3, :]
    value = jnp.concatenate([jnp.where(here, part.astype(F32), 0.0).astype(BF) for part in split3(found)], axis=0)
    value = mm_t(value, onehot(iota((128, MAIN), 0).astype(F32) == rows_ref[4:5, :]))
    value = value[0:16] + value[16:32] + value[32:48]
    flag = jnp.maximum(flag_ref[0:1, :], jnp.where(rows_ref[3:4, 0:128] >= 128.0, 1.0, 0.0))
    common = [lanes_to_rows(fix_found), lanes_to_rows(fix_code), flag, jnp.zeros((1, 128), F32)]
    common = jnp.concatenate(common, axis=0)
    shape = (16, 8, 128)
    row = iota(shape, 1)
    table = jnp.broadcast_to(jnp.concatenate([jnp.zeros((2, 128), F32), common], axis=0)[None], shape)
    table = jnp.where(row == 0, value[:, None, :], jnp.where(row == 1, code_ref[...][:, None, :], table))
    out_ref[0:16] = table
    out_ref[16:32] = table


def split3(v):
    a = v.astype(BF)
    r = v - a.astype(F32)
    b = r.astype(BF)
    return a, b, (r - b.astype(F32)).astype(BF)


def place_kernel(ids_ref, in_ref, out_ref):
    core = ids_ref[0]
    base = (ids_ref[3] * 6).astype(F32)
    wide = (128, 128)
    outs = []
    spread = [onehot(iota(wide, 1) == lax.shift_right_logical(iota(wide, 0), 4) * 6 + q) for q in range(6)]
    fix_val, fix_code = [], []
    for c in range(2):
        acc = [jnp.zeros((8, 128), F32) for _ in range(6)]
        for k in range(LABELS):
            dev = c * 16 + core * 8 + k
            val = in_ref[dev, 0:8, :]
            code = in_ref[dev, 8:16, :]
            for q in range(6):
                acc[q] = acc[q] + jnp.where(code == base + q, val, 0.0)
            fix_val.append(in_ref[dev, 16:17, :])
            fix_code.append(in_ref[dev, 17:18, :])
        total = jnp.zeros((8, 128), F32)
        for q in range(6):
            for part in split3(acc[q]):
                total = total + mm(part, spread[q])
        outs.append(total)
    main = jnp.concatenate([outs[c][2 * x:2 * x + 2] for x in range(4) for c in range(2)], axis=0)
    val = jnp.concatenate(fix_val, axis=1)
    code = jnp.concatenate(fix_code, axis=1).astype(I32)
    source = lax.shift_right_arithmetic(code, 7)
    q = (code & 127).astype(F32) - base
    ok = (code >= 0) & (q >= 0.0) & (q < 6.0)
    n = val.shape[1]
    left = jnp.where(ok & (iota((16, n), 0) == lax.shift_right_arithmetic(source, 3)), val, 0.0)
    right = onehot(iota((128, n), 0).astype(F32) == (source & 7).astype(F32) * 6.0 + q)
    for part in split3(left):
        main = main + mm_t(part, right)
    out_ref[...] = jnp.maximum(main, -1.0)


def put_kernel(ids_ref, in_ref, out_ref, flag_ref):
    core = ids_ref[0]
    base = ids_ref[3] * 6
    outs = []
    for c in range(2):
        val, at = [], []
        for k in range(LABELS):
            block = in_ref[c * 16 + core * 8 + k]
            val += [block[0:1], block[2:3], block[3:4]]
            code = block[4:6].astype(I32)
            q = (code & 127) - base
            ok = (code >= 0) & (q >= 0) & (q < 6)
            fix_at = jnp.where(ok, lax.shift_right_arithmetic(code, 7) * 6 + q, -1)
            at += [block[1:2].astype(I32), fix_at[0:1], fix_at[1:2]]
        val = jnp.concatenate(val, axis=1) + 2.0
        at = jnp.concatenate(at, axis=1)
        n = val.shape[1]
        left = jnp.where(iota((8, n), 0) == lax.shift_right_arithmetic(at, 7), val, 0.0)
        out = mm_t(jnp.concatenate(split3(left), axis=0), onehot(iota((128, n), 0) == (at & 127)))
        outs.append(out[0:8] + out[8:16] + out[16:24])
    out_ref[...] = jnp.maximum(jnp.maximum(outs[0], outs[1]) - 2.0, -1.0)[0:6]
    flag_ref[0] = jnp.max(jnp.max(in_ref[...], axis=0)[6:7]).astype(I32)


def call(kernel, shapes, args, flops, memory=pltpu.VMEM, scratch=(), vmem=VMEM, out_memory=pltpu.VMEM, out_specs=None):
    memory = memory if isinstance(memory, list) else [memory] * (len(args) - 1)
    specs = [pl.BlockSpec(memory_space=space) for space in [pltpu.SMEM] + memory]
    return pl.pallas_call(
        kernel,
        out_shape=shapes,
        in_specs=specs,
        out_specs=out_specs or jax.tree.map(lambda _: pl.BlockSpec(memory_space=out_memory), shapes),
        scratch_shapes=scratch,
        compiler_params=pltpu.CompilerParams(vmem_limit_bytes=vmem),
        cost_estimate=pl.CostEstimate(flops=flops, bytes_accessed=4 << 20, transcendentals=0),
    )(*args)


def struct(shape, dtype):
    return jax.ShapeDtypeStruct(shape, dtype)


def place(table, ids):
    back = lax.all_to_all(table, PLANE, split_axis=0, concat_axis=0, tiled=True)
    out = call(place_kernel, struct((16, 128), F32), (ids, back), 1 << 27)
    return out[:, :48].reshape(ROWS)


def general_path(main, ids, label_of_chip, core):
    tags = main[CAP::SLOT, :32].astype(F32)
    label = tags[:, 0:16].reshape(MAIN)
    dest = tags[:, 16:32].reshape(MAIN)
    slot = jnp.arange(MAIN, dtype=I32)
    chip = slot // 16
    home = main_order((MAIN,), 0, core)
    away = away_order(source_of(chip, core), (label_of_chip - chip) & 7, slot & 15)
    order = jnp.where(label == (label_of_chip + 1).astype(F32), home, away)
    key_order = jnp.where(label > 0.5, order, NEVER)
    axes = ("core", "yl", "z")
    ring = [(i, (i + 1) % 16) for i in range(16)]

    def step(_, state):
        found, rows, tag = state
        scores = mm_t(main, rows)
        ok = (tag[0:1] == label[:, None]) & (tag[1:2] < order[:, None])
        found = jnp.maximum(found, jnp.max(jnp.where(ok, scores, -1.0), axis=1))
        return found, lax.ppermute(rows, axes, ring), lax.ppermute(tag, axes, ring)

    tag = jnp.stack([label, key_order])
    found, _, _ = lax.fori_loop(0, 16, step, (jnp.full((MAIN,), -1.0, F32), main, tag))
    code = jnp.where(label > 0.5, dest, -1.0)
    none = jnp.full((8, 128), -1.0, F32)
    table = jnp.concatenate([found.reshape(8, 128), code.reshape(8, 128), none], axis=0)
    return place(jnp.broadcast_to(table, (32, 24, 128)), ids)


def pack_call(ids, *arrays):
    arrays = [pltpu.with_memory_space_constraint(array, pltpu.HBM) for array in arrays]
    return call(
        pack_kernel,
        struct((MAIN, D), BF),
        (ids, *arrays),
        3 << 30,
        pl.ANY,
        (
            pltpu.VMEM((ROWS, D), BF),
            pltpu.VMEM((ROWS,), I32),
            pltpu.VMEM((1, ROWS), I32),
            pltpu.SemaphoreType.DMA((3,)),
        ),
    )


def fix_call(ids, main):
    shapes = (struct((FIX, D), BF), struct((8, 128), F32), struct((CHIPS, 128), BF), struct((8, MAIN), F32))
    specs = tuple(pl.BlockSpec(memory_space=space) for space in (pltpu.HBM,) + (pltpu.VMEM,) * 3)
    scratch = (pltpu.VMEM((FIX, D), BF), pltpu.SemaphoreType.DMA((4,)))
    return call(fix_kernel, shapes, (ids, main), 1 << 30, scratch=scratch, out_specs=specs)


def main_call(*args):
    wide = struct((MAIN, 128), F32)
    shapes = (struct((8, MAIN), F32), wide, struct((16, 128), F32))
    memory = [pltpu.VMEM] * 3 + [pl.ANY]
    scratch = (pltpu.VMEM((MAIN, D), BF), pltpu.SemaphoreType.DMA((4,)))
    return call(main_kernel, shapes, args, 3 << 30, memory, scratch)


def last_call(*args):
    return call(last_kernel, struct((32, 8, 128), F32), args, 1 << 30)


def put_call(ids, back):
    specs = (pl.BlockSpec(memory_space=pltpu.VMEM), pl.BlockSpec(memory_space=pltpu.SMEM))
    return call(put_kernel, (struct((6, 128), F32), struct((1,), I32)), (ids, back), 1 << 27, out_specs=specs)


def body(embeddings, labels, send_list):
    core = lax.axis_index("core").astype(I32)
    member = lax.axis_index(("yh", "yl", "z")).astype(I32)
    label_of_chip = member & 7
    ids = jnp.stack([core, label_of_chip, label_of_chip, member])
    packed = pack_call(ids, embeddings, labels, send_list)
    main = lax.all_to_all(
        packed.reshape(CHIPS, SLOT, D), CHIP_AXES, split_axis=0, concat_axis=0, tiled=True
    ).reshape(MAIN, D)
    swap = [(0, 1), (1, 0)]
    twin = lax.ppermute(main, "core", swap)
    fix, flag, tags, lanes = fix_call(ids, main)
    fix = lax.all_to_all(
        fix.reshape(LABELS, SLOT, D), GROUP_CHIPS, split_axis=0, concat_axis=0, tiled=True
    ).reshape(FIX, D)
    parts = main_call(ids, tags, lanes, main, twin)
    fix, code = lax.optimization_barrier((fix, parts[2]))
    fix_twin = lax.ppermute(fix, "core", swap)
    table = last_call(ids, flag, *parts[:2], code, main, fix, fix_twin)
    back = lax.all_to_all(table, PLANE, split_axis=0, concat_axis=0, tiled=True)
    out, flag = put_call(ids, back)
    _, out = lax.while_loop(
        lambda state: state[0] > 0,
        lambda state: (state[0] * 0, general_path(lax.ppermute(twin, "core", swap), ids, label_of_chip, core)),
        (flag[0], out.reshape(ROWS)),
    )
    return out


def solution(mesh):
    fine = Mesh(mesh.devices.reshape(4, 2, 2, 2, 4), ALL)
    return jax.shard_map(body, mesh=fine, in_specs=(P(ALL, None), P(ALL), P(ALL, None)), out_specs=P(ALL), check_vma=False)
```
